128 devices in a mesh: ctx: 16 (over z_hi, x, core), tp: 8 (over z_lo, y).
Axes of the slice: x: 4, y: 4, z: 4 (z_hi: 2, z_lo: 2; z = z_hi * 2 + z_lo), core: 2. Of those that a mesh axis runs over, the one named last changes fastest.
Arguments:
- block_input: bfloat16 [8192, 1536], P('ctx'), may hold values from -6 to 6
- positions: int32 [8192], replicated, may hold values from 0 to 8191, as said below
- attn_gain: bfloat16 [1536], P('ctx'), may hold values from 0.5 to 1.5
- query_weight: bfloat16 [1536, 1536], P('ctx', 'tp'), may hold values from -0.15625 to 0.15625
- key_weight: bfloat16 [1536, 512], P('ctx', 'tp'), may hold values from -0.15625 to 0.15625
- value_weight: bfloat16 [1536, 512], P('ctx', 'tp'), may hold values from -0.15625 to 0.15625
- query_gain: bfloat16 [64], P('ctx'), may hold values from 0.25 to 1.75
- key_gain: bfloat16 [64], P('ctx'), may hold values from 0.25 to 1.75
- output_weight: bfloat16 [1536, 1536], P('tp', 'ctx'), may hold values from -2.5 to 2.5
- ffn_gain: bfloat16 [1536], P('ctx'), may hold values from 0.5 to 1.5
- gate_weight: bfloat16 [1536, 6912], P('ctx', 'tp'), may hold values from -0.15625 to 0.15625
- up_weight: bfloat16 [1536, 6912], P('ctx', 'tp'), may hold values from -0.15625 to 0.15625
- down_weight: bfloat16 [6912, 1536], P('tp', 'ctx'), may hold values from -0.078125 to 0.078125
- out_cotangent: bfloat16 [8192, 1536], P('ctx'), may hold values from -6 to 6
Outputs:
- block_output: bfloat16 [8192, 1536], P('ctx')
- grad_input: float32 [8192, 1536], P('ctx')
- grad_attn_gain: float32 [1536], P('ctx')
- grad_query_weight: float32 [1536, 1536], P('ctx', 'tp')
- grad_key_weight: float32 [1536, 512], P('ctx', 'tp')
- grad_value_weight: float32 [1536, 512], P('ctx', 'tp')
- grad_query_gain: float32 [64], P('ctx')
- grad_key_gain: float32 [64], P('ctx')
- grad_output_weight: float32 [1536, 1536], P('tp', 'ctx')
- grad_ffn_gain: float32 [1536], P('ctx')
- grad_gate_weight: float32 [1536, 6912], P('ctx', 'tp')
- grad_up_weight: float32 [1536, 6912], P('ctx', 'tp')
- grad_down_weight: float32 [6912, 1536], P('tp', 'ctx')
The draws below stay inside these ranges and needn't reach their ends.
Inputs may be any that keep to these rules, and one draw needn't show every extreme that they name: positions holds every one of 0 to 8191 once; each aligned run of 256 stored rows holds 256 consecutive increasing positions, the runs in any order.
All inputs are finite; a program needn't handle non-finite values.
Results may differ from the reference program's by a relative error of at most 0.039.
Values may be sent and summed in bfloat16 or wider, within the bound.
A program may use at most 128 MiB of HBM per device.

```python
import math
import jax
import jax.numpy as jnp
from jax import lax

D = 1536
HQ = 24
KVH = 8
HD = 64
FF = 6912
SEQ = 8192
HALF = 256
GROUP = 3


def draw_positions(key, part):
    key = jax.random.fold_in(key, 11)
    run_order = jax.random.permutation(key, SEQ // HALF).astype(jnp.int32)
    offsets = jnp.arange(HALF, dtype=jnp.int32)
    return (run_order[:, None] * HALF + offsets[None, :]).reshape(SEQ)


def block_scale(key, extent, pieces, smallest, top_value):
    level, own = 1.0, jax.random.fold_in(key, 6)
    for dim, blocks in pieces:
        draws = jnp.exp(jax.random.uniform(jax.random.fold_in(own, dim), (blocks,), jnp.float32, smallest / len(pieces), top_value / len(pieces)))
        level = level * jnp.repeat(draws, extent[dim] // blocks).reshape([-1 if axis == dim else 1 for axis in range(len(extent))])
    return level


def normal_values(own_key, dims, scale, reach, pieces=(), held_as=jnp.bfloat16):
    values = jax.random.normal(own_key, dims, jnp.float32) * scale
    if len(pieces) > 0:
        values = block_scale(own_key, dims, pieces, -0.22, 0.18) * values
    return jnp.clip(values, min=-reach, max=reach).astype(held_as)


def setup_inputs(seed: int = 0) -> dict:
    streams_of = jax.random.split(jax.random.key(seed), 15)
    return {
        "block_input": normal_values(streams_of[0], (SEQ, D), 1.0, 6.0, ((0, 16),)),
        "positions": draw_positions(jax.random.fold_in(streams_of[14], 71), 0),
        "attn_gain": jnp.clip(1.0 + 0.1 * jax.random.normal(streams_of[2], (D,), jnp.float32), 0.5, 1.5).astype(jnp.bfloat16),
        "query_weight": normal_values(streams_of[3], (D, HQ * HD), D ** -0.5, 0.15625, ((0, 16), (1, 8))),
        "key_weight": normal_values(streams_of[4], (D, KVH * HD), D ** -0.5, 0.15625, ((0, 16), (1, 8))),
        "value_weight": normal_values(streams_of[5], (D, KVH * HD), D ** -0.5, 0.15625, ((0, 16), (1, 8))),
        "query_gain": jnp.clip(1.0 + 0.15 * jax.random.normal(streams_of[6], (HD,), jnp.float32), 0.25, 1.75).astype(jnp.bfloat16),
        "key_gain": jnp.clip(1.0 + 0.15 * jax.random.normal(streams_of[7], (HD,), jnp.float32), 0.25, 1.75).astype(jnp.bfloat16),
        "output_weight": normal_values(streams_of[8], (HQ * HD, D), (max(1, HQ * HD * 32 // SEQ)) ** -0.5, 2.5, ((0, 8), (1, 16))),
        "ffn_gain": jnp.clip(1.0 + 0.1 * jax.random.normal(streams_of[9], (D,), jnp.float32), 0.5, 1.5).astype(jnp.bfloat16),
        "gate_weight": normal_values(streams_of[10], (D, FF), D ** -0.5, 0.15625, ((0, 16), (1, 8))),
        "up_weight": normal_values(streams_of[11], (D, FF), D ** -0.5, 0.15625, ((0, 16), (1, 8))),
        "down_weight": normal_values(streams_of[12], (FF, D), FF ** -0.5, 0.078125, ((0, 8), (1, 16))),
        "out_cotangent": normal_values(streams_of[13], (SEQ, D), 1.0, 6.0, ((0, 16),)),
    }


@jax.custom_vjp
def low(v):
    return lax.optimization_barrier(v.astype(jnp.bfloat16)).astype(jnp.float32)

@jax.custom_vjp
def low_back(v):
    return v

def low_keep(v):
    return (low(v), None)

def low_pass(kept, grad):
    return (grad,)

def back_keep(v):
    return (v, None)

def back_low(kept, grad):
    return (low(grad),)
low.defvjp(low_keep, low_pass)
low_back.defvjp(back_keep, back_low)
EPS = 1e-05
THETA = 1000000.0
NEG = -1e+30

def matmul(left, right):
    return jnp.dot(left, right, precision=lax.Precision.HIGHEST, preferred_element_type=jnp.float32)

def rms_scale(value):
    return value * lax.rsqrt(lax.optimization_barrier(jnp.mean(value * value, axis=-1, keepdims=True)) + EPS)

def rotary_tables(places, width):
    half_width = width // 2
    freq_table = THETA ** (-(jnp.arange(half_width, dtype=jnp.float32) * 2.0 / width))
    angles = places.astype(jnp.float32)[:, None] * freq_table[None, :]
    cosine_table = jnp.concatenate([jnp.cos(angles), jnp.cos(angles)], axis=-1)
    sine_table = jnp.concatenate([jnp.sin(angles), jnp.sin(angles)], axis=-1)
    return (cosine_table[:, None, :], sine_table[:, None, :])

def rotate(value, cosine_table, sine_table):
    half_width = value.shape[-1] // 2
    turned = jnp.concatenate([-value[..., half_width:], value[..., :half_width]], axis=-1)
    return value * cosine_table + turned * sine_table

def forward(block_input, positions, attn_gain, query_weight, key_weight, value_weight, query_gain, key_gain, output_weight, ffn_gain, gate_weight, up_weight, down_weight):
    seq_len = block_input.shape[0]
    hidden_one = low(rms_scale(block_input) * attn_gain)
    query_raw = low_back(matmul(hidden_one, query_weight)).reshape(seq_len, HQ, HD)
    key_raw = low_back(matmul(hidden_one, key_weight)).reshape(seq_len, KVH, HD)
    value_rows = low(low_back(matmul(hidden_one, value_weight))).reshape(seq_len, KVH, HD)
    cosine_table, sine_table = rotary_tables(positions, HD)
    queries = low(rotate(rms_scale(query_raw) * query_gain, cosine_table, sine_table))
    key_rows = low(rotate(rms_scale(key_raw) * key_gain, cosine_table, sine_table))
    query_heads = queries.transpose(1, 0, 2).reshape(KVH, GROUP, seq_len, HD)
    key_heads = key_rows.transpose(1, 0, 2)
    value_heads = value_rows.transpose(1, 0, 2)
    block_rows = math.gcd(seq_len, 512)

    def attend(block_index):
        first = block_index * block_rows
        query_part = lax.dynamic_slice_in_dim(query_heads, first, block_rows, 2)
        query_pos = lax.dynamic_slice_in_dim(positions, first, block_rows, 0)
        scores = jnp.einsum('kgqd,ksd->kgqs', query_part, key_heads, precision=lax.Precision.HIGHEST)
        scores = low_back(scores * HD ** (-0.5))
        allowed = positions[None, :] <= query_pos[:, None]
        scores = jnp.where(allowed, scores, NEG)
        row_max = lax.optimization_barrier(jnp.max(scores, axis=-1, keepdims=True))
        weights = jnp.exp(scores - row_max)
        row_sum = lax.optimization_barrier(jnp.sum(weights, axis=-1, keepdims=True))
        summed = jnp.einsum('kgqs,ksd->kgqd', low(weights), value_heads, precision=lax.Precision.HIGHEST)
        return low_back(summed) / row_sum
    attended = lax.map(jax.checkpoint(attend), jnp.arange(seq_len // block_rows, dtype=jnp.int32))
    attended = attended.transpose(0, 3, 1, 2, 4).reshape(seq_len, HQ * HD)
    residual_mid = block_input + low_back(matmul(low(attended), output_weight))
    hidden_two = low(rms_scale(residual_mid) * ffn_gain)
    gate = low_back(matmul(hidden_two, gate_weight))
    up_proj = low_back(matmul(hidden_two, up_weight))
    activation = low(jax.nn.silu(gate) * up_proj)
    return residual_mid + matmul(activation, down_weight)

def reference(block_input, positions, attn_gain, query_weight, key_weight, value_weight, query_gain, key_gain, output_weight, ffn_gain, gate_weight, up_weight, down_weight, out_cotangent):
    floats = tuple((array.astype(jnp.float32) for array in (block_input, attn_gain, query_weight, key_weight, value_weight, query_gain, key_gain, output_weight, ffn_gain, gate_weight, up_weight, down_weight)))

    def local_forward(*arrays):
        return forward(arrays[0], positions, *arrays[1:])
    result, pullback = jax.vjp(local_forward, *floats)
    grads = pullback(out_cotangent.astype(jnp.float32))
    return (result.astype(jnp.bfloat16), grads[0], grads[1], grads[2], grads[3], grads[4], grads[5], grads[6], grads[7], grads[8], grads[9], grads[10], grads[11])
```

```python
import functools
import math

import jax
import jax.numpy as jnp
from jax import lax
from jax.experimental import pallas as pl
from jax.experimental.pallas import tpu as pltpu
from jax.sharding import PartitionSpec as P

HD = 64
EPS = 1e-05
THETA = 1000000.0
LOG2E = math.log2(math.e)
LN2 = math.log(2.0)
BF = jnp.bfloat16
F32 = jnp.float32
MESH = pl.DeviceIdType.MESH
VM = pl.BlockSpec(memory_space=pltpu.VMEM)
SM = pl.BlockSpec(memory_space=pltpu.SMEM)
HB = pl.BlockSpec(memory_space=pl.ANY)
DMA = pltpu.SemaphoreType.DMA


class Place:
    def __init__(self):
        self.c = lax.axis_index("ctx")
        self.t = lax.axis_index("tp")
        self.core = lax.rem(self.c, 2)
        self.x = lax.rem(self.c // 2, 4)
        self.zh = self.c // 8
        self.y = lax.rem(self.t, 4)
        self.zl = self.t // 4

    def ctx(self, dz, dx, other=0):
        core = self.core if not other else 1 - self.core
        zh = self.zh if not dz else 1 - self.zh
        return (zh * 4 + lax.rem(self.x + dx, 4)) * 2 + core

    def tp(self, dz, dy):
        zl = self.zl if not dz else 1 - self.zl
        return zl * 4 + lax.rem(self.y + dy, 4)


def greet(peers):
    barrier = pltpu.get_barrier_semaphore()
    for peer in peers:
        pl.semaphore_signal(barrier, inc=1, device_id=peer, device_id_type=MESH)
    pl.semaphore_wait(barrier, len(peers))


class Gather:
    def __init__(self, buf, rows, block, pair, right, left, sibling, send, recv, own=None):
        self.buf, self.rows, self.block = buf, rows, block
        self.to = {"z": pair, "r": right, "l": left, "s": sibling}
        self.send, self.recv, self.own = send, recv, own
        self.plan = {
            0: ((0, 0), 0, "z"),
            1: ((0, 0), 0, "r"),
            2: ((0, 0), 0, "l"),
            3: ((0, 3), 1, "r"),
            4: ((0, 1), 2, "l"),
            5: ((1, 0), 0, "r"),
            6: ((1, 0), 0, "l"),
            7: ((1, 3), 1, "r"),
            8: ((1, 1), 2, "l"),
            9: ((0, 0), 0, "s"),
            10: ((1, 0), 0, "s"),
            11: ((0, 3), 0, "s"),
            12: ((0, 1), 0, "s"),
            13: ((0, 2), 0, "s"),
            14: ((1, 3), 0, "s"),
            15: ((1, 1), 0, "s"),
            16: ((1, 2), 0, "s"),
        }
        self.count = 17 if sibling is not None else 9

    def copy(self, k):
        where, part, to = self.plan[k]
        rows = self.rows if part == 0 else self.rows // 2
        start = pl.multiple_of(self.block(*where) * self.rows, self.rows)
        if part == 2:
            start = pl.multiple_of(start + rows, rows)
        there = self.buf.at[pl.ds(start, rows)]
        here = there
        if where == (0, 0) and self.own is not None:
            here = self.own
        return pltpu.make_async_remote_copy(
            src_ref=here,
            dst_ref=there,
            send_sem=self.send.at[k],
            recv_sem=self.recv.at[k],
            device_id=self.to[to],
            device_id_type=MESH,
        )

    def go(self, *which):
        for k in which:
            if k < self.count:
                self.copy(k).start()

    def got(self, *which):
        for k in which:
            if k < self.count:
                self.copy(k).wait_recv()

    def begin(self):
        self.go(0, 1, 2, 9)

    def near(self):
        self.got(1)
        self.go(3, 11)
        self.got(2)
        self.go(4, 12)

    def pair(self):
        self.got(0)
        self.go(5, 6, 10)

    def far(self):
        self.got(5)
        self.go(7, 14)
        self.got(6)
        self.go(8, 15)
        self.got(3, 4)
        self.go(13)

    def last(self):
        self.got(7, 8)
        self.go(16)

    def sent(self):
        for k in range(self.count):
            self.copy(k).wait_send()

    def end(self):
        self.got(*range(9, 17))
        self.sent()


def ctx_neighbours(me):
    return (
        (me.ctx(1, 0), me.t),
        (me.ctx(0, 1), me.t),
        (me.ctx(0, 3), me.t),
        (me.ctx(0, 0, 1), me.t),
    )


def tp_neighbours(me):
    return (me.c, me.tp(1, 0)), (me.c, me.tp(0, 1)), (me.c, me.tp(0, 3))


def rms_inverse(value):
    return lax.rsqrt(jnp.mean(value * value, axis=-1, keepdims=True) + EPS)


def column_inverse(value):
    return lax.rsqrt(jnp.mean(value * value, axis=0, keepdims=True) + EPS)


def gain_columns(wq):
    total = wq[0:64, 256:384].astype(F32)
    for k in range(1, 16):
        total += wq[96 * k : 96 * k + 64, 256:384].astype(F32)
    return total[:, 64:65], total[:, 65:66]


def dot(a, b):
    return jnp.dot(a, b, preferred_element_type=F32)


def dot_nt(a, b):
    return lax.dot_general(a, b, (((1,), (1,)), ((), ())), preferred_element_type=F32)


def dot_tn(a, b):
    return lax.dot_general(a, b, (((0,), (0,)), ((), ())), preferred_element_type=F32)


PAIRS = ((0, 0), (0, 3), (0, 1), (1, 0), (0, 2), (1, 3), (1, 1), (1, 2))


def pair_of(me, step):
    dz = sum(jnp.where(step == k, p[0], 0) for k, p in enumerate(PAIRS) if p[0])
    dx = sum(jnp.where(step == k, p[1], 0) for k, p in enumerate(PAIRS) if p[1])
    zh = lax.rem(me.zh + dz, 2)
    return (zh * 4 + lax.rem(me.x + dx, 4)) * 2


def forward_kernel(
    kb, x_ref, wq_s, wf_s, cos_ref, sin_ref,
    wq, wf, wo, kv, qt, raw, att, sums, normed,
    acc, s_w, r_w, s_f, r_f, s_o, r_o, s_k, r_k, s_a, r_a, s_l,
):
    me = Place()
    ctx_z, ctx_r, ctx_l, ctx_s = ctx_neighbours(me)
    tp_z, tp_r, tp_l = tp_neighbours(me)
    tokens = x_ref.shape[0]
    greet([ctx_z, ctx_r, ctx_l, ctx_s, tp_z, tp_r, tp_l])
    weights = Gather(wq, 96, me.ctx, ctx_z, ctx_r, ctx_l, ctx_s, s_w, r_w, own=wq_s)
    feed = Gather(wf, 96, me.ctx, ctx_z, ctx_r, ctx_l, ctx_s, s_f, r_f, own=wf_s)
    keys = Gather(kv, tokens, me.ctx, ctx_z, ctx_r, ctx_l, ctx_s, s_k, r_k)
    outw = Gather(
        wo, 96, lambda dz, dy: me.tp(dz, dy) * 2 + me.core, tp_z, tp_r, tp_l, ctx_s, s_o, r_o
    )
    share = Gather(att, 192, me.tp, tp_z, tp_r, tp_l, None, s_a, r_a)

    weights.begin()
    mine = pl.multiple_of(me.c * 96, 96)
    keep = [
        pltpu.make_async_copy(wq_s, wq.at[pl.ds(mine, 96)], s_l.at[0]),
        pltpu.make_async_copy(wf_s, wf.at[pl.ds(mine, 96)], s_l.at[1]),
    ]
    for k in keep:
        k.start()

    def norm_rows(i, carry):
        rows = pl.ds(pl.multiple_of(i * 64, 64), 64)
        value = x_ref[rows].astype(F32)
        normed[rows] = (value * rms_inverse(value)).astype(BF)
        return carry

    lax.fori_loop(0, tokens // 64, norm_rows, 0)
    weights.near()
    weights.pair()
    weights.far()
    weights.last()
    keep[0].wait()
    weights.end()

    def project(i, carry):
        cols = pl.ds(pl.multiple_of(i * 256, 256), 256)
        raw[:, cols] = dot(normed[cols], wq[:, 0:384]).T
        return carry

    lax.fori_loop(0, tokens // 256, project, 0)
    query_gain, key_gain = gain_columns(wq)
    cosine, sine = cos_ref[...], sin_ref[...]

    def turned(value, gain):
        hat = value * column_inverse(value) * gain
        a, b = hat[:32], hat[32:]
        return jnp.concatenate([a * cosine - b * sine, b * cosine + a * sine], axis=0)

    both = jnp.concatenate([turned(raw[192:256], key_gain), raw[256:320]], axis=0)
    kv[pl.ds(pl.multiple_of(me.c * tokens, tokens), tokens)] = both.T.astype(BF)
    keys.begin()
    qt[64:128] = jnp.zeros((64, 3 * tokens), BF)
    for h in range(3):
        rows = raw[64 * h : 64 * h + 64]
        qt[0:64, h * tokens : (h + 1) * tokens] = (
            turned(rows, query_gain) * (LOG2E / 8.0)
        ).astype(BF)
    heads = wq[:, 384:640].T
    wo[pl.ds(pl.multiple_of(me.t * 192 + me.core * 96, 96), 96)] = jnp.where(
        me.core == 0, heads[0:96], heads[96:192]
    )
    outw.begin()
    feed.begin()
    acc[...] = jnp.zeros_like(acc)
    ones = jnp.concatenate([jnp.ones((1, 1024), BF), jnp.zeros((15, 1024), BF)], axis=0)
    apart = lax.broadcasted_iota(jnp.int32, (256, 256), 0) - lax.broadcasted_iota(
        jnp.int32, (256, 256), 1
    )

    def key_step(step, carry):
        @pl.when(step == 0)
        def _():
            keys.got(9)

        @pl.when(step == 1)
        def _():
            keys.near()
            keys.got(11)

        @pl.when(step == 2)
        def _():
            keys.pair()
            keys.got(12)

        @pl.when(step == 3)
        def _():
            keys.got(10)
            outw.near()

        @pl.when(step == 4)
        def _():
            keys.far()
            outw.pair()
            keys.got(13)

        @pl.when(step == 5)
        def _():
            keys.got(14)

        @pl.when(step == 6)
        def _():
            keys.last()
            outw.far()
            keys.got(15)

        @pl.when(step == 7)
        def _():
            keys.got(16)

        first = pair_of(me, step)
        rows = kv[pl.ds(pl.multiple_of(first * tokens, 1024), 1024), :]
        scores = dot(rows, qt[...])
        parts = []
        for a in range(4):
            line = []
            for b in range(6):
                sub = scores[a * 256 : a * 256 + 256, b * 256 : b * 256 + 256]
                seen = apart <= kb[me.c * 2 + b % 2] - kb[first * 2 + a]
                line.append(jnp.where(seen, jnp.exp2(sub), 0.0).astype(BF))
            parts.append(jnp.concatenate(line, axis=1))
        weight = jnp.concatenate(parts, axis=0)
        left = jnp.concatenate([rows.T[64:128], ones], axis=0)
        acc[...] += dot(left, weight)
        return carry

    lax.fori_loop(0, 8, key_step, 0)
    total = acc[64:65, :]
    sums[...] = jnp.broadcast_to(total, sums.shape)
    own = pl.multiple_of(me.t * 192, 192)
    for h in range(3):
        cols = slice(h * tokens, (h + 1) * tokens)
        att[pl.ds(own + 64 * h, 64)] = (acc[0:64, cols] / total[:, cols]).astype(BF)
    share.begin()
    outw.last()
    feed.near()
    share.near()
    share.pair()
    feed.pair()
    share.far()
    share.last()
    feed.far()
    keys.sent()
    share.sent()
    outw.end()
    feed.last()
    keep[1].wait()
    feed.end()


def forward_part(kb, block_input, wq_s, wf_s, cosine, sine):
    tokens = block_input.shape[0]
    shapes = [
        jax.ShapeDtypeStruct((1536, 640), BF),
        jax.ShapeDtypeStruct((1536, wf_s.shape[1]), BF),
        jax.ShapeDtypeStruct((1536, 1536), BF),
        jax.ShapeDtypeStruct((16 * tokens, 128), BF),
        jax.ShapeDtypeStruct((128, 3 * tokens), BF),
        jax.ShapeDtypeStruct((384, tokens), F32),
        jax.ShapeDtypeStruct((1536, tokens), BF),
        jax.ShapeDtypeStruct((8, 3 * tokens), F32),
        jax.ShapeDtypeStruct((tokens, 1536), BF),
    ]
    return pl.pallas_call(
        forward_kernel,
        out_shape=shapes,
        in_specs=[SM, VM, VM, HB, VM, VM],
        out_specs=[VM, HB, VM, VM, VM, VM, VM, VM, VM],
        scratch_shapes=[pltpu.VMEM((80, 3 * tokens), F32)]
        + [DMA((17,))] * 8
        + [DMA((9,))] * 2
        + [DMA((2,))],
        name="forward_part",
        compiler_params=pltpu.CompilerParams(
            collective_id=0, has_side_effects=True, vmem_limit_bytes=58 << 20
        ),
    )(kb, block_input, wq_s, wf_s, cosine, sine)


def backward_keys(kb, qt_ref, gt_ref, drift_ref, kv_ref, dq_ref, out_ref):
    me = Place()
    apart = lax.broadcasted_iota(jnp.int32, (256, 256), 0) - lax.broadcasted_iota(
        jnp.int32, (256, 256), 1
    )
    dq_ref[...] = jnp.zeros_like(dq_ref)

    def key_step(j, carry):
        rows = kv_ref[pl.ds(pl.multiple_of(j * 1024, 1024), 1024), :]
        scores = dot(rows, qt_ref[...])
        slopes = dot(rows, gt_ref[...])
        parts, grads = [], []
        for a in range(4):
            line, grad_line = [], []
            for b in range(6):
                at = (slice(a * 256, a * 256 + 256), slice(b * 256, b * 256 + 256))
                seen = apart <= kb[me.c * 2 + b % 2] - kb[j * 4 + a]
                weight = jnp.where(seen, jnp.exp2(scores[at]), 0.0)
                line.append(weight.astype(BF))
                grad_line.append((weight * (slopes[at] - drift_ref[0:1, at[1]])).astype(BF))
            parts.append(jnp.concatenate(line, axis=1))
            grads.append(jnp.concatenate(grad_line, axis=1))
        weight = jnp.concatenate(parts, axis=0)
        grad = jnp.concatenate(grads, axis=0)
        dq_ref[...] += dot(rows.T[0:64], grad)
        key_grad = dot_nt(qt_ref[0:64], grad) * LN2
        value_grad = dot_nt(gt_ref[64:128], weight)
        both = jnp.concatenate([key_grad, value_grad], axis=0).astype(BF)
        out_ref[2 * j] = both[:, 0:512]
        out_ref[2 * j + 1] = both[:, 512:1024]
        return carry

    lax.fori_loop(0, 8, key_step, 0)


def backward_part(kb, qt, gt, drift, kv):
    return pl.pallas_call(
        backward_keys,
        out_shape=[
            jax.ShapeDtypeStruct((64, 1536), F32),
            jax.ShapeDtypeStruct((16, 128, 512), BF),
        ],
        in_specs=[SM, VM, VM, VM, VM],
        out_specs=[VM, VM],
        name="backward_keys",
        compiler_params=pltpu.CompilerParams(vmem_limit_bytes=58 << 20),
    )(kb, qt, gt, drift, kv)


def rotary_tables(places, width):
    half_width = width // 2
    freq_table = THETA ** (-(jnp.arange(half_width, dtype=F32) * 2.0 / width))
    angles = freq_table[:, None] * places.astype(F32)[None, :]
    return jnp.cos(angles), jnp.sin(angles)


def cut_along(shard, dim, devices):
    dims = shard.shape
    blocks = shard.reshape(*dims[:dim], devices, dims[dim] // devices, *dims[dim + 1 :])
    return jnp.moveaxis(blocks, dim, 0)


def row_reduce(partial):
    blocks = cut_along(partial.astype(BF), 0, lax.axis_size("tp"))
    arrived = lax.all_to_all(blocks, "tp", split_axis=0, concat_axis=0, tiled=True)
    return arrived.astype(F32).sum(axis=0)


def row_collect(rows):
    return lax.all_gather(rows, "tp", axis=0, tiled=True)


def body(
    block_input, positions, attn_gain, query_weight, key_weight, value_weight, query_gain,
    key_gain, output_weight, ffn_gain, gate_weight, up_weight, down_weight, out_cotangent,
):
    tokens = block_input.shape[0]
    c, t = lax.axis_index("ctx"), lax.axis_index("tp")
    gain_one = attn_gain.astype(F32)[:, None]
    gain_two = ffn_gain.astype(F32)[:, None]
    kb = positions.reshape(32, 256)[:, 0]
    own_pos = lax.dynamic_slice_in_dim(positions, c * tokens, tokens, 0)
    cosine, sine = rotary_tables(own_pos, HD)
    spot = (jnp.arange(96)[:, None] == 4 * c + jnp.arange(4)[None, :]).astype(F32)
    head_gains = jnp.stack(
        [spot @ query_gain.astype(F32), spot @ key_gain.astype(F32)], axis=1
    ).astype(BF)

    def lifted(weight, gain):
        return (weight.astype(F32) * gain).astype(BF)

    def padded(weight, width):
        return jnp.pad(weight, ((0, 0), (0, width - weight.shape[1])))

    wq_s = jnp.concatenate(
        [
            lifted(query_weight, gain_one),
            lifted(key_weight, gain_one),
            lifted(value_weight, gain_one),
            padded(head_gains, 64),
            output_weight.T,
            jnp.zeros((96, 64), BF),
        ],
        axis=1,
    )
    wf_s = jnp.concatenate(
        [
            padded(lifted(gate_weight, gain_two), 896),
            padded(lifted(up_weight, gain_two), 896),
            padded(down_weight.T, 896),
        ],
        axis=1,
    )
    wq, wf, wo, kv, qt, raw, att, sums, normed = forward_part(
        kb, block_input, wq_s, wf_s, cosine, sine
    )
    x = block_input.astype(F32)
    mid = x + dot_tn(att, wo)
    inv_two = rms_inverse(mid)
    normed_two = mid * inv_two
    low_two = normed_two.astype(BF)
    gate_full, up_full, down_full = wf[:, 0:896], wf[:, 896:1792], wf[:, 1792:2688]
    gate = dot(low_two, gate_full)
    up = dot(low_two, up_full)
    sig = jax.nn.sigmoid(gate)
    act = (gate * sig * up).astype(BF)
    ffn_part = dot_nt(act, down_full)
    grad_act = dot(out_cotangent, down_full)
    grad_gate = (grad_act * up * sig * (1.0 + gate * (1.0 - sig))).astype(BF)
    grad_up = (grad_act * gate * sig).astype(BF)
    down_grad = dot_tn(out_cotangent, act)
    gate_grad = dot_tn(low_two, grad_gate)
    up_grad = dot_tn(low_two, grad_up)
    back_two = dot_nt(grad_gate, gate_full) + dot_nt(grad_up, up_full)
    gain_two_part = jnp.sum(back_two * normed_two, axis=0)
    pull = jnp.mean(back_two * normed_two, axis=-1, keepdims=True)
    share_mid = (
        out_cotangent.astype(F32) * 0.125 + inv_two * (back_two - normed_two * pull)
    ).astype(BF)
    grad_att = row_reduce(dot_nt(wo, share_mid))
    rows = tokens // 8

    def own_rows(a):
        return lax.dynamic_slice_in_dim(a, t * rows, rows, 0)

    block_output = row_collect((own_rows(mid) + row_reduce(ffn_part)).astype(BF))
    grad_mid = row_reduce(share_mid)
    grad_branch = row_collect(grad_mid.astype(BF))
    own_att = lax.dynamic_slice_in_dim(att, t * 192, 192, 0)
    out_grad = lax.dot_general(
        grad_branch, own_att, (((0,), (1,)), ((), ())), preferred_element_type=F32
    )
    total = sums[0].reshape(3, 1, tokens)
    heads = grad_att.reshape(3, HD, tokens)
    drift = jnp.sum(heads * own_att.reshape(3, HD, tokens).astype(F32), axis=1, keepdims=True) / total
    scaled = (heads / total).astype(BF).transpose(1, 0, 2).reshape(HD, 3 * tokens)
    gt = jnp.concatenate([jnp.zeros_like(scaled), scaled], axis=0)
    drift8 = jnp.broadcast_to(drift.reshape(1, 3 * tokens), (8, 3 * tokens))
    grad_q, grad_kv = backward_part(kb, qt, gt, drift8, kv)
    own_kv = lax.psum_scatter(
        grad_kv.reshape(16 * 128, 512), "ctx", scatter_dimension=0, tiled=True
    ).astype(F32)
    gains = wq.reshape(16, 96, 640)[:, :64, 320:322].astype(F32).sum(axis=0)

    def unturn(grad, value, gain):
        hat_inv = column_inverse(value)
        hat = value * hat_inv
        a, b = grad[:32], grad[32:]
        plain = jnp.concatenate([a * cosine + b * sine, b * cosine - a * sine], axis=0)
        gain_grad = jnp.sum(plain * hat, axis=1)
        pulled = plain * gain
        return gain_grad, (
            hat_inv * (pulled - hat * jnp.mean(pulled * hat, axis=0, keepdims=True))
        ).astype(BF)

    parts, qg_grad = [], 0.0
    for h in range(3):
        g, back = unturn(
            grad_q[:, h * tokens : (h + 1) * tokens] * 0.125, raw[64 * h : 64 * h + 64], gains[:, 0:1]
        )
        qg_grad += g
        parts.append(back)
    kg_grad, key_back = unturn(own_kv[0:64], raw[192:256], gains[:, 1:2])
    pre = jnp.concatenate(parts + [key_back, own_kv[64:128].astype(BF)], axis=0)
    qkv_grad = lax.dot_general(normed, pre, (((0,), (1,)), ((), ())), preferred_element_type=F32)
    back_part = lax.dot_general(
        pre, wq[:, 0:320], (((0,), (1,)), ((), ())), preferred_element_type=F32
    )
    inv_one = rms_inverse(x)
    normed_one = x * inv_one
    gain_one_part = jnp.sum(back_part * normed_one, axis=0)
    back_one = row_reduce(back_part)
    own_normed = own_rows(normed_one)
    grad_rows = grad_mid + own_rows(inv_one) * (
        back_one - own_normed * jnp.mean(back_one * own_normed, axis=-1, keepdims=True)
    )
    grad_input = row_collect(grad_rows.astype(BF)).astype(F32)
    vectors = jnp.concatenate([gain_one_part, gain_two_part, qg_grad, kg_grad])
    vectors = lax.psum(vectors, ("ctx", "tp"))
    weight_grads = jnp.concatenate([qkv_grad, out_grad, gate_grad, up_grad, down_grad], axis=1)
    own = lax.psum_scatter(
        weight_grads.astype(BF), "ctx", scatter_dimension=0, tiled=True
    ).astype(F32)

    def mine(a, width):
        return lax.dynamic_slice_in_dim(a, c * width, width, 0)

    return (
        block_output,
        grad_input,
        mine(vectors[0:1536], 96) / gain_one[:, 0],
        own[:, 0:192] * gain_one,
        own[:, 192:256] * gain_one,
        own[:, 256:320] * gain_one,
        mine(vectors[3072:3136], 4),
        mine(vectors[3136:3200], 4),
        own[:, 320:512].T,
        mine(vectors[1536:3072], 96) / gain_two[:, 0],
        own[:, 512 : 512 + 864] * gain_two,
        own[:, 1408 : 1408 + 864] * gain_two,
        own[:, 2304 : 2304 + 864].T,
    )


def solution(mesh):
    in_specs = (
        P("ctx", None),
        P(),
        P("ctx"),
        P("ctx", "tp"),
        P("ctx", "tp"),
        P("ctx", "tp"),
        P("ctx"),
        P("ctx"),
        P("tp", "ctx"),
        P("ctx"),
        P("ctx", "tp"),
        P("ctx", "tp"),
        P("tp", "ctx"),
        P("ctx", None),
    )
    out_specs = (
        P("ctx", None),
        P("ctx", None),
        P("ctx"),
        P("ctx", "tp"),
        P("ctx", "tp"),
        P("ctx", "tp"),
        P("ctx"),
        P("ctx"),
        P("tp", "ctx"),
        P("ctx"),
        P("ctx", "tp"),
        P("ctx", "tp"),
        P("tp", "ctx"),
    )
    return jax.shard_map(body, mesh=mesh, in_specs=in_specs, out_specs=out_specs, check_vma=False)
```

```python
import functools
import math

import jax
import jax.numpy as jnp
from jax import lax
from jax.experimental import pallas as pl
from jax.experimental.pallas import tpu as pltpu
from jax.sharding import PartitionSpec as P

HD = 64
EPS = 1e-05
THETA = 1000000.0
LOG2E = math.log2(math.e)
LN2 = math.log(2.0)
BF = jnp.bfloat16
F32 = jnp.float32
MESH = pl.DeviceIdType.MESH
VM = pl.BlockSpec(memory_space=pltpu.VMEM)
SM = pl.BlockSpec(memory_space=pltpu.SMEM)
HB = pl.BlockSpec(memory_space=pl.ANY)
DMA = pltpu.SemaphoreType.DMA


class Place:
    def __init__(self):
        self.c = lax.axis_index("ctx")
        self.t = lax.axis_index("tp")
        self.core = lax.rem(self.c, 2)
        self.x = lax.rem(self.c // 2, 4)
        self.zh = self.c // 8
        self.y = lax.rem(self.t, 4)
        self.zl = self.t // 4

    def ctx(self, dz, dx, other=0):
        core = self.core if not other else 1 - self.core
        zh = self.zh if not dz else 1 - self.zh
        return (zh * 4 + lax.rem(self.x + dx, 4)) * 2 + core

    def tp(self, dz, dy):
        zl = self.zl if not dz else 1 - self.zl
        return zl * 4 + lax.rem(self.y + dy, 4)


def greet(peers):
    barrier = pltpu.get_barrier_semaphore()
    for peer in peers:
        pl.semaphore_signal(barrier, inc=1, device_id=peer, device_id_type=MESH)
    pl.semaphore_wait(barrier, len(peers))


class Gather:
    def __init__(self, buf, rows, block, pair, right, left, sibling, send, recv, own=None):
        self.buf, self.rows, self.block = buf, rows, block
        self.to = {"z": pair, "r": right, "l": left, "s": sibling}
        self.send, self.recv, self.own = send, recv, own
        self.plan = {
            0: ((0, 0), 0, "z"),
            1: ((0, 0), 0, "r"),
            2: ((0, 0), 0, "l"),
            3: ((0, 3), 1, "r"),
            4: ((0, 1), 2, "l"),
            5: ((1, 0), 0, "r"),
            6: ((1, 0), 0, "l"),
            7: ((1, 3), 1, "r"),
            8: ((1, 1), 2, "l"),
            9: ((0, 0), 0, "s"),
            10: ((1, 0), 0, "s"),
            11: ((0, 3), 0, "s"),
            12: ((0, 1), 0, "s"),
            13: ((0, 2), 0, "s"),
            14: ((1, 3), 0, "s"),
            15: ((1, 1), 0, "s"),
            16: ((1, 2), 0, "s"),
        }
        self.count = 17 if sibling is not None else 9

    def copy(self, k):
        where, part, to = self.plan[k]
        rows = self.rows if part == 0 else self.rows // 2
        start = pl.multiple_of(self.block(*where) * self.rows, self.rows)
        if part == 2:
            start = pl.multiple_of(start + rows, rows)
        there = self.buf.at[pl.ds(start, rows)]
        here = there
        if where == (0, 0) and self.own is not None:
            here = self.own
        return pltpu.make_async_remote_copy(
            src_ref=here,
            dst_ref=there,
            send_sem=self.send.at[k],
            recv_sem=self.recv.at[k],
            device_id=self.to[to],
            device_id_type=MESH,
        )

    def go(self, *which):
        for k in which:
            if k < self.count:
                self.copy(k).start()

    def got(self, *which):
        for k in which:
            if k < self.count:
                self.copy(k).wait_recv()

    def begin(self):
        self.go(0, 1, 2, 9)

    def near(self):
        self.got(1)
        self.go(3, 11)
        self.got(2)
        self.go(4, 12)

    def pair(self):
        self.got(0)
        self.go(5, 6, 10)

    def far(self):
        self.got(5)
        self.go(7, 14)
        self.got(6)
        self.go(8, 15)
        self.got(3, 4)
        self.go(13)

    def last(self):
        self.got(7, 8)
        self.go(16)

    def sent(self):
        for k in range(self.count):
            self.copy(k).wait_send()

    def end(self):
        self.got(*range(9, 17))
        self.sent()


def ctx_neighbours(me):
    return (
        (me.ctx(1, 0), me.t),
        (me.ctx(0, 1), me.t),
        (me.ctx(0, 3), me.t),
        (me.ctx(0, 0, 1), me.t),
    )


def tp_neighbours(me):
    return (me.c, me.tp(1, 0)), (me.c, me.tp(0, 1)), (me.c, me.tp(0, 3))


def rms_inverse(value):
    return lax.rsqrt(jnp.mean(value * value, axis=-1, keepdims=True) + EPS)


def column_inverse(value):
    return lax.rsqrt(jnp.mean(value * value, axis=0, keepdims=True) + EPS)


def gain_columns(wq):
    total = wq[0:64, 256:384].astype(F32)
    for k in range(1, 16):
        total += wq[96 * k : 96 * k + 64, 256:384].astype(F32)
    return total[:, 64:65], total[:, 65:66]


def dot(a, b):
    return jnp.dot(a, b, preferred_element_type=F32)


def dot_nt(a, b):
    return lax.dot_general(a, b, (((1,), (1,)), ((), ())), preferred_element_type=F32)


def dot_tn(a, b):
    return lax.dot_general(a, b, (((0,), (0,)), ((), ())), preferred_element_type=F32)


PAIRS = ((0, 0), (0, 3), (0, 1), (1, 0), (0, 2), (1, 3), (1, 1), (1, 2))


def pair_of(me, step):
    dz = sum(jnp.where(step == k, p[0], 0) for k, p in enumerate(PAIRS) if p[0])
    dx = sum(jnp.where(step == k, p[1], 0) for k, p in enumerate(PAIRS) if p[1])
    zh = lax.rem(me.zh + dz, 2)
    return (zh * 4 + lax.rem(me.x + dx, 4)) * 2


def forward_kernel(
    kb, x_ref, wq_s, wf_s, cos_ref, sin_ref,
    wq, wf, wo, kv, qt, raw, att, sums, normed,
    acc, s_w, r_w, s_f, r_f, s_o, r_o, s_k, r_k, s_a, r_a, s_l,
):
    me = Place()
    ctx_z, ctx_r, ctx_l, ctx_s = ctx_neighbours(me)
    tp_z, tp_r, tp_l = tp_neighbours(me)
    tokens = x_ref.shape[0]
    greet([ctx_z, ctx_r, ctx_l, ctx_s, tp_z, tp_r, tp_l])
    weights = Gather(wq, 96, me.ctx, ctx_z, ctx_r, ctx_l, ctx_s, s_w, r_w, own=wq_s)
    feed = Gather(wf, 96, me.ctx, ctx_z, ctx_r, ctx_l, ctx_s, s_f, r_f, own=wf_s)
    keys = Gather(kv, tokens, me.ctx, ctx_z, ctx_r, ctx_l, ctx_s, s_k, r_k)
    outw = Gather(
        wo, 96, lambda dz, dy: me.tp(dz, dy) * 2 + me.core, tp_z, tp_r, tp_l, ctx_s, s_o, r_o
    )
    share = Gather(att, 192, me.tp, tp_z, tp_r, tp_l, None, s_a, r_a)

    weights.begin()
    mine = pl.multiple_of(me.c * 96, 96)
    keep = [
        pltpu.make_async_copy(wq_s, wq.at[pl.ds(mine, 96)], s_l.at[0]),
        pltpu.make_async_copy(wf_s, wf.at[pl.ds(mine, 96)], s_l.at[1]),
    ]
    for k in keep:
        k.start()

    def norm_rows(i, carry):
        rows = pl.ds(pl.multiple_of(i * 64, 64), 64)
        value = x_ref[rows].astype(F32)
        normed[rows] = (value * rms_inverse(value)).astype(BF)
        return carry

    lax.fori_loop(0, tokens // 64, norm_rows, 0)
    weights.near()
    weights.pair()
    weights.far()
    weights.last()
    keep[0].wait()
    weights.end()

    def project(i, carry):
        cols = pl.ds(pl.multiple_of(i * 256, 256), 256)
        raw[:, cols] = dot(normed[cols], wq[:, 0:384]).T
        return carry

    lax.fori_loop(0, tokens // 256, project, 0)
    query_gain, key_gain = gain_columns(wq)
    cosine, sine = cos_ref[...], sin_ref[...]

    def turned(value, gain):
        hat = value * column_inverse(value) * gain
        a, b = hat[:32], hat[32:]
        return jnp.concatenate([a * cosine - b * sine, b * cosine + a * sine], axis=0)

    both = jnp.concatenate([turned(raw[192:256], key_gain), raw[256:320]], axis=0)
    kv[pl.ds(pl.multiple_of(me.c * tokens, tokens), tokens)] = both.T.astype(BF)
    keys.begin()
    qt[64:128] = jnp.zeros((64, 3 * tokens), BF)
    for h in range(3):
        rows = raw[64 * h : 64 * h + 64]
        qt[0:64, h * tokens : (h + 1) * tokens] = (
            turned(rows, query_gain) * (LOG2E / 8.0)
        ).astype(BF)
    heads = wq[:, 384:640].T
    wo[pl.ds(pl.multiple_of(me.t * 192 + me.core * 96, 96), 96)] = jnp.where(
        me.core == 0, heads[0:96], heads[96:192]
    )
    outw.begin()
    feed.begin()
    acc[...] = jnp.zeros_like(acc)
    ones = jnp.concatenate([jnp.ones((1, 1024), BF), jnp.zeros((15, 1024), BF)], axis=0)
    apart = lax.broadcasted_iota(jnp.int32, (256, 256), 0) - lax.broadcasted_iota(
        jnp.int32, (256, 256), 1
    )

    def key_step(step, carry):
        @pl.when(step == 0)
        def _():
            keys.got(9)

        @pl.when(step == 1)
        def _():
            keys.near()
            keys.got(11)

        @pl.when(step == 2)
        def _():
            keys.pair()
            keys.got(12)

        @pl.when(step == 3)
        def _():
            keys.got(10)
            outw.near()

        @pl.when(step == 4)
        def _():
            keys.far()
            outw.pair()
            keys.got(13)

        @pl.when(step == 5)
        def _():
            keys.got(14)

        @pl.when(step == 6)
        def _():
            keys.last()
            outw.far()
            keys.got(15)

        @pl.when(step == 7)
        def _():
            keys.got(16)

        first = pair_of(me, step)
        rows = kv[pl.ds(pl.multiple_of(first * tokens, 1024), 1024), :]
        scores = dot(rows, qt[...])
        parts = []
        for a in range(4):
            line = []
            for b in range(6):
                sub = scores[a * 256 : a * 256 + 256, b * 256 : b * 256 + 256]
                seen = apart <= kb[me.c * 2 + b % 2] - kb[first * 2 + a]
                line.append(jnp.where(seen, jnp.exp2(sub), 0.0).astype(BF))
            parts.append(jnp.concatenate(line, axis=1))
        weight = jnp.concatenate(parts, axis=0)
        left = jnp.concatenate([rows.T[64:128], ones], axis=0)
        acc[...] += dot(left, weight)
        return carry

    lax.fori_loop(0, 8, key_step, 0)
    total = acc[64:65, :]
    sums[...] = jnp.broadcast_to(total, sums.shape)
    own = pl.multiple_of(me.t * 192, 192)
    for h in range(3):
        cols = slice(h * tokens, (h + 1) * tokens)
        att[pl.ds(own + 64 * h, 64)] = (acc[0:64, cols] / total[:, cols]).astype(BF)
    share.begin()
    outw.last()
    feed.near()
    share.near()
    share.pair()
    feed.pair()
    share.far()
    share.last()
    feed.far()
    keys.sent()
    share.sent()
    outw.end()
    feed.last()
    keep[1].wait()
    feed.end()


def forward_part(kb, block_input, wq_s, wf_s, cosine, sine):
    tokens = block_input.shape[0]
    shapes = [
        jax.ShapeDtypeStruct((1536, 640), BF),
        jax.ShapeDtypeStruct((1536, wf_s.shape[1]), BF),
        jax.ShapeDtypeStruct((1536, 1536), BF),
        jax.ShapeDtypeStruct((16 * tokens, 128), BF),
        jax.ShapeDtypeStruct((128, 3 * tokens), BF),
        jax.ShapeDtypeStruct((384, tokens), F32),
        jax.ShapeDtypeStruct((1536, tokens), BF),
        jax.ShapeDtypeStruct((8, 3 * tokens), F32),
        jax.ShapeDtypeStruct((tokens, 1536), BF),
    ]
    return pl.pallas_call(
        forward_kernel,
        out_shape=shapes,
        in_specs=[SM, VM, VM, HB, VM, VM],
        out_specs=[VM, HB, VM, VM, VM, VM, VM, VM, VM],
        scratch_shapes=[pltpu.VMEM((80, 3 * tokens), F32)]
        + [DMA((17,))] * 8
        + [DMA((9,))] * 2
        + [DMA((2,))],
        name="forward_part",
        compiler_params=pltpu.CompilerParams(
            collective_id=0, has_side_effects=True, vmem_limit_bytes=58 << 20
        ),
    )(kb, block_input, wq_s, wf_s, cosine, sine)


SLOTS = ((0, 2), (1, 2), (1, 1), (1, 3), (0, 1), (0, 3), (1, 0), (0, 0))


def slot_chip(me, step):
    dz = sum(jnp.where(step == k, p[0], 0) for k, p in enumerate(SLOTS) if p[0])
    dx = sum(jnp.where(step == k, p[1], 0) for k, p in enumerate(SLOTS) if p[1])
    return lax.rem(me.zh + dz, 2) * 4 + lax.rem(me.x + dx, 4)


def add_into(out, *terms):
    total = terms[0][...].astype(F32)
    for term in terms[1:]:
        total += term[...].astype(F32)
    out[...] = total.astype(out.dtype)


class RingSum:
    def __init__(self, src, half, stage, rel_l, rel_r, col_l, col_r, from_z, pair, right, left, send, recv):
        self.src, self.half = src, half
        at_stage = {2: (0, 0), 3: (0, 1), 4: (1, 0), 5: (1, 1)}

        def put(k, part):
            if stage is None:
                return src(k, part)
            rows = pl.ds(part * half, half)
            return stage.at[2 if k == 6 else at_stage[k][0], rows]

        self.put = put
        self.rel_l, self.rel_r, self.col_l, self.col_r, self.from_z = rel_l, rel_r, col_l, col_r, from_z
        self.to = {"z": pair, "r": right, "l": left}
        self.send, self.recv = send, recv
        low, high = pl.ds(0, half), pl.ds(half, half)
        self.low, self.high = low, high
        self.plan = [
            (src(1, 0), rel_l.at[1], "r"),
            (src(1, 1), rel_r.at[1], "l"),
            (src(0, 0), rel_l.at[0], "r"),
            (src(0, 1), rel_r.at[0], "l"),
            (src(2, 1), col_l.at[1, high], "r"),
            (src(3, 0), col_r.at[1, low], "l"),
            (src(4, 1), col_l.at[0, high], "r"),
            (src(5, 0), col_r.at[0, low], "l"),
            (put(2, 0), col_l.at[1, low], "r"),
            (put(3, 1), col_r.at[1, high], "l"),
            (put(4, 0), col_l.at[0, low], "r"),
            (put(5, 1), col_r.at[0, high], "l"),
            (put(6, 0), from_z.at[low], "z"),
            (put(6, 1), from_z.at[high], "z"),
        ]

    def copy(self, k):
        here, there, to = self.plan[k]
        return pltpu.make_async_remote_copy(
            src_ref=here,
            dst_ref=there,
            send_sem=self.send.at[k],
            recv_sem=self.recv.at[k],
            device_id=self.to[to],
            device_id_type=MESH,
        )

    def go(self, *which):
        for k in which:
            self.copy(k).start()

    def got(self, *which):
        for k in which:
            self.copy(k).wait_recv()

    def begin(self):
        self.go(*range(8))

    def relay_right(self, plane):
        k = 2 if plane else 4
        self.got(0 if plane else 2)
        add_into(self.put(k, 0), self.src(k, 0), self.rel_l.at[plane])
        self.go(8 if plane else 10)

    def relay_left(self, plane):
        k = 3 if plane else 5
        self.got(1 if plane else 3)
        add_into(self.put(k, 1), self.src(k, 1), self.rel_r.at[plane])
        self.go(9 if plane else 11)

    def relay(self):
        for plane in (1, 0):
            self.relay_right(plane)
            self.relay_left(plane)

    def column(self):
        self.got(4, 8, 5, 9)
        for part, rows in enumerate((self.low, self.high)):
            add_into(
                self.put(6, part),
                self.src(6, part),
                self.col_l.at[1, rows],
                self.col_r.at[1, rows],
            )
            self.go(12 + part)

    def finish(self, part):
        if part == 0:
            self.got(6, 10, 7, 11, 12, 13)
        rows = self.low if part == 0 else self.high
        total = self.src(7, part)[...].astype(F32)
        for term in (self.col_l.at[0, rows], self.col_r.at[0, rows], self.from_z.at[rows]):
            total += term[...].astype(F32)
        return total

    def sent(self):
        for k in range(14):
            self.copy(k).wait_send()


def ring_scratch(half, width, stage=False):
    return [
        pltpu.VMEM((3, 2 * half, width) if stage else (1, 16, 128), BF),
        pltpu.VMEM((2, half, width), BF),
        pltpu.VMEM((2, half, width), BF),
        pltpu.VMEM((2, 2 * half, width), BF),
        pltpu.VMEM((2, 2 * half, width), BF),
        pltpu.VMEM((2 * half, width), BF),
        DMA((14,)),
        DMA((14,)),
    ]


def ring(src, half, scratch, neighbours, stage=False):
    room, rel_l, rel_r, col_l, col_r, from_z, send, recv = scratch
    return RingSum(
        src, half, room if stage else None, rel_l, rel_r, col_l, col_r, from_z, *neighbours[:3],
        send, recv,
    )


def backward_kernel(
    kb, u_ref, ffn_ref, share_ref, mid_ref, gate_g, up_g, down_g, gain_two,
    x_ref, normed, wq, raw, att_own, sums, qt, kv, cos_ref, sin_ref,
    two, gin, own_q, own_w, gains,
    mid_rows, gt, drift, dq, gk, gk_sib, part_w, sib_w, pw, sib_p, back, pre, extra,
    s_two, r_two, s_in, r_in, s_ex, r_ex, s_sib, r_sib, s_loc,
    *rest,
):
    me = Place()
    cn = ctx_neighbours(me)
    tn = tp_neighbours(me)
    sib = cn[3]
    tokens = normed.shape[0]
    scratch = [rest[8 * k : 8 * k + 8] for k in range(8)]
    greet([*cn, *tn])

    def tp_block(k):
        return me.tp(*SLOTS[k])

    def chip(k):
        dz, dx = SLOTS[k]
        return me.ctx(dz, dx) // 2

    def rows_of(ref, size):
        def src(k, part):
            start = pl.multiple_of(tp_block(k) * size, size) + part * (size // 2)
            return ref.at[pl.ds(pl.multiple_of(start, size // 2), size // 2)]

        return src

    def two_rows(k, part):
        ref = share_ref if part else ffn_ref
        return ref.at[pl.ds(pl.multiple_of(tp_block(k) * 64, 64), 64)]

    sum_u = ring(rows_of(u_ref, 192), 96, scratch[0], tn, True)
    sum_two = ring(two_rows, 64, scratch[1], tn, True)
    sum_b = ring(rows_of(back, 64), 32, scratch[2], tn)
    sum_kv = ring(
        lambda k, part: gk.at[k, me.core, pl.ds(64 * part, 64)], 64, scratch[3], cn
    )
    sum_w = [
        ring(
            lambda k, part, p=p: part_w.at[p, chip(k), pl.ds(48 * part, 48)],
            48,
            scratch[4 + p],
            cn,
        )
        for p in range(3)
    ]
    sum_q = ring(
        lambda k, part: pw.at[chip(k), me.core, pl.ds(48 * part, 48)], 48, scratch[7], cn
    )
    put_two = Gather(two, 128, me.tp, *tn, None, s_two, r_two)
    put_in = Gather(gin, 64, me.tp, *tn, None, s_in, r_in)
    put_ex = Gather(extra, 96, me.tp, *tn, None, s_ex, r_ex)

    def to_sibling(k, here, there):
        return pltpu.make_async_remote_copy(
            src_ref=here,
            dst_ref=there,
            send_sem=s_sib.at[k],
            recv_sem=r_sib.at[k],
            device_id=sib,
            device_id_type=MESH,
        )

    def key_swap(k):
        return to_sibling(k, gk.at[k, 1 - me.core], gk_sib.at[k])

    swap_w = [
        to_sibling(8 + p, g.at[:, 1 - me.core], sib_w.at[p])
        for p, g in enumerate((gate_g, up_g, down_g))
    ]
    swap_p = to_sibling(11, pw.at[:, 1 - me.core], sib_p)
    keep_w = [
        pltpu.make_async_copy(g.at[:, me.core], part_w.at[p], s_loc.at[p])
        for p, g in enumerate((gate_g, up_g, down_g))
    ]

    sum_u.begin()
    for p in range(3):
        swap_w[p].start()
        keep_w[p].start()

    def join_w(p):
        keep_w[p].wait()
        swap_w[p].wait_recv()

        def one(j, carry):
            add_into(part_w.at[p, j], part_w.at[p, j], sib_w.at[p, j])
            return carry

        lax.fori_loop(0, 8, one, 0)

    sum_u.relay()
    join_w(0)
    sum_w[0].begin()
    sum_u.column()
    join_w(1)
    join_w(2)
    halves = [sum_u.finish(0), sum_u.finish(1)]
    grad_att = jnp.concatenate(halves, axis=0)
    sum_two.begin()
    gt[0:64] = jnp.zeros((64, 3 * tokens), BF)
    for h in range(3):
        cols = slice(h * tokens, (h + 1) * tokens)
        grad = grad_att[64 * h : 64 * h + 64]
        inverse = 1.0 / sums[0:1, cols]
        gt[64:128, cols] = (grad * inverse).astype(BF)
        drift[0:1, cols] = (
            jnp.sum(grad * att_own[64 * h : 64 * h + 64].astype(F32), axis=0, keepdims=True)
            * inverse
        )
    dq[...] = jnp.zeros_like(dq)
    sum_w[0].relay()
    sum_w[1].begin()
    apart = lax.broadcasted_iota(jnp.int32, (256, 256), 0) - lax.broadcasted_iota(
        jnp.int32, (256, 256), 1
    )

    def join_keys(k):
        key_swap(k).wait_recv()
        add_into(gk.at[k, me.core], gk.at[k, me.core], gk_sib.at[k])

    def key_step(step, carry):
        @pl.when(step == 1)
        def _():
            join_keys(0)
            sum_kv.go(2, 3)
            sum_w[0].column()
            sum_w[1].relay()
            sum_w[2].begin()

        @pl.when(step == 2)
        def _():
            join_keys(1)
            sum_kv.go(0, 1)
            sum_two.relay()

        @pl.when(step == 3)
        def _():
            join_keys(2)
            sum_kv.go(4)
            sum_kv.relay_right(1)
            sum_w[2].relay()
            sum_w[1].column()

        @pl.when(step == 4)
        def _():
            join_keys(3)
            sum_kv.go(5)
            sum_kv.relay_left(1)
            sum_two.column()

        @pl.when(step == 5)
        def _():
            join_keys(4)
            sum_kv.go(6)
            sum_kv.relay_right(0)
            sum_w[2].column()

        @pl.when(step == 6)
        def _():
            join_keys(5)
            sum_kv.go(7)
            sum_kv.relay_left(0)
            own = pl.multiple_of(me.t * 128, 128)
            two[pl.ds(own, 64)] = (mid_ref[...] + sum_two.finish(0)).astype(BF)
            branch = sum_two.finish(1)
            mid_rows[...] = branch
            two[pl.ds(own + 64, 64)] = branch.astype(BF)
            put_two.begin()

        @pl.when(step == 7)
        def _():
            join_keys(6)
            sum_kv.column()
            for p in range(3):
                for half in range(2):
                    own_w[p, 48 * half : 48 * half + 48] = sum_w[p].finish(half)

        place = slot_chip(me, step)
        rows = kv[pl.ds(pl.multiple_of(place * 1024, 1024), 1024), :]
        key_t = rows.T[0:64]
        key_grad = value_grad = 0.0
        for h in range(3):
            cols = slice(h * tokens, (h + 1) * tokens)
            scores = dot(rows, qt[:, cols])
            slopes = dot(rows, gt[:, cols])
            parts, grads = [], []
            for a in range(4):
                line, grad_line = [], []
                for b in range(2):
                    at = (slice(a * 256, a * 256 + 256), slice(b * 256, b * 256 + 256))
                    seen = apart <= kb[me.c * 2 + b] - kb[place * 4 + a]
                    weight = jnp.where(seen, jnp.exp2(scores[at]), 0.0)
                    line.append(weight.astype(BF))
                    lean = drift[0:1, h * tokens + b * 256 : h * tokens + b * 256 + 256]
                    grad_line.append((weight * (slopes[at] - lean)).astype(BF))
                parts.append(jnp.concatenate(line, axis=1))
                grads.append(jnp.concatenate(grad_line, axis=1))
            weight = jnp.concatenate(parts, axis=0)
            grad = jnp.concatenate(grads, axis=0)
            dq[:, cols] += dot(key_t, grad)
            key_grad += dot_nt(qt[0:64, cols], grad)
            value_grad += dot_nt(gt[64:128, cols], weight)
        both = jnp.concatenate([key_grad * LN2, value_grad], axis=0).astype(BF)
        gk[step, 0] = both[:, 0:512]
        gk[step, 1] = both[:, 512:1024]
        key_swap(step).start()
        return carry

    lax.fori_loop(0, 8, key_step, 0)
    query_gain, key_gain = gain_columns(wq)
    cosine, sine = cos_ref[...], sin_ref[...]

    def unturn(grad, value, gain):
        inverse = column_inverse(value)
        hat = value * inverse
        a, b = grad[:32], grad[32:]
        plain = jnp.concatenate([a * cosine + b * sine, b * cosine - a * sine], axis=0)
        gain_grad = jnp.sum(plain * hat, axis=1, keepdims=True)
        pulled = plain * gain
        back_grad = inverse * (pulled - hat * jnp.mean(pulled * hat, axis=0, keepdims=True))
        return gain_grad, back_grad

    query_gain_grad = 0.0
    for h in range(3):
        part, grad = unturn(
            dq[:, h * tokens : (h + 1) * tokens] * 0.125, raw[64 * h : 64 * h + 64], query_gain
        )
        query_gain_grad += part
        pre[64 * h : 64 * h + 64] = grad
    put_two.near()
    put_two.pair()
    join_keys(7)
    key_grad, value_grad = sum_kv.finish(0), sum_kv.finish(1)
    key_gain_grad, grad = unturn(key_grad, raw[192:256], key_gain)
    pre[192:256] = grad
    pre[256:320] = value_grad
    pre[320:384] = jnp.zeros((64, tokens), F32)
    pre_n = pre[...].T.astype(BF)
    gain_one = 0.0
    for i in range(2):
        rows = slice(256 * i, 256 * i + 256)
        part = dot_nt(pre_n[rows], wq[:, 0:384])
        back[rows] = part.astype(BF)
        gain_one += jnp.sum(part * normed[rows].astype(F32), axis=0, keepdims=True)
    sum_b.begin()
    lane = lax.broadcasted_iota(jnp.int32, (64, 1536), 1)
    unit = lax.broadcasted_iota(jnp.int32, (64, 1536), 0)
    spot = lane == (unit // 4) * 96 + lax.rem(unit, 4)

    def spread(column):
        return jnp.sum(jnp.where(spot, column, 0.0), axis=0, keepdims=True)

    lines = jnp.concatenate(
        [
            jnp.zeros((64, 1536), F32),
            gain_one,
            gain_two[...],
            spread(query_gain_grad),
            spread(key_gain_grad),
            jnp.zeros((60, 1536), F32),
        ],
        axis=0,
    )
    sides = lines.T
    put_two.far()
    put_two.last()
    sum_b.relay()
    att_n = jnp.concatenate([att_own[...].astype(F32), jnp.zeros((64, tokens), F32)], axis=0).T.astype(BF)
    for i in range(4):
        at = slice(384 * i, 384 * i + 384)
        part = dot(normed[:, at].T, pre_n)
        part = jnp.concatenate([part[:, 0:256], part[:, 256:384] + sides[at]], axis=1)
        branch = jnp.concatenate(
            [two[128 * b + 64 : 128 * b + 128, at] for b in range(8)], axis=0
        )
        whole = jnp.concatenate([part, dot(branch.T, att_n)], axis=1).astype(BF)
        for q in range(4):
            pw[2 * i + q // 2, q % 2] = whole[96 * q : 96 * q + 96]
    swap_p.start()
    sum_b.column()
    swap_p.wait_recv()

    def join_p(j, carry):
        add_into(pw.at[j, me.core], pw.at[j, me.core], sib_p.at[j])
        return carry

    lax.fori_loop(0, 8, join_p, 0)
    sum_q.begin()
    own = pl.multiple_of(me.t * 64, 64)
    value = x_ref[...].astype(F32)
    inverse = rms_inverse(value)
    hat = value * inverse
    back_one = jnp.concatenate([sum_b.finish(0), sum_b.finish(1)], axis=0)
    gin[pl.ds(own, 64)] = (
        mid_rows[...]
        + inverse * (back_one - hat * jnp.mean(back_one * hat, axis=-1, keepdims=True))
    ).astype(BF)
    put_in.begin()
    sum_q.relay()
    put_in.near()
    put_in.pair()
    sum_q.column()
    put_in.far()
    for half in range(2):
        own_q[48 * half : 48 * half + 48] = sum_q.finish(half)
    extra[pl.ds(pl.multiple_of(me.t * 96, 96), 96)] = own_q[:, 256:384]
    put_ex.begin()
    put_in.last()
    put_ex.near()
    put_ex.pair()
    put_ex.far()
    put_ex.last()
    total = extra[0:96]
    for b in range(1, 8):
        total += extra[96 * b : 96 * b + 96]
    gains[...] = total
    for s in [sum_u, sum_two, sum_b, sum_kv, sum_q, *sum_w, put_two, put_in, put_ex, ]:
        s.sent()
    for k in range(8):
        key_swap(k).wait_send()
    for s in [*swap_w, swap_p]:
        s.wait_send()


def backward_part(*operands):
    tokens = 512
    shapes = [
        jax.ShapeDtypeStruct((1024, 1536), BF),
        jax.ShapeDtypeStruct((512, 1536), BF),
        jax.ShapeDtypeStruct((96, 640), F32),
        jax.ShapeDtypeStruct((3, 96, 896), F32),
        jax.ShapeDtypeStruct((96, 128), F32),
    ]
    scratch = [
        pltpu.VMEM((64, 1536), F32),
        pltpu.VMEM((128, 3 * tokens), BF),
        pltpu.VMEM((8, 3 * tokens), F32),
        pltpu.VMEM((64, 3 * tokens), F32),
        pltpu.VMEM((8, 2, 128, 512), BF),
        pltpu.VMEM((8, 128, 512), BF),
        pltpu.VMEM((3, 8, 96, 896), BF),
        pltpu.VMEM((3, 8, 96, 896), BF),
        pltpu.VMEM((8, 2, 96, 640), BF),
        pltpu.VMEM((8, 96, 640), BF),
        pltpu.VMEM((tokens, 1536), BF),
        pltpu.VMEM((384, tokens), F32),
        pltpu.VMEM((768, 128), F32),
        *[DMA((9,))] * 6,
        DMA((12,)),
        DMA((12,)),
        DMA((3,)),
        *ring_scratch(96, 512, True),
        *ring_scratch(64, 1536, True),
        *ring_scratch(32, 1536),
        *ring_scratch(64, 512),
        *ring_scratch(48, 896) * 3,
        *ring_scratch(48, 640),
    ]
    return pl.pallas_call(
        backward_kernel,
        out_shape=shapes,
        in_specs=[SM, VM, VM, VM, VM, HB, HB, HB] + [VM] * 11,
        out_specs=[VM] * 5,
        scratch_shapes=scratch,
        name="backward_part",
        compiler_params=pltpu.CompilerParams(
            collective_id=1, has_side_effects=True, vmem_limit_bytes=58 << 20
        ),
    )(*operands)


def rotary_tables(places, width):
    half_width = width // 2
    freq_table = THETA ** (-(jnp.arange(half_width, dtype=F32) * 2.0 / width))
    angles = freq_table[:, None] * places.astype(F32)[None, :]
    return jnp.cos(angles), jnp.sin(angles)


def body(
    block_input, positions, attn_gain, query_weight, key_weight, value_weight, query_gain,
    key_gain, output_weight, ffn_gain, gate_weight, up_weight, down_weight, out_cotangent,
):
    tokens = block_input.shape[0]
    c, t = lax.axis_index("ctx"), lax.axis_index("tp")
    gain_one = attn_gain.astype(F32)[:, None]
    gain_two = ffn_gain.astype(F32)[:, None]
    kb = positions.reshape(32, 256)[:, 0]
    own_pos = lax.dynamic_slice_in_dim(positions, c * tokens, tokens, 0)
    cosine, sine = rotary_tables(own_pos, HD)
    spot = (jnp.arange(96)[:, None] == 4 * c + jnp.arange(4)[None, :]).astype(F32)
    head_gains = jnp.stack(
        [spot @ query_gain.astype(F32), spot @ key_gain.astype(F32)], axis=1
    ).astype(BF)

    def lifted(weight, gain):
        return (weight.astype(F32) * gain).astype(BF)

    def padded(weight, width):
        return jnp.pad(weight, ((0, 0), (0, width - weight.shape[1])))

    wq_s = jnp.concatenate(
        [
            lifted(query_weight, gain_one),
            lifted(key_weight, gain_one),
            lifted(value_weight, gain_one),
            padded(head_gains, 64),
            output_weight.T,
            jnp.zeros((96, 64), BF),
        ],
        axis=1,
    )
    wf_s = jnp.concatenate(
        [
            padded(lifted(gate_weight, gain_two), 896),
            padded(lifted(up_weight, gain_two), 896),
            padded(down_weight.T, 896),
        ],
        axis=1,
    )
    wq, wf, wo, kv, qt, raw, att, sums, normed = forward_part(
        kb, block_input, wq_s, wf_s, cosine, sine
    )
    x = block_input.astype(F32)
    mid = x + dot_tn(att, wo)
    inv_two = rms_inverse(mid)
    normed_two = mid * inv_two
    low_two = normed_two.astype(BF)
    gate_full, up_full, down_full = wf[:, 0:896], wf[:, 896:1792], wf[:, 1792:2688]
    gate = dot(low_two, gate_full)
    up = dot(low_two, up_full)
    sig = jax.nn.sigmoid(gate)
    act = (gate * sig * up).astype(BF)
    ffn_part = dot_nt(act, down_full).astype(BF)
    grad_act = dot(out_cotangent, down_full)
    grad_gate = (grad_act * up * sig * (1.0 + gate * (1.0 - sig))).astype(BF)
    grad_up = (grad_act * gate * sig).astype(BF)

    def blocks(grad):
        return grad.astype(BF).reshape(8, 2, 96, 896)

    down_grad = blocks(dot_tn(out_cotangent, act))
    gate_grad = blocks(dot_tn(low_two, grad_gate))
    up_grad = blocks(dot_tn(low_two, grad_up))
    back_two = dot_nt(grad_gate, gate_full) + dot_nt(grad_up, up_full)
    gain_two_part = jnp.sum(back_two * normed_two, axis=0, keepdims=True)
    pull = jnp.mean(back_two * normed_two, axis=-1, keepdims=True)
    share_mid = (
        out_cotangent.astype(F32) * 0.125 + inv_two * (back_two - normed_two * pull)
    ).astype(BF)
    grad_att = dot_nt(wo, share_mid).astype(BF)
    mid_rows = lax.dynamic_slice_in_dim(mid, t * 64, 64, 0)
    att_own = lax.dynamic_slice_in_dim(att, t * 192, 192, 0)
    two, gin, own_q, own_w, gains = backward_part(
        kb, grad_att, ffn_part, share_mid, mid_rows, gate_grad, up_grad, down_grad, gain_two_part,
        lax.dynamic_slice_in_dim(block_input, t * 64, 64, 0), normed, wq, raw, att_own, sums, qt, kv, cosine, sine,
    )
    return (
        two.reshape(8, 2, 64, 1536)[:, 0].reshape(tokens, 1536),
        gin.astype(F32),
        gains[:, 64] / gain_one[:, 0],
        own_q[:, 0:192] * gain_one,
        own_q[:, 192:256] * gain_one,
        own_q[:, 256:320] * gain_one,
        gains[0:4, 66],
        gains[0:4, 67],
        own_q[:, 384:576].T,
        gains[:, 65] / gain_two[:, 0],
        own_w[0, :, 0:864] * gain_two,
        own_w[1, :, 0:864] * gain_two,
        own_w[2, :, 0:864].T,
    )


def solution(mesh):
    in_specs = (
        P("ctx", None),
        P(),
        P("ctx"),
        P("ctx", "tp"),
        P("ctx", "tp"),
        P("ctx", "tp"),
        P("ctx"),
        P("ctx"),
        P("tp", "ctx"),
        P("ctx"),
        P("ctx", "tp"),
        P("ctx", "tp"),
        P("tp", "ctx"),
        P("ctx", None),
    )
    out_specs = (
        P("ctx", None),
        P("ctx", None),
        P("ctx"),
        P("ctx", "tp"),
        P("ctx", "tp"),
        P("ctx", "tp"),
        P("ctx"),
        P("ctx"),
        P("tp", "ctx"),
        P("ctx"),
        P("ctx", "tp"),
        P("ctx", "tp"),
        P("tp", "ctx"),
    )
    return jax.shard_map(body, mesh=mesh, in_specs=in_specs, out_specs=out_specs, check_vma=False)
```

```python
import functools
import math

import jax
import jax.numpy as jnp
from jax import lax
from jax.experimental import pallas as pl
from jax.experimental.pallas import tpu as pltpu
from jax.sharding import PartitionSpec as P

HD = 64
EPS = 1e-05
THETA = 1000000.0
LOG2E = math.log2(math.e)
LN2 = math.log(2.0)
BF = jnp.bfloat16
F32 = jnp.float32
MESH = pl.DeviceIdType.MESH
VM = pl.BlockSpec(memory_space=pltpu.VMEM)
SM = pl.BlockSpec(memory_space=pltpu.SMEM)
HB = pl.BlockSpec(memory_space=pl.ANY)
DMA = pltpu.SemaphoreType.DMA


class Place:
    def __init__(self):
        self.c = lax.axis_index("ctx")
        self.t = lax.axis_index("tp")
        self.core = lax.rem(self.c, 2)
        self.x = lax.rem(self.c // 2, 4)
        self.zh = self.c // 8
        self.y = lax.rem(self.t, 4)
        self.zl = self.t // 4

    def ctx(self, dz, dx, other=0):
        core = self.core if not other else 1 - self.core
        zh = self.zh if not dz else 1 - self.zh
        return (zh * 4 + lax.rem(self.x + dx, 4)) * 2 + core

    def tp(self, dz, dy):
        zl = self.zl if not dz else 1 - self.zl
        return zl * 4 + lax.rem(self.y + dy, 4)


def greet(peers):
    barrier = pltpu.get_barrier_semaphore()
    for peer in peers:
        pl.semaphore_signal(barrier, inc=1, device_id=peer, device_id_type=MESH)
    pl.semaphore_wait(barrier, len(peers))


class Gather:
    def __init__(self, buf, rows, block, pair, right, left, sibling, send, recv, own=None):
        self.buf, self.rows, self.block = buf, rows, block
        self.to = {"z": pair, "r": right, "l": left, "s": sibling}
        self.send, self.recv, self.own = send, recv, own
        self.plan = {
            0: ((0, 0), 0, "z"),
            1: ((0, 0), 0, "r"),
            2: ((0, 0), 0, "l"),
            3: ((0, 3), 1, "r"),
            4: ((0, 1), 2, "l"),
            5: ((1, 0), 0, "r"),
            6: ((1, 0), 0, "l"),
            7: ((1, 3), 1, "r"),
            8: ((1, 1), 2, "l"),
            9: ((0, 0), 0, "s"),
            10: ((1, 0), 0, "s"),
            11: ((0, 3), 0, "s"),
            12: ((0, 1), 0, "s"),
            13: ((0, 2), 0, "s"),
            14: ((1, 3), 0, "s"),
            15: ((1, 1), 0, "s"),
            16: ((1, 2), 0, "s"),
        }
        self.count = 17 if sibling is not None else 9

    def copy(self, k):
        where, part, to = self.plan[k]
        rows = self.rows if part == 0 else self.rows // 2
        start = pl.multiple_of(self.block(*where) * self.rows, self.rows)
        if part == 2:
            start = pl.multiple_of(start + rows, rows)
        there = self.buf.at[pl.ds(start, rows)]
        here = there
        if where == (0, 0) and self.own is not None:
            here = self.own
        return pltpu.make_async_remote_copy(
            src_ref=here,
            dst_ref=there,
            send_sem=self.send.at[k],
            recv_sem=self.recv.at[k],
            device_id=self.to[to],
            device_id_type=MESH,
        )

    def go(self, *which):
        for k in which:
            if k < self.count:
                self.copy(k).start()

    def got(self, *which):
        for k in which:
            if k < self.count:
                self.copy(k).wait_recv()

    def begin(self):
        self.go(0, 1, 2, 9)

    def near(self):
        self.got(1)
        self.go(3, 11)
        self.got(2)
        self.go(4, 12)

    def pair(self):
        self.got(0)
        self.go(5, 6, 10)

    def far(self):
        self.got(5)
        self.go(7, 14)
        self.got(6)
        self.go(8, 15)
        self.got(3, 4)
        self.go(13)

    def last(self):
        self.got(7, 8)
        self.go(16)

    def sent(self):
        for k in range(self.count):
            self.copy(k).wait_send()

    def end(self):
        self.got(*range(9, 17))
        self.sent()


def ctx_neighbours(me):
    return (
        (me.ctx(1, 0), me.t),
        (me.ctx(0, 1), me.t),
        (me.ctx(0, 3), me.t),
        (me.ctx(0, 0, 1), me.t),
    )


def tp_neighbours(me):
    return (me.c, me.tp(1, 0)), (me.c, me.tp(0, 1)), (me.c, me.tp(0, 3))


def rms_inverse(value):
    return lax.rsqrt(jnp.mean(value * value, axis=-1, keepdims=True) + EPS)


def column_inverse(value):
    return lax.rsqrt(jnp.mean(value * value, axis=0, keepdims=True) + EPS)


def gain_columns(wq):
    total = wq[0:64, 256:384].astype(F32)
    for k in range(1, 16):
        total += wq[96 * k : 96 * k + 64, 256:384].astype(F32)
    return total[:, 64:65], total[:, 65:66]


def dot(a, b):
    return jnp.dot(a, b, preferred_element_type=F32)


def dot_nt(a, b):
    return lax.dot_general(a, b, (((1,), (1,)), ((), ())), preferred_element_type=F32)


def dot_tn(a, b):
    return lax.dot_general(a, b, (((0,), (0,)), ((), ())), preferred_element_type=F32)


PAIRS = ((0, 0), (0, 3), (0, 1), (1, 0), (0, 2), (1, 3), (1, 1), (1, 2))


def chip_of(me, step, order):
    dz = sum(jnp.where(step == k, p[0], 0) for k, p in enumerate(order) if p[0])
    dx = sum(jnp.where(step == k, p[1], 0) for k, p in enumerate(order) if p[1])
    return lax.rem(me.zh + dz, 2) * 4 + lax.rem(me.x + dx, 4)


SLOTS = ((0, 2), (1, 2), (1, 1), (1, 3), (0, 1), (0, 3), (1, 0), (0, 0))


def add_into(out, *terms):
    total = terms[0][...].astype(F32)
    for term in terms[1:]:
        total += term[...].astype(F32)
    out[...] = total.astype(out.dtype)


class RingSum:
    def __init__(self, src, half, stage, rel_l, rel_r, col_l, col_r, from_z, pair, right, left, send, recv):
        self.src, self.half = src, half
        at_stage = {2: (0, 0), 3: (0, 1), 4: (1, 0), 5: (1, 1)}

        def put(k, part):
            if stage is None:
                return src(k, part)
            rows = pl.ds(part * half, half)
            return stage.at[2 if k == 6 else at_stage[k][0], rows]

        self.put = put
        self.rel_l, self.rel_r, self.col_l, self.col_r, self.from_z = rel_l, rel_r, col_l, col_r, from_z
        self.to = {"z": pair, "r": right, "l": left}
        self.send, self.recv = send, recv
        low, high = pl.ds(0, half), pl.ds(half, half)
        self.low, self.high = low, high
        self.plan = [
            (src(1, 0), rel_l.at[1], "r"),
            (src(1, 1), rel_r.at[1], "l"),
            (src(0, 0), rel_l.at[0], "r"),
            (src(0, 1), rel_r.at[0], "l"),
            (src(2, 1), col_l.at[1, high], "r"),
            (src(3, 0), col_r.at[1, low], "l"),
            (src(4, 1), col_l.at[0, high], "r"),
            (src(5, 0), col_r.at[0, low], "l"),
            (put(2, 0), col_l.at[1, low], "r"),
            (put(3, 1), col_r.at[1, high], "l"),
            (put(4, 0), col_l.at[0, low], "r"),
            (put(5, 1), col_r.at[0, high], "l"),
            (put(6, 0), from_z.at[low], "z"),
            (put(6, 1), from_z.at[high], "z"),
        ]

    def copy(self, k):
        here, there, to = self.plan[k]
        return pltpu.make_async_remote_copy(
            src_ref=here,
            dst_ref=there,
            send_sem=self.send.at[k],
            recv_sem=self.recv.at[k],
            device_id=self.to[to],
            device_id_type=MESH,
        )

    def go(self, *which):
        for k in which:
            self.copy(k).start()

    def got(self, *which):
        for k in which:
            self.copy(k).wait_recv()

    def begin(self):
        self.go(*range(8))

    def relay_right(self, plane):
        k = 2 if plane else 4
        self.got(0 if plane else 2)
        add_into(self.put(k, 0), self.src(k, 0), self.rel_l.at[plane])
        self.go(8 if plane else 10)

    def relay_left(self, plane):
        k = 3 if plane else 5
        self.got(1 if plane else 3)
        add_into(self.put(k, 1), self.src(k, 1), self.rel_r.at[plane])
        self.go(9 if plane else 11)

    def relay(self):
        for plane in (1, 0):
            self.relay_right(plane)
            self.relay_left(plane)

    def column(self):
        self.got(4, 8, 5, 9)
        for part, rows in enumerate((self.low, self.high)):
            add_into(
                self.put(6, part),
                self.src(6, part),
                self.col_l.at[1, rows],
                self.col_r.at[1, rows],
            )
            self.go(12 + part)

    def finish(self, part):
        if part == 0:
            self.got(6, 10, 7, 11, 12, 13)
        rows = self.low if part == 0 else self.high
        total = self.src(7, part)[...].astype(F32)
        for term in (self.col_l.at[0, rows], self.col_r.at[0, rows], self.from_z.at[rows]):
            total += term[...].astype(F32)
        return total

    def sent(self):
        for k in range(14):
            self.copy(k).wait_send()


def ring_scratch(half, width, stage=False):
    return [
        pltpu.VMEM((3, 2 * half, width) if stage else (1, 16, 128), BF),
        pltpu.VMEM((2, half, width), BF),
        pltpu.VMEM((2, half, width), BF),
        pltpu.VMEM((2, 2 * half, width), BF),
        pltpu.VMEM((2, 2 * half, width), BF),
        pltpu.VMEM((2 * half, width), BF),
        DMA((14,)),
        DMA((14,)),
    ]


def ring(src, half, scratch, neighbours, stage=False):
    room, rel_l, rel_r, col_l, col_r, from_z, send, recv = scratch
    return RingSum(
        src, half, room if stage else None, rel_l, rel_r, col_l, col_r, from_z, *neighbours[:3],
        send, recv,
    )


def forward_kernel(
    kb, x_ref, cot, wq_s, wo_s, wf_s, cos_ref, sin_ref,
    wq, kv, qt, raw, sums, normed, att_own, u_ref, share_ref, block, gain_two, low, act, grad_g, grad_u, p_all,
    wo_t, wf, wo, att, acc, pbuf, mid, inv, gate, up, ffn,
    s_w, r_w, s_v, r_v, s_f, r_f, s_o, r_o, s_k, r_k, s_a, r_a, s_l, s_p,
    *rest,
):
    me = Place()
    cn = ctx_neighbours(me)
    tn = tp_neighbours(me)
    tokens = x_ref.shape[0]
    greet([*cn, *tn])
    weights = Gather(wq, 96, me.ctx, *cn, s_w, r_w, own=wq_s)
    outs = Gather(wo_t, 96, me.ctx, *cn, s_v, r_v, own=wo_s)
    feed = [
        Gather(
            wf.at[p], 96, me.ctx, *cn, s_f.at[p], r_f.at[p], own=wf_s.at[:, 896 * p : 896 * p + 896]
        )
        for p in range(3)
    ]
    keys = Gather(kv, tokens, me.ctx, *cn, s_k, r_k)
    outw = Gather(
        wo, 96, lambda dz, dy: me.tp(dz, dy) * 2 + me.core, *tn, cn[3], s_o, r_o
    )
    share = [
        Gather(
            att, 64, lambda dz, dy, h=h: me.tp(dz, dy) * 3 + h, *tn, None, s_a.at[h], r_a.at[h]
        )
        for h in range(3)
    ]
    sum_f = ring(
        lambda k, part: ffn.at[
            pl.ds(pl.multiple_of(me.tp(*SLOTS[k]) * 64 + 32 * part, 32), 32)
        ],
        32, rest, tn,
    )

    weights.begin()
    outs.begin()
    mine = pl.ds(pl.multiple_of(me.c * 96, 96), 96)
    keep = [
        pltpu.make_async_copy(wq_s, wq.at[mine], s_l.at[0]),
        pltpu.make_async_copy(wo_s, wo_t.at[mine], s_l.at[1]),
    ] + [
        pltpu.make_async_copy(wf_s.at[:, 896 * p : 896 * p + 896], wf.at[p, mine], s_l.at[2 + p])
        for p in range(3)
    ]
    for k in keep:
        k.start()

    def norm_rows(i, carry):
        rows = pl.ds(pl.multiple_of(i * 64, 64), 64)
        value = x_ref[rows].astype(F32)
        normed[rows] = (value * rms_inverse(value)).astype(BF)
        return carry

    lax.fori_loop(0, tokens // 64, norm_rows, 0)
    weights.near()
    weights.pair()
    outs.near()
    outs.pair()
    weights.far()
    weights.last()
    outs.far()
    feed[0].begin()
    keep[0].wait()
    weights.end()

    def project(i, carry):
        cols = pl.ds(pl.multiple_of(i * 256, 256), 256)
        raw[:, cols] = dot(normed[cols], wq[...]).T
        return carry

    lax.fori_loop(0, tokens // 256, project, 0)
    query_gain, key_gain = gain_columns(wq)
    cosine, sine = cos_ref[...], sin_ref[...]

    def turned(value, gain):
        hat = value * column_inverse(value) * gain
        a, b = hat[:32], hat[32:]
        return jnp.concatenate([a * cosine - b * sine, b * cosine + a * sine], axis=0)

    both = jnp.concatenate([turned(raw[192:256], key_gain), raw[256:320]], axis=0)
    kv[pl.ds(pl.multiple_of(me.c * tokens, tokens), tokens)] = both.T.astype(BF)
    keys.begin()
    qt[64:128] = jnp.zeros((64, 3 * tokens), BF)
    for h in range(3):
        qt[0:64, h * tokens : (h + 1) * tokens] = (
            turned(raw[64 * h : 64 * h + 64], query_gain) * (LOG2E / 8.0)
        ).astype(BF)
    outs.last()
    keep[1].wait()
    outs.end()
    heads = wo_t[...].T
    wo[pl.ds(pl.multiple_of(me.t * 192 + me.core * 96, 96), 96)] = jnp.where(
        me.core == 0, heads[0:96], heads[96:192]
    )
    outw.begin()
    feed[1].begin()
    acc[...] = jnp.zeros_like(acc)
    ones = jnp.concatenate([jnp.ones((1, 1024), BF), jnp.zeros((15, 1024), BF)], axis=0)
    apart = lax.broadcasted_iota(jnp.int32, (256, 256), 0) - lax.broadcasted_iota(
        jnp.int32, (256, 256), 1
    )

    def attend(h, place, slot):
        rows = kv[pl.ds(pl.multiple_of(place * 1024, 1024), 1024), :]
        scores = dot(rows, qt[:, pl.ds(pl.multiple_of(h * tokens, tokens), tokens)])
        parts = []
        for a in range(4):
            line = []
            for b in range(2):
                sub = scores[a * 256 : a * 256 + 256, b * 256 : b * 256 + 256]
                seen = apart <= kb[me.c * 2 + b] - kb[place * 4 + a]
                line.append(jnp.where(seen, jnp.exp2(sub), 0.0).astype(BF))
            parts.append(jnp.concatenate(line, axis=1))
        weight = jnp.concatenate(parts, axis=0)
        pbuf[slot] = weight
        left = jnp.concatenate([rows.T[64:128], ones], axis=0)
        return dot(left, weight)

    def store(h, place, slot):
        return pltpu.make_async_copy(pbuf.at[slot], p_all.at[place, h], s_p.at[slot])

    def close(h):
        total = acc[h, 64:65]
        sums[0:1, h * tokens : (h + 1) * tokens] = total
        value = (acc[h, 0:64] / total).astype(BF)
        att_own[64 * h : 64 * h + 64] = value
        att[pl.ds(pl.multiple_of(me.t * 192 + 64 * h, 64), 64)] = value
        share[h].begin()

    def first_head(step, carry):
        @pl.when(step == 0)
        def _():
            keys.got(9)

        @pl.when(step == 1)
        def _():
            keys.near()
            keys.got(11)

        @pl.when(step == 2)
        def _():
            keys.pair()
            keys.got(12)

        @pl.when(step == 3)
        def _():
            keys.got(10)
            feed[0].near()

        @pl.when(step == 4)
        def _():
            keys.far()
            keys.got(13)
            outw.near()

        @pl.when(step == 5)
        def _():
            keys.got(14)
            feed[0].pair()
            outw.pair()

        @pl.when(step == 6)
        def _():
            keys.last()
            keys.got(15)
            feed[2].begin()

        @pl.when(step == 7)
        def _():
            keys.got(16)

        place = chip_of(me, step, PAIRS)
        slot = lax.rem(step, 4)

        @pl.when(step >= 4)
        def _():
            store(0, place, slot).wait()

        acc[0] += attend(0, place, slot)
        store(0, place, slot).start()
        return carry

    lax.fori_loop(0, 8, first_head, 0)
    close(0)

    def more_heads(i, carry):
        @pl.when(i == 0)
        def _():
            feed[1].near()
            outw.far()

        @pl.when(i == 1)
        def _():
            feed[0].far()
            feed[1].pair()

        @pl.when(i == 2)
        def _():
            share[0].near()
            share[0].pair()
            outw.last()

        @pl.when(i == 3)
        def _():
            feed[0].last()
            share[0].far()

        @pl.when(i == 4)
        def _():
            close(1)
            share[0].last()
            feed[2].near()

        @pl.when(i == 5)
        def _():
            feed[1].far()
            feed[2].pair()

        @pl.when(i == 6)
        def _():
            share[1].near()
            share[1].pair()

        @pl.when(i == 7)
        def _():
            feed[1].last()
            share[1].far()

        h = 1 + i // 4
        for half in range(2):
            place = chip_of(me, 2 * lax.rem(i, 4) + half, PAIRS)
            slot = 2 * lax.rem(i, 2) + half
            store(h, place, slot).wait()
            acc[h] += attend(h, place, slot)
            store(h, place, slot).start()
        return carry

    lax.fori_loop(0, 8, more_heads, 0)
    close(2)
    share[1].last()
    share[2].near()
    share[2].pair()
    feed[2].far()
    share[2].far()
    share[2].last()
    feed[2].last()
    outw.end()
    keep[2].wait()
    keep[3].wait()
    feed[0].end()
    feed[1].end()

    def forward_rows(i, carry):
        rows = pl.ds(pl.multiple_of(i * 256, 256), 256)
        value = x_ref[rows].astype(F32) + dot(att[:, rows].T, wo[...])
        inverse = rms_inverse(value)
        mid[rows] = value
        inv[rows] = jnp.broadcast_to(inverse, (256, 128))
        hidden = (value * inverse).astype(BF)
        low[rows] = hidden
        g = dot(hidden, wf[0])
        u = dot(hidden, wf[1])
        gate[rows] = g
        up[rows] = u
        a = (g * jax.nn.sigmoid(g) * u).astype(BF)
        act[rows] = a

        @pl.when(i == 0)
        def _():
            keep[4].wait()
            feed[2].end()

        ffn[rows] = dot_nt(a, wf[2]).astype(BF)
        return carry

    lax.fori_loop(0, 2, forward_rows, 0)
    sum_f.begin()
    gain_two[...] = jnp.zeros_like(gain_two)

    def backward_rows(i, carry):
        @pl.when(i == 1)
        def _():
            sum_f.relay()

        rows = pl.ds(pl.multiple_of(i * 256, 256), 256)
        ct = cot[rows]
        g, u = gate[rows], up[rows]
        sig = jax.nn.sigmoid(g)
        grad_act = dot(ct, wf[2])
        gg = (grad_act * u * sig * (1.0 + g * (1.0 - sig))).astype(BF)
        gu = (grad_act * g * sig).astype(BF)
        grad_g[rows] = gg
        grad_u[rows] = gu
        back = dot_nt(gg, wf[0]) + dot_nt(gu, wf[1])
        hat = low[rows].astype(F32)
        both = back * hat
        gain_two[...] += jnp.sum(both, axis=0, keepdims=True)
        pull = jnp.mean(both, axis=-1, keepdims=True)
        part = (ct.astype(F32) * 0.125 + inv[rows][:, 0:1] * (back - hat * pull)).astype(BF)
        share_ref[rows] = part
        u_ref[:, rows] = dot_nt(wo[...], part).astype(BF)
        return carry

    lax.fori_loop(0, 2, backward_rows, 0)
    sum_f.column()
    own = pl.multiple_of(me.t * 64, 64)
    block[0:32] = (mid[pl.ds(own, 32)] + sum_f.finish(0)).astype(BF)
    block[32:64] = (mid[pl.ds(pl.multiple_of(own + 32, 32), 32)] + sum_f.finish(1)).astype(BF)
    keys.sent()
    sum_f.sent()
    for s in share:
        s.sent()
    for slot in range(4):
        store(0, 0, slot).wait()


def forward_part(*operands):
    tokens = 512
    shapes = [
        jax.ShapeDtypeStruct((1536, 384), BF),
        jax.ShapeDtypeStruct((16 * tokens, 128), BF),
        jax.ShapeDtypeStruct((128, 3 * tokens), BF),
        jax.ShapeDtypeStruct((384, tokens), F32),
        jax.ShapeDtypeStruct((8, 3 * tokens), F32),
        jax.ShapeDtypeStruct((tokens, 1536), BF),
        jax.ShapeDtypeStruct((192, tokens), BF),
        jax.ShapeDtypeStruct((1536, tokens), BF),
        jax.ShapeDtypeStruct((tokens, 1536), BF),
        jax.ShapeDtypeStruct((64, 1536), BF),
        jax.ShapeDtypeStruct((1, 1536), F32),
        jax.ShapeDtypeStruct((tokens, 1536), BF),
        jax.ShapeDtypeStruct((tokens, 896), BF),
        jax.ShapeDtypeStruct((tokens, 896), BF),
        jax.ShapeDtypeStruct((tokens, 896), BF),
        jax.ShapeDtypeStruct((8, 3, 1024, tokens), BF),
    ]
    scratch = [
        pltpu.VMEM((1536, 256), BF),
        pltpu.VMEM((3, 1536, 896), BF),
        pltpu.VMEM((1536, 1536), BF),
        pltpu.VMEM((1536, tokens), BF),
        pltpu.VMEM((3, 80, tokens), F32),
        pltpu.VMEM((4, 1024, tokens), BF),
        pltpu.VMEM((tokens, 1536), F32),
        pltpu.VMEM((tokens, 128), F32),
        pltpu.VMEM((tokens, 896), F32),
        pltpu.VMEM((tokens, 896), F32),
        pltpu.VMEM((tokens, 1536), BF),
        *[DMA((17,))] * 4,
        *[DMA((3, 17))] * 2,
        *[DMA((17,))] * 4,
        *[DMA((3, 9))] * 2,
        DMA((5,)),
        DMA((4,)),
        *ring_scratch(32, 1536),
    ]
    return pl.pallas_call(
        forward_kernel,
        out_shape=shapes,
        in_specs=[SM] + [VM] * 7,
        out_specs=[VM] * 15 + [HB],
        scratch_shapes=scratch,
        name="forward_part",
        compiler_params=pltpu.CompilerParams(
            collective_id=0, has_side_effects=True, vmem_limit_bytes=59 << 20
        ),
    )(*operands)


def backward_kernel(
    kb, u_ref, share_ref, block, cot, low, act, grad_g, grad_u, gain_two,
    x_ref, normed, wq, raw, att_own, sums, qt, kv, cos_ref, sin_ref, p_all,
    two, gin, own_q, own_w, gains,
    mid_rows, own_two, branch, gt, drift, dq, gk, gk_sib, wg, sib_w, pw, sib_p, back, pre, extra,
    s_two, r_two, s_in, r_in, s_ex, r_ex, s_sib, r_sib, s_loc, s_p,
    *rest,
):
    me = Place()
    cn = ctx_neighbours(me)
    tn = tp_neighbours(me)
    sib = cn[3]
    tokens = normed.shape[0]
    scratch = [rest[8 * k : 8 * k + 8] for k in range(8)]
    greet([*cn, *tn])

    def tp_block(k):
        return me.tp(*SLOTS[k])

    def chip(k):
        dz, dx = SLOTS[k]
        return me.ctx(dz, dx) // 2

    def rows_of(ref, size):
        def src(k, part):
            start = pl.multiple_of(tp_block(k) * size, size) + part * (size // 2)
            return ref.at[pl.ds(pl.multiple_of(start, size // 2), size // 2)]

        return src

    sum_u = ring(rows_of(u_ref, 192), 96, scratch[0], tn, True)
    sum_two = ring(rows_of(share_ref, 64), 32, scratch[1], tn, True)
    sum_b = ring(rows_of(back, 64), 32, scratch[2], tn)
    sum_kv = ring(
        lambda k, part: gk.at[k, me.core, pl.ds(64 * part, 64)], 64, scratch[3], cn
    )
    sum_w = [
        ring(
            lambda k, part, p=p: wg.at[p, chip(k), me.core, pl.ds(48 * part, 48)],
            48,
            scratch[4 + p],
            cn,
        )
        for p in range(3)
    ]
    sum_q = ring(
        lambda k, part: pw.at[chip(k), me.core, pl.ds(48 * part, 48)], 48, scratch[7], cn
    )
    put_two = Gather(two, 128, me.tp, *tn, None, s_two, r_two, own=own_two)
    put_in = Gather(gin, 64, me.tp, *tn, None, s_in, r_in)
    put_ex = Gather(extra, 96, me.tp, *tn, None, s_ex, r_ex)

    def to_sibling(k, here, there):
        return pltpu.make_async_remote_copy(
            src_ref=here,
            dst_ref=there,
            send_sem=s_sib.at[k],
            recv_sem=r_sib.at[k],
            device_id=sib,
            device_id_type=MESH,
        )

    def key_swap(k):
        return to_sibling(k, gk.at[k, 1 - me.core], gk_sib.at[k])

    swap_w = [to_sibling(8 + p, wg.at[p, :, 1 - me.core], sib_w.at[p]) for p in range(3)]
    swap_p = to_sibling(11, pw.at[:, 1 - me.core], sib_p)

    sum_u.begin()

    def weight_grads(b_low, b_cot, b_act, b_g, b_u):
        loads = [
            pltpu.make_async_copy(h, v, s_loc.at[k])
            for k, (h, v) in enumerate(
                [(low, b_low), (grad_g, b_g), (grad_u, b_u), (cot, b_cot), (act, b_act)]
            )
        ]
        for k in loads:
            k.start()
        loads[0].wait()
        for p, (left, right) in enumerate([(b_low, b_g), (b_low, b_u), (b_cot, b_act)]):
            loads[1 + p].wait()
            if p == 2:
                loads[4].wait()

            def chunk(i, carry, p=p, left=left, right=right):
                at = pl.ds(pl.multiple_of(384 * i, 384), 384)
                whole = dot(left[:, at].T, right[...]).astype(BF)
                for q in range(4):
                    wg[p, 2 * i + q // 2, q % 2] = whole[96 * q : 96 * q + 96]
                return carry

            lax.fori_loop(0, 4, chunk, 0)
            swap_w[p].start()
            if p == 0:
                sum_u.relay()
            if p == 1:
                sum_u.column()

    pl.run_scoped(
        weight_grads,
        pltpu.VMEM((tokens, 1536), BF),
        pltpu.VMEM((tokens, 1536), BF),
        pltpu.VMEM((tokens, 896), BF),
        pltpu.VMEM((tokens, 896), BF),
        pltpu.VMEM((tokens, 896), BF),
    )

    def join_w(p):
        swap_w[p].wait_recv()

        def one(j, carry):
            add_into(wg.at[p, j, me.core], wg.at[p, j, me.core], sib_w.at[p, j])
            return carry

        lax.fori_loop(0, 8, one, 0)

    join_w(0)
    sum_w[0].begin()
    grad_att = jnp.concatenate([sum_u.finish(0), sum_u.finish(1)], axis=0)
    sum_two.begin()
    gt[0:64] = jnp.zeros((64, 3 * tokens), BF)
    for h in range(3):
        cols = slice(h * tokens, (h + 1) * tokens)
        grad = grad_att[64 * h : 64 * h + 64]
        inverse = 1.0 / sums[0:1, cols]
        gt[64:128, cols] = (grad * inverse).astype(BF)
        drift[0:1, cols] = (
            jnp.sum(grad * att_own[64 * h : 64 * h + 64].astype(F32), axis=0, keepdims=True)
            * inverse
        )
    dq[...] = jnp.zeros_like(dq)

    def join_keys(k):
        key_swap(k).wait_recv()
        add_into(gk.at[k, me.core], gk.at[k, me.core], gk_sib.at[k])

    def key_loop(pbuf):
        def load(step, slot):
            return pltpu.make_async_copy(
                p_all.at[chip_of(me, step, SLOTS)], pbuf.at[slot], s_p.at[slot]
            )

        load(0, 0).start()

        def key_step(step, carry):
            slot = lax.rem(step, 2)

            @pl.when(step < 7)
            def _():
                load(step + 1, 1 - slot).start()

            @pl.when(step == 0)
            def _():
                sum_w[0].relay()
                join_w(1)
                sum_w[1].begin()

            @pl.when(step == 1)
            def _():
                join_keys(0)
                sum_kv.go(2, 3)
                sum_w[0].column()

            @pl.when(step == 2)
            def _():
                join_keys(1)
                sum_kv.go(0, 1)
                sum_two.relay()
                sum_w[1].relay()
                join_w(2)
                sum_w[2].begin()

            @pl.when(step == 3)
            def _():
                join_keys(2)
                sum_kv.go(4)
                sum_kv.relay_right(1)
                sum_w[1].column()
                sum_two.column()

            @pl.when(step == 4)
            def _():
                join_keys(3)
                sum_kv.go(5)
                sum_kv.relay_left(1)
                sum_w[2].relay()
                branch_rows = jnp.concatenate([sum_two.finish(0), sum_two.finish(1)], axis=0)
                mid_rows[...] = branch_rows
                own_two[0:64] = block[...]
                own_two[64:128] = branch_rows.astype(BF)
                put_two.begin()
                keep_two.start()

            @pl.when(step == 5)
            def _():
                join_keys(4)
                sum_kv.go(6)
                sum_kv.relay_right(0)
                for half in range(2):
                    own_w[0, 48 * half : 48 * half + 48] = sum_w[0].finish(half)

            @pl.when(step == 6)
            def _():
                join_keys(5)
                sum_kv.go(7)
                sum_kv.relay_left(0)
                put_two.near()
                sum_w[2].column()

            @pl.when(step == 7)
            def _():
                join_keys(6)
                sum_kv.column()
                put_two.pair()
                for half in range(2):
                    own_w[1, 48 * half : 48 * half + 48] = sum_w[1].finish(half)

            place = chip_of(me, step, SLOTS)
            load(step, slot).wait()
            rows = kv[pl.ds(pl.multiple_of(place * 1024, 1024), 1024), :]
            key_t = rows.T[0:64]
            key_grad = value_grad = 0.0
            for h in range(3):
                cols = slice(h * tokens, (h + 1) * tokens)
                slopes = dot(rows, gt[:, cols])
                weight = pbuf[slot, h]
                grad = (weight.astype(F32) * (slopes - drift[0:1, cols])).astype(BF)
                dq[:, cols] += dot(key_t, grad)
                key_grad += dot_nt(qt[0:64, cols], grad)
                value_grad += dot_nt(gt[64:128, cols], weight)
            both = jnp.concatenate([key_grad * LN2, value_grad], axis=0).astype(BF)
            gk[step, 0] = both[:, 0:512]
            gk[step, 1] = both[:, 512:1024]
            key_swap(step).start()
            return carry

        lax.fori_loop(0, 8, key_step, 0)

    keep_two = pltpu.make_async_copy(
        own_two, two.at[pl.ds(pl.multiple_of(me.t * 128, 128), 128)], s_loc.at[5]
    )
    pl.run_scoped(key_loop, pltpu.VMEM((2, 3, 1024, tokens), BF))
    query_gain, key_gain = gain_columns(wq)
    cosine, sine = cos_ref[...], sin_ref[...]

    def unturn(grad, value, gain):
        inverse = column_inverse(value)
        hat = value * inverse
        a, b = grad[:32], grad[32:]
        plain = jnp.concatenate([a * cosine + b * sine, b * cosine - a * sine], axis=0)
        gain_grad = jnp.sum(plain * hat, axis=1, keepdims=True)
        pulled = plain * gain
        back_grad = inverse * (pulled - hat * jnp.mean(pulled * hat, axis=0, keepdims=True))
        return gain_grad, back_grad

    query_gain_grad = 0.0
    for h in range(3):
        part, grad = unturn(
            dq[:, h * tokens : (h + 1) * tokens] * 0.125, raw[64 * h : 64 * h + 64], query_gain
        )
        query_gain_grad += part
        pre[64 * h : 64 * h + 64] = grad
    put_two.far()
    join_keys(7)
    key_grad, value_grad = sum_kv.finish(0), sum_kv.finish(1)
    key_gain_grad, grad = unturn(key_grad, raw[192:256], key_gain)
    pre[192:256] = grad
    pre[256:320] = value_grad
    pre[320:384] = jnp.zeros((64, tokens), F32)
    pre_n = pre[...].T.astype(BF)
    gain_one = 0.0
    for i in range(2):
        rows = slice(256 * i, 256 * i + 256)
        part = dot_nt(pre_n[rows], wq[...])
        back[rows] = part.astype(BF)
        gain_one += jnp.sum(part * normed[rows].astype(F32), axis=0, keepdims=True)
    sum_b.begin()
    put_two.last()
    keep_two.wait()
    fetch = [
        pltpu.make_async_copy(
            two.at[pl.ds(128 * b + 64, 64)], branch.at[pl.ds(64 * b, 64)], s_loc.at[6 + b]
        )
        for b in range(8)
    ]
    for f in fetch:
        f.start()
    for half in range(2):
        own_w[2, 48 * half : 48 * half + 48] = sum_w[2].finish(half)
    lane = lax.broadcasted_iota(jnp.int32, (64, 1536), 1)
    unit = lax.broadcasted_iota(jnp.int32, (64, 1536), 0)
    spot = lane == (unit // 4) * 96 + lax.rem(unit, 4)

    def spread(column):
        return jnp.sum(jnp.where(spot, column, 0.0), axis=0, keepdims=True)

    lines = jnp.concatenate(
        [
            jnp.zeros((64, 1536), F32),
            gain_one,
            gain_two[...],
            spread(query_gain_grad),
            spread(key_gain_grad),
            jnp.zeros((60, 1536), F32),
        ],
        axis=0,
    )
    sides = lines.T
    sum_b.relay()
    att_n = jnp.concatenate([att_own[...].astype(F32), jnp.zeros((64, tokens), F32)], axis=0).T.astype(BF)
    for f in fetch:
        f.wait()
    for i in range(4):
        at = slice(384 * i, 384 * i + 384)
        part = dot(normed[:, at].T, pre_n)
        part = jnp.concatenate([part[:, 0:256], part[:, 256:384] + sides[at]], axis=1)
        whole = jnp.concatenate([part, dot(branch[:, at].T, att_n)], axis=1).astype(BF)
        for q in range(4):
            pw[2 * i + q // 2, q % 2] = whole[96 * q : 96 * q + 96]
    swap_p.start()
    sum_b.column()
    swap_p.wait_recv()

    def join_p(j, carry):
        add_into(pw.at[j, me.core], pw.at[j, me.core], sib_p.at[j])
        return carry

    lax.fori_loop(0, 8, join_p, 0)
    sum_q.begin()
    own = pl.multiple_of(me.t * 64, 64)
    value = x_ref[...].astype(F32)
    inverse = rms_inverse(value)
    hat = value * inverse
    back_one = jnp.concatenate([sum_b.finish(0), sum_b.finish(1)], axis=0)
    gin[pl.ds(own, 64)] = (
        mid_rows[...]
        + inverse * (back_one - hat * jnp.mean(back_one * hat, axis=-1, keepdims=True))
    ).astype(BF)
    put_in.begin()
    sum_q.relay()
    put_in.near()
    put_in.pair()
    sum_q.column()
    put_in.far()
    for half in range(2):
        own_q[48 * half : 48 * half + 48] = sum_q.finish(half)
    extra[pl.ds(pl.multiple_of(me.t * 96, 96), 96)] = own_q[:, 256:384]
    put_ex.begin()
    put_in.last()
    put_ex.near()
    put_ex.pair()
    put_ex.far()
    put_ex.last()
    total = extra[0:96]
    for b in range(1, 8):
        total += extra[96 * b : 96 * b + 96]
    gains[...] = total
    for s in [sum_u, sum_two, sum_b, sum_kv, sum_q, *sum_w, put_two, put_in, put_ex]:
        s.sent()
    for k in range(8):
        key_swap(k).wait_send()
    for s in [*swap_w, swap_p]:
        s.wait_send()


def backward_part(*operands):
    tokens = 512
    shapes = [
        jax.ShapeDtypeStruct((1024, 1536), BF),
        jax.ShapeDtypeStruct((512, 1536), BF),
        jax.ShapeDtypeStruct((96, 640), F32),
        jax.ShapeDtypeStruct((3, 96, 896), F32),
        jax.ShapeDtypeStruct((96, 128), F32),
    ]
    scratch = [
        pltpu.VMEM((64, 1536), F32),
        pltpu.VMEM((128, 1536), BF),
        pltpu.VMEM((tokens, 1536), BF),
        pltpu.VMEM((128, 3 * tokens), BF),
        pltpu.VMEM((8, 3 * tokens), F32),
        pltpu.VMEM((64, 3 * tokens), F32),
        pltpu.VMEM((8, 2, 128, 512), BF),
        pltpu.VMEM((8, 128, 512), BF),
        pltpu.VMEM((3, 8, 2, 96, 896), BF),
        pltpu.VMEM((3, 8, 96, 896), BF),
        pltpu.VMEM((8, 2, 96, 640), BF),
        pltpu.VMEM((8, 96, 640), BF),
        pltpu.VMEM((tokens, 1536), BF),
        pltpu.VMEM((384, tokens), F32),
        pltpu.VMEM((768, 128), F32),
        *[DMA((9,))] * 6,
        DMA((12,)),
        DMA((12,)),
        DMA((14,)),
        DMA((2,)),
        *ring_scratch(96, 512, True),
        *ring_scratch(32, 1536, True),
        *ring_scratch(32, 1536),
        *ring_scratch(64, 512),
        *ring_scratch(48, 896) * 3,
        *ring_scratch(48, 640),
    ]
    return pl.pallas_call(
        backward_kernel,
        out_shape=shapes,
        in_specs=[SM, VM, VM, VM, HB, HB, HB, HB, HB] + [VM] * 11 + [HB],
        out_specs=[HB] + [VM] * 4,
        scratch_shapes=scratch,
        name="backward_part",
        compiler_params=pltpu.CompilerParams(
            collective_id=1, has_side_effects=True, vmem_limit_bytes=59 << 20
        ),
    )(*operands)


def rotary_tables(places, width):
    half_width = width // 2
    freq_table = THETA ** (-(jnp.arange(half_width, dtype=F32) * 2.0 / width))
    angles = freq_table[:, None] * places.astype(F32)[None, :]
    return jnp.cos(angles), jnp.sin(angles)


def body(
    block_input, positions, attn_gain, query_weight, key_weight, value_weight, query_gain,
    key_gain, output_weight, ffn_gain, gate_weight, up_weight, down_weight, out_cotangent,
):
    tokens = block_input.shape[0]
    c, t = lax.axis_index("ctx"), lax.axis_index("tp")
    gain_one = attn_gain.astype(F32)[:, None]
    gain_two = ffn_gain.astype(F32)[:, None]
    kb = positions.reshape(32, 256)[:, 0]
    own_pos = lax.dynamic_slice_in_dim(positions, c * tokens, tokens, 0)
    cosine, sine = rotary_tables(own_pos, HD)
    spot = (jnp.arange(96)[:, None] == 4 * c + jnp.arange(4)[None, :]).astype(F32)
    head_gains = jnp.stack(
        [spot @ query_gain.astype(F32), spot @ key_gain.astype(F32)], axis=1
    ).astype(BF)

    def lifted(weight, gain):
        return (weight.astype(F32) * gain).astype(BF)

    def padded(weight, width):
        return jnp.pad(weight, ((0, 0), (0, width - weight.shape[1])))

    wq_s = jnp.concatenate(
        [
            lifted(query_weight, gain_one),
            lifted(key_weight, gain_one),
            lifted(value_weight, gain_one),
            padded(head_gains, 64),
        ],
        axis=1,
    )
    wo_s = padded(output_weight.T, 256)
    wf_s = jnp.concatenate(
        [
            padded(lifted(gate_weight, gain_two), 896),
            padded(lifted(up_weight, gain_two), 896),
            padded(down_weight.T, 896),
        ],
        axis=1,
    )
    (
        wq, kv, qt, raw, sums, normed, att_own, u, share, block, gain_two_part, low, act, grad_g,
        grad_u, p_all,
    ) = forward_part(kb, block_input, out_cotangent, wq_s, wo_s, wf_s, cosine, sine)
    two, gin, own_q, own_w, gains = backward_part(
        kb, u, share, block, out_cotangent, low, act, grad_g, grad_u, gain_two_part,
        lax.dynamic_slice_in_dim(block_input, t * 64, 64, 0),
        normed, wq, raw, att_own, sums, qt, kv, cosine, sine, p_all,
    )
    return (
        two.reshape(8, 2, 64, 1536)[:, 0].reshape(tokens, 1536),
        gin.astype(F32),
        gains[:, 64] / gain_one[:, 0],
        own_q[:, 0:192] * gain_one,
        own_q[:, 192:256] * gain_one,
        own_q[:, 256:320] * gain_one,
        gains[0:4, 66],
        gains[0:4, 67],
        own_q[:, 384:576].T,
        gains[:, 65] / gain_two[:, 0],
        own_w[0, :, 0:864] * gain_two,
        own_w[1, :, 0:864] * gain_two,
        own_w[2, :, 0:864].T,
    )


def solution(mesh):
    in_specs = (
        P("ctx", None),
        P(),
        P("ctx"),
        P("ctx", "tp"),
        P("ctx", "tp"),
        P("ctx", "tp"),
        P("ctx"),
        P("ctx"),
        P("tp", "ctx"),
        P("ctx"),
        P("ctx", "tp"),
        P("ctx", "tp"),
        P("tp", "ctx"),
        P("ctx", None),
    )
    out_specs = (
        P("ctx", None),
        P("ctx", None),
        P("ctx"),
        P("ctx", "tp"),
        P("ctx", "tp"),
        P("ctx", "tp"),
        P("ctx"),
        P("ctx"),
        P("tp", "ctx"),
        P("ctx"),
        P("ctx", "tp"),
        P("ctx", "tp"),
        P("tp", "ctx"),
    )
    return jax.shard_map(body, mesh=mesh, in_specs=in_specs, out_specs=out_specs, check_vma=False)
```

```python
import functools
import math

import jax
import jax.numpy as jnp
from jax import lax
from jax.experimental import pallas as pl
from jax.experimental.pallas import tpu as pltpu
from jax.sharding import PartitionSpec as P

HD = 64
EPS = 1e-05
THETA = 1000000.0
LOG2E = math.log2(math.e)
LN2 = math.log(2.0)
BF = jnp.bfloat16
F32 = jnp.float32
MESH = pl.DeviceIdType.MESH
VM = pl.BlockSpec(memory_space=pltpu.VMEM)
SM = pl.BlockSpec(memory_space=pltpu.SMEM)
HB = pl.BlockSpec(memory_space=pl.ANY)
DMA = pltpu.SemaphoreType.DMA


class Place:
    def __init__(self):
        self.c = lax.axis_index("ctx")
        self.t = lax.axis_index("tp")
        self.core = lax.rem(self.c, 2)
        self.x = lax.rem(self.c // 2, 4)
        self.zh = self.c // 8
        self.y = lax.rem(self.t, 4)
        self.zl = self.t // 4

    def ctx(self, dz, dx, other=0):
        core = self.core if not other else 1 - self.core
        zh = self.zh if not dz else 1 - self.zh
        return (zh * 4 + lax.rem(self.x + dx, 4)) * 2 + core

    def tp(self, dz, dy):
        zl = self.zl if not dz else 1 - self.zl
        return zl * 4 + lax.rem(self.y + dy, 4)


def greet(peers):
    barrier = pltpu.get_barrier_semaphore()
    for peer in peers:
        pl.semaphore_signal(barrier, inc=1, device_id=peer, device_id_type=MESH)
    pl.semaphore_wait(barrier, len(peers))


class Gather:
    def __init__(self, buf, rows, block, pair, right, left, sibling, send, recv, own=None, cross=(), over=False):
        self.buf, self.rows, self.block = buf, rows, block
        self.to = {"z": pair, "r": right, "l": left, "s": sibling}
        self.cross = len(cross) > 0
        if self.cross:
            self.to["zr"], self.to["zl"] = cross
        self.send, self.recv, self.own = send, recv, own
        self.plan = {
            0: ((0, 0), 0, "z"),
            1: ((0, 0), 0, "r"),
            2: ((0, 0), 0, "l"),
            3: ((0, 3), 1, "r"),
            4: ((0, 1), 2, "l"),
            5: ((1, 0), 0, "r"),
            6: ((1, 0), 0, "l"),
            7: ((1, 3), 1, "r"),
            8: ((1, 1), 2, "l"),
            9: ((0, 0), 0, "s"),
            10: ((1, 0), 0, "s"),
            11: ((0, 3), 0, "s"),
            12: ((0, 1), 0, "s"),
            13: ((0, 2), 0, "s"),
            14: ((1, 3), 0, "s"),
            15: ((1, 1), 0, "s"),
            16: ((1, 2), 0, "s"),
        }
        if self.cross:
            self.plan[5] = ((0, 0), 0, "zr")
            self.plan[6] = ((0, 0), 0, "zl")
        self.over = over
        if over:
            self.plan[5] = ((0, 3), 0, "z")
            self.plan[6] = ((0, 1), 0, "z")
            self.plan[7] = ((0, 2), 1, "z")
            self.plan[8] = ((0, 2), 2, "z")
        self.count = 17 if sibling is not None else 9

    def copy(self, k):
        where, part, to = self.plan[k]
        rows = self.rows if part == 0 else self.rows // 2
        start = pl.multiple_of(self.block(*where) * self.rows, self.rows)
        if part == 2:
            start = pl.multiple_of(start + rows, rows)
        there = self.buf.at[pl.ds(start, rows)]
        here = there
        if where == (0, 0) and self.own is not None:
            here = self.own
        return pltpu.make_async_remote_copy(
            src_ref=here,
            dst_ref=there,
            send_sem=self.send.at[k],
            recv_sem=self.recv.at[k],
            device_id=self.to[to],
            device_id_type=MESH,
        )

    def go(self, *which):
        for k in which:
            if k < self.count:
                self.copy(k).start()

    def got(self, *which):
        for k in which:
            if k < self.count:
                self.copy(k).wait_recv()

    def begin(self):
        self.go(0, 1, 2, 9)
        if self.cross:
            self.go(5, 6)

    def near(self):
        self.got(1)
        self.go(3, 11)
        if self.over:
            self.go(5)
        self.got(2)
        self.go(4, 12)
        if self.over:
            self.go(6)

    def pair(self):
        self.got(0)
        if not self.cross and not self.over:
            self.go(5, 6)
        self.go(10)

    def far(self):
        if self.over:
            self.got(3)
            self.go(7)
            self.got(4)
            self.go(8)
            self.got(5, 6)
            return
        self.got(5)
        self.go(7, 14)
        self.got(6)
        self.go(8, 15)
        self.got(3, 4)
        self.go(13)

    def last(self):
        self.got(7, 8)
        self.go(16)

    def sent(self):
        for k in range(self.count):
            self.copy(k).wait_send()

    def end(self):
        self.got(*range(9, 17))
        self.sent()


def ctx_neighbours(me):
    return (
        (me.ctx(1, 0), me.t),
        (me.ctx(0, 1), me.t),
        (me.ctx(0, 3), me.t),
        (me.ctx(0, 0, 1), me.t),
    )


def tp_neighbours(me):
    return (me.c, me.tp(1, 0)), (me.c, me.tp(0, 1)), (me.c, me.tp(0, 3))


def tp_cross(me):
    return (me.c, me.tp(1, 1)), (me.c, me.tp(1, 3))


def rms_inverse(value):
    return lax.rsqrt(jnp.mean(value * value, axis=-1, keepdims=True) + EPS)


def column_inverse(value):
    return lax.rsqrt(jnp.mean(value * value, axis=0, keepdims=True) + EPS)


def gain_columns(wq):
    total = wq[0:64, 256:384].astype(F32)
    for k in range(1, 16):
        total += wq[96 * k : 96 * k + 64, 256:384].astype(F32)
    return total[:, 64:65], total[:, 65:66]


def dot(a, b):
    return jnp.dot(a, b, preferred_element_type=F32)


def dot_nt(a, b):
    return lax.dot_general(a, b, (((1,), (1,)), ((), ())), preferred_element_type=F32)


def dot_tn(a, b):
    return lax.dot_general(a, b, (((0,), (0,)), ((), ())), preferred_element_type=F32)


PAIRS = ((0, 0), (0, 3), (0, 1), (1, 0), (0, 2), (1, 3), (1, 1), (1, 2))


def chip_of(me, step, order):
    dz = sum(jnp.where(step == k, p[0], 0) for k, p in enumerate(order) if p[0])
    dx = sum(jnp.where(step == k, p[1], 0) for k, p in enumerate(order) if p[1])
    return lax.rem(me.zh + dz, 2) * 4 + lax.rem(me.x + dx, 4)


SLOTS = ((1, 2), (0, 2), (1, 1), (1, 3), (0, 1), (0, 3), (1, 0), (0, 0))


def add_into(out, *terms):
    total = terms[0][...].astype(F32)
    for term in terms[1:]:
        total += term[...].astype(F32)
    out[...] = total.astype(out.dtype)


class RingSum:
    def __init__(self, src, half, stage, rel_l, rel_r, col_l, col_r, from_z, pair, right, left, send, recv, cross=()):
        self.src, self.half = src, half
        at_stage = {2: (0, 0), 3: (0, 1), 4: (1, 0), 5: (1, 1)}

        def put(k, part):
            if stage is None:
                return src(k, part)
            rows = pl.ds(part * half, half)
            return stage.at[2 if k == 6 else at_stage[k][0], rows]

        self.put = put
        self.rel_l, self.rel_r, self.col_l, self.col_r, self.from_z = rel_l, rel_r, col_l, col_r, from_z
        self.to = {"z": pair, "r": right, "l": left, "zr": right, "zl": left}
        self.cross = len(cross) > 0
        if self.cross:
            self.to["zr"], self.to["zl"] = cross
        self.send, self.recv = send, recv
        low, high = pl.ds(0, half), pl.ds(half, half)
        self.low, self.high = low, high
        self.last = 14
        self.plan = [
            (src(0, 0), rel_l.at[1], "r"),
            (src(0, 1), rel_r.at[1], "l"),
            (src(1, 0), rel_l.at[0], "r"),
            (src(1, 1), rel_r.at[0], "l"),
            (src(2, 1), col_l.at[1, high], "zr"),
            (src(3, 0), col_r.at[1, low], "zl"),
            (src(4, 1), col_l.at[0, high], "r"),
            (src(5, 0), col_r.at[0, low], "l"),
            (put(2, 0), col_l.at[1, low], "zr"),
            (put(3, 1), col_r.at[1, high], "zl"),
            (put(4, 0), col_l.at[0, low], "r"),
            (put(5, 1), col_r.at[0, high], "l"),
            ((src if self.cross else put)(6, 0), from_z.at[low], "z"),
            ((src if self.cross else put)(6, 1), from_z.at[high], "z"),
        ]

    def copy(self, k):
        here, there, to = self.plan[k]
        return pltpu.make_async_remote_copy(
            src_ref=here,
            dst_ref=there,
            send_sem=self.send.at[k],
            recv_sem=self.recv.at[k],
            device_id=self.to[to],
            device_id_type=MESH,
        )

    def go(self, *which):
        for k in which:
            self.copy(k).start()

    def got(self, *which):
        for k in which:
            self.copy(k).wait_recv()

    def begin(self):
        self.go(*range(8))
        if self.cross:
            self.go(12, 13)

    def relay_right(self, plane):
        k = 2 if plane else 4
        self.got(0 if plane else 2)
        add_into(self.put(k, 0), self.src(k, 0), self.rel_l.at[plane])
        self.go(8 if plane else 10)

    def relay_left(self, plane):
        k = 3 if plane else 5
        self.got(1 if plane else 3)
        add_into(self.put(k, 1), self.src(k, 1), self.rel_r.at[plane])
        self.go(9 if plane else 11)

    def relay(self):
        for plane in (1, 0):
            self.relay_right(plane)
            self.relay_left(plane)

    def column(self):
        self.got(4, 8, 5, 9)
        for part, rows in enumerate((self.low, self.high)):
            add_into(
                self.put(6, part),
                self.src(6, part),
                self.col_l.at[1, rows],
                self.col_r.at[1, rows],
            )
            self.go(12 + part)

    def columns(self, out):
        self.last = 12
        self.got(4, 8, 5, 9, 6, 10, 7, 11)
        for plane, k in ((0, 7), (1, 6)):
            for part, rows in enumerate((self.low, self.high)):
                add_into(
                    out.at[plane, rows],
                    self.src(k, part),
                    self.col_l.at[plane, rows],
                    self.col_r.at[plane, rows],
                )

    def finish(self, part):
        if part == 0:
            self.got(6, 10, 7, 11, 12, 13)
            if self.cross:
                self.got(4, 8, 5, 9)
        rows = self.low if part == 0 else self.high
        total = self.src(7, part)[...].astype(F32)
        terms = [self.col_l.at[0, rows], self.col_r.at[0, rows], self.from_z.at[rows]]
        if self.cross:
            terms += [self.col_l.at[1, rows], self.col_r.at[1, rows]]
        for term in terms:
            total += term[...].astype(F32)
        return total

    def sent(self):
        for k in range(self.last):
            self.copy(k).wait_send()


def ring_scratch(half, width, stage=False):
    return [
        pltpu.VMEM((3, 2 * half, width) if stage else (1, 16, 128), BF),
        pltpu.VMEM((2, half, width), BF),
        pltpu.VMEM((2, half, width), BF),
        pltpu.VMEM((2, 2 * half, width), BF),
        pltpu.VMEM((2, 2 * half, width), BF),
        pltpu.VMEM((2 * half, width), BF),
        DMA((14,)),
        DMA((14,)),
    ]


def ring(src, half, scratch, neighbours, stage=False, cross=()):
    room, rel_l, rel_r, col_l, col_r, from_z, send, recv = scratch
    return RingSum(
        src, half, room if stage else None, rel_l, rel_r, col_l, col_r, from_z, *neighbours[:3],
        send, recv, cross,
    )


def gain_lines(lines, refs):
    lines[...] = jnp.zeros_like(lines)
    for k, ref in enumerate(refs):
        lines[k : k + 1, 0 : ref.shape[1]] = ref[...].astype(F32)
    columns = lines[...].T
    return columns[0:96, 0:1], columns[0:96, 1:2]


def prepare_kernel(
    places, attn_gain, ffn_gain, query_gain, key_gain, freq,
    query, key_t, value_t, output, gate, up, down_t, wq_s, wo_s, wf_s, cosine, sine, lines,
):
    c = lax.axis_index("ctx")
    gain_one, gain_two = gain_lines(lines, [attn_gain, ffn_gain, query_gain, key_gain])
    row = lax.broadcasted_iota(jnp.int32, (96, 64), 0)
    col = lax.broadcasted_iota(jnp.int32, (96, 64), 1)
    sides = jnp.zeros((96, 64), F32)
    for k in range(2):
        for j in range(4):
            at = (row == 4 * c + j) & (col == k)
            sides = jnp.where(at, lines[2 + k : 3 + k, j : j + 1], sides)

    def lifted(weight, gain):
        return (weight.astype(F32) * gain).astype(BF)

    both = jnp.concatenate([key_t[...].astype(F32), value_t[...].astype(F32)], axis=0).T
    wq_s[:, 0:192] = lifted(query[...], gain_one)
    wq_s[:, 192:320] = lifted(both, gain_one)
    wq_s[:, 320:384] = sides.astype(BF)
    wo_s[:, 192:256] = jnp.zeros((96, 64), BF)
    wo_s[:, 0:192] = output[...].astype(F32).T.astype(BF)
    for k in range(3):
        wf_s[:, 896 * k + 768 : 896 * k + 896] = jnp.zeros((96, 128), BF)
    wf_s[:, 0:864] = lifted(gate[...], gain_two)
    wf_s[:, 896:1760] = lifted(up[...], gain_two)
    wf_s[:, 1792:2656] = down_t[...]
    place = places[0:1, pl.ds(pl.multiple_of(c * 512, 512), 512)]
    angle = freq[:, 0:1] * place.astype(F32)
    cosine[...] = jnp.cos(angle)
    sine[...] = jnp.sin(angle)


def prepare(*operands):
    shapes = [
        jax.ShapeDtypeStruct((96, 384), BF),
        jax.ShapeDtypeStruct((96, 256), BF),
        jax.ShapeDtypeStruct((96, 2688), BF),
        jax.ShapeDtypeStruct((32, 512), F32),
        jax.ShapeDtypeStruct((32, 512), F32),
    ]
    return pl.pallas_call(
        prepare_kernel,
        out_shape=shapes,
        in_specs=[VM] * 13,
        out_specs=[VM] * 5,
        scratch_shapes=[pltpu.VMEM((8, 128), F32)],
        name="prepare",
        compiler_params=pltpu.CompilerParams(vmem_limit_bytes=59 << 20),
    )(*operands)


def conclude_kernel(
    attn_gain, ffn_gain, block, gin, own_q, own_w, side,
    block_output, grad_input, g_attn, g_query, g_key, g_value, g_qg, g_kg, g_out, g_ffn, g_gate, g_up, g_down,
    lines,
):
    gain_one, gain_two = gain_lines(lines, [attn_gain, ffn_gain])
    block_output[...] = block[...]
    grad_input[...] = gin[...].astype(F32)
    g_query[...] = own_q[:, 0:192] * gain_one
    both = (own_q[:, 192:320] * gain_one).T
    g_key[...] = both[0:64]
    g_value[...] = both[64:128]
    g_out[...] = own_q[:, 384:576].T
    g_gate[...] = own_w[0, :, 0:864] * gain_two
    g_up[...] = own_w[1, :, 0:864] * gain_two
    g_down[...] = own_w[2, :, 0:864]
    g_attn[...] = side[0:1, 0:96] / lines[0:1, 0:96]
    g_ffn[...] = side[1:2, 0:96] / lines[1:2, 0:96]
    g_qg[...] = side[2:3, 0:4]
    g_kg[...] = side[3:4, 0:4]


def conclude(*operands):
    dims = [
        ((512, 1536), BF), ((512, 1536), F32), ((1, 96), F32), ((96, 192), F32), ((64, 96), F32),
        ((64, 96), F32), ((1, 4), F32), ((1, 4), F32), ((192, 96), F32), ((1, 96), F32),
        ((96, 864), F32), ((96, 864), F32), ((96, 864), F32),
    ]
    results = pl.pallas_call(
        conclude_kernel,
        out_shape=[jax.ShapeDtypeStruct(*d) for d in dims],
        in_specs=[VM] * 7,
        out_specs=[VM] * 13,
        scratch_shapes=[pltpu.VMEM((8, 128), F32)],
        name="conclude",
        compiler_params=pltpu.CompilerParams(vmem_limit_bytes=59 << 20),
    )(*operands)
    results = [r.T if k in (4, 5, 12) else r for k, r in enumerate(results)]
    return tuple(r.reshape(-1) if r.shape[0] == 1 else r for r in results)


def forward_kernel(
    kb, x_ref, cot, wq_s, wo_s, wf_s, cos_ref, sin_ref,
    wq_out, kv_out, qt_out, raw_out, normed_out, low_out, act_out, g_out, u_out, share_out,
    sums, att_own, u_ref, mid_own, col_sum, gain_two, p_all,
    wq, kv, qt, raw, normed, low, act, grad_g, grad_u, share_ref,
    wo_t, wf, wo, att, acc, pbuf, mid, inv, gate, up, ffn,
    s_w, r_w, s_v, r_v, s_f, r_f, s_o, r_o, s_k, r_k, s_a, r_a, s_l, s_p, s_out,
    *rest,
):
    me = Place()
    cn = ctx_neighbours(me)
    tn = tp_neighbours(me)
    tokens = x_ref.shape[0]
    greet([*cn, *tn])
    weights = Gather(wq, 96, me.ctx, *cn, s_w, r_w, own=wq_s)
    outs = Gather(wo_t, 96, me.ctx, *cn, s_v, r_v, own=wo_s)
    feed = [
        Gather(
            wf.at[p], 96, me.ctx, *cn, s_f.at[p], r_f.at[p], own=wf_s.at[:, 896 * p : 896 * p + 896]
        )
        for p in range(3)
    ]
    keys = Gather(kv, tokens, me.ctx, *cn, s_k, r_k)
    outw = Gather(
        wo, 96, lambda dz, dy: me.tp(dz, dy) * 2 + me.core, *tn, cn[3], s_o, r_o
    )
    share = [
        Gather(
            att, 64, lambda dz, dy, h=h: me.tp(dz, dy) * 3 + h, *tn, None, s_a.at[h], r_a.at[h]
        )
        for h in range(3)
    ]
    sum_f = ring(
        lambda k, part: ffn.at[
            pl.ds(pl.multiple_of(me.tp(*SLOTS[k]) * 64 + 32 * part, 32), 32)
        ],
        32, rest, tn,
    )

    weights.begin()
    outs.begin()
    mine = pl.ds(pl.multiple_of(me.c * 96, 96), 96)
    keep = [
        pltpu.make_async_copy(wq_s, wq.at[mine], s_l.at[0]),
        pltpu.make_async_copy(wo_s, wo_t.at[mine], s_l.at[1]),
    ] + [
        pltpu.make_async_copy(wf_s.at[:, 896 * p : 896 * p + 896], wf.at[p, mine], s_l.at[2 + p])
        for p in range(3)
    ]
    for k in keep:
        k.start()
    emits = [
        pltpu.make_async_copy(v, h, s_out.at[k])
        for k, (v, h) in enumerate(
            [
                (wq, wq_out),
                (kv, kv_out),
                (qt, qt_out),
                (raw, raw_out),
                (normed, normed_out),
                (low, low_out),
                (act, act_out),
                (grad_g, g_out),
                (grad_u, u_out),
                (share_ref, share_out),
            ]
        )
    ]

    def norm_rows(i, carry):
        rows = pl.ds(pl.multiple_of(i * 64, 64), 64)
        value = x_ref[rows].astype(F32)
        normed[rows] = (value * rms_inverse(value)).astype(BF)
        return carry

    lax.fori_loop(0, tokens // 64, norm_rows, 0)
    weights.near()
    weights.pair()
    outs.near()
    outs.pair()
    emits[4].start()
    weights.far()
    weights.last()
    outs.far()
    outs.last()
    keep[1].wait()
    outs.end()
    heads = wo_t[...].T
    wo[pl.ds(pl.multiple_of(me.t * 192 + me.core * 96, 96), 96)] = jnp.where(
        me.core == 0, heads[0:96], heads[96:192]
    )
    outw.begin()
    keep[0].wait()
    weights.end()
    feed[0].begin()
    emits[0].start()

    def project(i, carry):
        cols = pl.ds(pl.multiple_of(i * 256, 256), 256)
        raw[:, cols] = dot(normed[cols], wq[...]).T
        return carry

    lax.fori_loop(0, tokens // 256, project, 0)
    emits[3].start()
    query_gain, key_gain = gain_columns(wq)
    cosine, sine = cos_ref[...], sin_ref[...]

    def turned(value, gain):
        hat = value * column_inverse(value) * gain
        a, b = hat[:32], hat[32:]
        return jnp.concatenate([a * cosine - b * sine, b * cosine + a * sine], axis=0)

    both = jnp.concatenate([turned(raw[192:256], key_gain), raw[256:320]], axis=0)
    kv[pl.ds(pl.multiple_of(me.c * tokens, tokens), tokens)] = both.T.astype(BF)
    keys.begin()
    qt[64:128] = jnp.zeros((64, 3 * tokens), BF)
    for h in range(3):
        qt[0:64, h * tokens : (h + 1) * tokens] = (
            turned(raw[64 * h : 64 * h + 64], query_gain) * (LOG2E / 8.0)
        ).astype(BF)
    emits[2].start()
    outw.near()
    feed[1].begin()
    acc[...] = jnp.zeros_like(acc)
    ones = jnp.concatenate([jnp.ones((1, 1024), BF), jnp.zeros((15, 1024), BF)], axis=0)
    apart = lax.broadcasted_iota(jnp.int32, (256, 256), 0) - lax.broadcasted_iota(
        jnp.int32, (256, 256), 1
    )

    def attend(h, place, slot):
        rows = kv[pl.ds(pl.multiple_of(place * 1024, 1024), 1024), :]
        scores = dot(rows, qt[:, pl.ds(pl.multiple_of(h * tokens, tokens), tokens)])
        parts = []
        for a in range(4):
            line = []
            for b in range(2):
                sub = scores[a * 256 : a * 256 + 256, b * 256 : b * 256 + 256]
                seen = apart <= kb[me.c * 512 + b * 256] - kb[place * 1024 + a * 256]
                line.append(jnp.where(seen, jnp.exp2(sub), 0.0).astype(BF))
            parts.append(jnp.concatenate(line, axis=1))
        weight = jnp.concatenate(parts, axis=0)
        pbuf[slot] = weight
        left = jnp.concatenate([rows.T[64:128], ones], axis=0)
        return dot(left, weight)

    def store(h, place, slot):
        return pltpu.make_async_copy(pbuf.at[slot], p_all.at[place, h], s_p.at[slot])

    def close(h):
        total = acc[h, 64:65]
        sums[0:1, h * tokens : (h + 1) * tokens] = total
        value = (acc[h, 0:64] / total).astype(BF)
        att_own[64 * h : 64 * h + 64] = value
        att[pl.ds(pl.multiple_of(me.t * 192 + 64 * h, 64), 64)] = value
        share[h].begin()

    def first_head(step, carry):
        @pl.when(step == 0)
        def _():
            keys.got(9)

        @pl.when(step == 1)
        def _():
            keys.near()
            outw.pair()
            keys.got(11)

        @pl.when(step == 2)
        def _():
            keys.pair()
            keys.got(12)

        @pl.when(step == 3)
        def _():
            keys.got(10)
            feed[0].near()

        @pl.when(step == 4)
        def _():
            keys.far()
            outw.far()
            keys.got(13)

        @pl.when(step == 5)
        def _():
            keys.got(14)
            feed[0].pair()

        @pl.when(step == 6)
        def _():
            keys.last()
            keys.got(15)
            feed[2].begin()

        @pl.when(step == 7)
        def _():
            keys.got(16)
            outw.last()
            emits[1].start()

        place = chip_of(me, step, PAIRS)
        slot = lax.rem(step, 4)

        @pl.when(step >= 4)
        def _():
            store(0, place, slot).wait()

        acc[0] += attend(0, place, slot)
        store(0, place, slot).start()
        return carry

    lax.fori_loop(0, 8, first_head, 0)
    close(0)

    def more_heads(i, carry):
        @pl.when(i == 0)
        def _():
            feed[1].near()

        @pl.when(i == 1)
        def _():
            feed[0].far()
            feed[1].pair()

        @pl.when(i == 2)
        def _():
            share[0].near()
            share[0].pair()

        @pl.when(i == 3)
        def _():
            feed[0].last()
            share[0].far()

        @pl.when(i == 4)
        def _():
            close(1)
            share[0].last()
            feed[2].near()

        @pl.when(i == 5)
        def _():
            feed[1].far()
            feed[2].pair()

        @pl.when(i == 6)
        def _():
            share[1].near()
            share[1].pair()

        @pl.when(i == 7)
        def _():
            feed[1].last()
            share[1].far()

        h = 1 + i // 4
        for half in range(2):
            place = chip_of(me, 2 * lax.rem(i, 4) + half, PAIRS)
            slot = 2 * lax.rem(i, 2) + half
            store(h, place, slot).wait()
            acc[h] += attend(h, place, slot)
            store(h, place, slot).start()
        return carry

    lax.fori_loop(0, 8, more_heads, 0)
    close(2)
    share[1].last()
    share[2].near()
    share[2].pair()
    share[2].far()
    share[2].last()
    outw.end()

    def forward_rows(i, carry):
        rows = pl.ds(pl.multiple_of(i * 256, 256), 256)
        value = x_ref[rows].astype(F32) + dot(att[:, rows].T, wo[...])
        inverse = rms_inverse(value)
        mid[rows] = value
        inv[rows] = jnp.broadcast_to(inverse, (256, 128))
        hidden = (value * inverse).astype(BF)
        low[rows] = hidden

        @pl.when(i == 0)
        def _():
            keep[2].wait()
            feed[0].end()
            keep[3].wait()
            feed[1].end()
            feed[2].far()

        g = dot(hidden, wf[0])
        u = dot(hidden, wf[1])
        gate[rows] = g
        up[rows] = u
        act[rows] = (g * jax.nn.sigmoid(g) * u).astype(BF)
        return carry

    lax.fori_loop(0, 2, forward_rows, 0)
    emits[5].start()
    emits[6].start()
    feed[2].last()
    keep[4].wait()
    feed[2].end()

    def down_rows(i, carry):
        rows = pl.ds(pl.multiple_of(i * 256, 256), 256)
        ffn[rows] = dot_nt(act[rows], wf[2]).astype(BF)
        return carry

    lax.fori_loop(0, 2, down_rows, 0)
    sum_f.begin()
    gain_two[...] = jnp.zeros_like(gain_two)

    def backward_rows(i, carry):
        @pl.when(i == 1)
        def _():
            sum_f.relay()

        rows = pl.ds(pl.multiple_of(i * 256, 256), 256)
        ct = cot[rows]
        g, u = gate[rows], up[rows]
        sig = jax.nn.sigmoid(g)
        grad_act = dot(ct, wf[2])
        gg = (grad_act * u * sig * (1.0 + g * (1.0 - sig))).astype(BF)
        gu = (grad_act * g * sig).astype(BF)
        grad_g[rows] = gg
        grad_u[rows] = gu
        back = dot_nt(gg, wf[0]) + dot_nt(gu, wf[1])
        hat = low[rows].astype(F32)
        both = back * hat
        gain_two[...] += jnp.sum(both, axis=0, keepdims=True)
        pull = jnp.mean(both, axis=-1, keepdims=True)
        part = (ct.astype(F32) * 0.125 + inv[rows][:, 0:1] * (back - hat * pull)).astype(BF)
        share_ref[rows] = part
        u_ref[:, rows] = dot_nt(wo[...], part).astype(BF)
        return carry

    lax.fori_loop(0, 2, backward_rows, 0)
    for k in range(7, 10):
        emits[k].start()
    mid_own[...] = mid[pl.ds(pl.multiple_of(me.t * 64, 64), 64)]
    sum_f.columns(col_sum)
    for k in range(10):
        emits[k].wait()
    keys.sent()
    sum_f.sent()
    for s in share:
        s.sent()
    for slot in range(4):
        store(0, 0, slot).wait()


def forward_part(*operands):
    tokens = 512
    kept = [
        ((1536, 384), BF),
        ((16 * tokens, 128), BF),
        ((128, 3 * tokens), BF),
        ((384, tokens), F32),
        ((tokens, 1536), BF),
        ((tokens, 1536), BF),
        ((tokens, 896), BF),
        ((tokens, 896), BF),
        ((tokens, 896), BF),
        ((tokens, 1536), BF),
    ]
    shapes = [jax.ShapeDtypeStruct(*k) for k in kept] + [
        jax.ShapeDtypeStruct((8, 3 * tokens), F32),
        jax.ShapeDtypeStruct((192, tokens), BF),
        jax.ShapeDtypeStruct((1536, tokens), BF),
        jax.ShapeDtypeStruct((64, 1536), F32),
        jax.ShapeDtypeStruct((2, 64, 1536), BF),
        jax.ShapeDtypeStruct((1, 1536), F32),
        jax.ShapeDtypeStruct((8, 3, 1024, tokens), BF),
    ]
    scratch = [
        *[pltpu.VMEM(*k) for k in kept],
        pltpu.VMEM((1536, 256), BF),
        pltpu.VMEM((3, 1536, 896), BF),
        pltpu.VMEM((1536, 1536), BF),
        pltpu.VMEM((1536, tokens), BF),
        pltpu.VMEM((3, 80, tokens), F32),
        pltpu.VMEM((4, 1024, tokens), BF),
        pltpu.VMEM((tokens, 1536), F32),
        pltpu.VMEM((tokens, 128), F32),
        pltpu.VMEM((tokens, 896), F32),
        pltpu.VMEM((tokens, 896), F32),
        pltpu.VMEM((tokens, 1536), BF),
        *[DMA((17,))] * 4,
        *[DMA((3, 17))] * 2,
        *[DMA((17,))] * 4,
        *[DMA((3, 9))] * 2,
        DMA((5,)),
        DMA((4,)),
        DMA((10,)),
        *ring_scratch(32, 1536),
    ]
    return pl.pallas_call(
        forward_kernel,
        out_shape=shapes,
        in_specs=[SM] + [VM] * 7,
        out_specs=[HB] * 10 + [VM] * 6 + [HB],
        scratch_shapes=scratch,
        name="forward_part",
        compiler_params=pltpu.CompilerParams(
            collective_id=0, has_side_effects=True, vmem_limit_bytes=59 << 20
        ),
    )(*operands)


def backward_kernel(
    wq_in, kv_in, qt_in, raw_in, normed_in, low, act, grad_g, grad_u, share_in,
    sums, att_own, u_ref, mid_own, col_sum, gain_two, p_all, cot, x_in, cos_ref, sin_ref,
    blk, gin, own_q, own_w, gains,
    wq, kv, qt, raw, share_ref, x_ref, col_z,
    mid_rows, branch, gt, drift, dq, gk, gk_sib, wg, sib_w, pw, sib_p, back, pre, extra,
    s_blk, r_blk, s_br, r_br, s_in, r_in, s_ex, r_ex, s_sib, r_sib, s_loc, s_p,
    *rest,
):
    me = Place()
    cn = ctx_neighbours(me)
    tn = tp_neighbours(me)
    sib = cn[3]
    tokens = 512
    scratch = [rest[8 * k : 8 * k + 8] for k in range(8)]
    crossing = tp_cross(me)
    greet([*cn, *tn, *crossing, (me.c, me.tp(0, 2)), (me.c, me.tp(1, 2))])

    def tp_block(k):
        return me.tp(*SLOTS[k])

    def chip(k):
        dz, dx = SLOTS[k]
        return me.ctx(dz, dx) // 2

    def rows_of(ref, size):
        def src(k, part):
            start = pl.multiple_of(tp_block(k) * size, size) + part * (size // 2)
            return ref.at[pl.ds(pl.multiple_of(start, size // 2), size // 2)]

        return src

    sum_u = ring(rows_of(u_ref, 192), 96, scratch[0], tn, True, crossing)
    sum_two = ring(rows_of(share_ref, 64), 32, scratch[1], tn, True, crossing)
    sum_b = ring(rows_of(back, 64), 32, scratch[2], tn, False, crossing)
    sum_kv = ring(
        lambda k, part: gk.at[k, me.core, pl.ds(64 * part, 64)], 64, scratch[3], cn
    )
    sum_w = [
        ring(
            lambda k, part, p=p: wg.at[p, chip(k), me.core, pl.ds(48 * part, 48)],
            48,
            scratch[4 + p],
            cn,
        )
        for p in range(3)
    ]
    sum_q = ring(
        lambda k, part: pw.at[chip(k), me.core, pl.ds(48 * part, 48)], 48, scratch[7], cn
    )
    put_two = Gather(blk, 64, me.tp, *tn, None, s_blk, r_blk, over=True)
    put_br = Gather(branch, 64, me.tp, *tn, None, s_br, r_br)
    put_in = Gather(gin, 64, me.tp, *tn, None, s_in, r_in)
    others = [(dz, dy) for dz in (0, 1) for dy in range(4) if (dz, dy) != (0, 0)]
    put_ex = [
        pltpu.make_async_remote_copy(
            src_ref=extra.at[0],
            dst_ref=extra.at[1 + k],
            send_sem=s_ex.at[k],
            recv_sem=r_ex.at[k],
            device_id=(me.c, me.tp(*o)),
            device_id_type=MESH,
        )
        for k, o in enumerate(others)
    ]

    def to_sibling(k, here, there):
        return pltpu.make_async_remote_copy(
            src_ref=here,
            dst_ref=there,
            send_sem=s_sib.at[k],
            recv_sem=r_sib.at[k],
            device_id=sib,
            device_id_type=MESH,
        )

    def key_swap(k):
        return to_sibling(k, gk.at[k, 1 - me.core], gk_sib.at[k])

    swap_w = [to_sibling(8 + p, wg.at[p, :, 1 - me.core], sib_w.at[p]) for p in range(3)]
    swap_p = to_sibling(11, pw.at[:, 1 - me.core], sib_p)
    cross = pltpu.make_async_remote_copy(
        src_ref=col_sum.at[1],
        dst_ref=col_z,
        send_sem=s_sib.at[12],
        recv_sem=r_sib.at[12],
        device_id=tn[0],
        device_id_type=MESH,
    )
    takes = [
        pltpu.make_async_copy(h, v, s_loc.at[14 + k])
        for k, (h, v) in enumerate(
            [
                (wq_in, wq),
                (kv_in, kv),
                (qt_in, qt),
                (raw_in, raw),
                (share_in, share_ref),
                (x_in.at[pl.ds(pl.multiple_of(me.t * 64, 64), 64)], x_ref),
            ]
        )
    ]

    sum_u.begin()
    cross.start()

    def weight_grads(b_low, b_cot, b_one, b_two):
        def load(k, here, there):
            return pltpu.make_async_copy(here, there, s_loc.at[k])

        loads = [load(0, low, b_low), load(1, grad_g, b_one), load(2, grad_u, b_two)]
        loads += [load(3, cot, b_cot), load(4, act, b_one)]
        for k in loads[0:4] + takes:
            k.start()
        loads[0].wait()
        for p, (left, right) in enumerate([(b_low, b_one), (b_low, b_two), (b_cot, b_one)]):
            loads[(1, 2, 4)[p]].wait()
            if p == 2:
                loads[3].wait()

            def chunk(i, carry, p=p, left=left, right=right):
                at = pl.ds(pl.multiple_of(384 * i, 384), 384)
                whole = dot(left[:, at].T, right[...]).astype(BF)
                for q in range(4):
                    wg[p, 2 * i + q // 2, q % 2] = whole[96 * q : 96 * q + 96]
                return carry

            lax.fori_loop(0, 4, chunk, 0)
            swap_w[p].start()
            if p == 0:
                loads[4].start()
                sum_u.relay()

    pl.run_scoped(
        weight_grads,
        pltpu.VMEM((tokens, 1536), BF),
        pltpu.VMEM((tokens, 1536), BF),
        pltpu.VMEM((tokens, 896), BF),
        pltpu.VMEM((tokens, 896), BF),
    )

    def join_w(p):
        swap_w[p].wait_recv()

        def one(j, carry):
            add_into(wg.at[p, j, me.core], wg.at[p, j, me.core], sib_w.at[p, j])
            return carry

        lax.fori_loop(0, 8, one, 0)

    join_w(0)
    sum_w[0].begin()
    for k in takes:
        k.wait()
    grad_att = jnp.concatenate([sum_u.finish(0), sum_u.finish(1)], axis=0)
    own = pl.multiple_of(me.t * 64, 64)
    cross.wait_recv()
    blk[pl.ds(own, 64)] = (
        mid_own[...] + col_sum[0].astype(F32) + col_z[...].astype(F32)
    ).astype(BF)
    sum_two.begin()
    put_two.begin()
    gt[0:64] = jnp.zeros((64, 3 * tokens), BF)
    for h in range(3):
        cols = slice(h * tokens, (h + 1) * tokens)
        grad = grad_att[64 * h : 64 * h + 64]
        inverse = 1.0 / sums[0:1, cols]
        gt[64:128, cols] = (grad * inverse).astype(BF)
        drift[0:1, cols] = (
            jnp.sum(grad * att_own[64 * h : 64 * h + 64].astype(F32), axis=0, keepdims=True)
            * inverse
        )
    dq[...] = jnp.zeros_like(dq)

    def join_keys(k):
        key_swap(k).wait_recv()
        add_into(gk.at[k, me.core], gk.at[k, me.core], gk_sib.at[k])

    def key_loop(pbuf):
        def load(step, h):
            return pltpu.make_async_copy(
                p_all.at[chip_of(me, step, SLOTS), h], pbuf.at[h], s_p.at[h]
            )

        for h in range(3):
            load(0, h).start()

        def key_step(step, carry):
            @pl.when(step == 1)
            def _():
                join_keys(0)
                sum_kv.go(0, 1)
                sum_two.relay()
                sum_w[0].relay()
                join_w(1)
                sum_w[1].begin()

            @pl.when(step == 2)
            def _():
                join_keys(1)
                sum_kv.go(2, 3)
                put_two.near()

            @pl.when(step == 3)
            def _():
                join_keys(2)
                sum_kv.go(4)
                sum_kv.relay_right(1)
                branch_rows = jnp.concatenate([sum_two.finish(0), sum_two.finish(1)], axis=0)
                mid_rows[...] = branch_rows
                branch[pl.ds(own, 64)] = branch_rows.astype(BF)
                put_br.begin()
                sum_w[0].column()
                sum_w[1].relay()
                join_w(2)
                sum_w[2].begin()

            @pl.when(step == 4)
            def _():
                join_keys(3)
                sum_kv.go(5)
                sum_kv.relay_left(1)
                put_two.far()

            @pl.when(step == 5)
            def _():
                join_keys(4)
                sum_kv.go(6)
                sum_kv.relay_right(0)
                sum_w[1].column()
                put_two.pair()
                put_br.near()
                put_br.pair()

            @pl.when(step == 6)
            def _():
                join_keys(5)
                sum_kv.go(7)
                sum_kv.relay_left(0)
                put_br.far()
                put_two.last()
                sum_w[2].relay()

            @pl.when(step == 7)
            def _():
                join_keys(6)
                sum_kv.column()
                put_br.last()

            place = chip_of(me, step, SLOTS)
            rows = kv[pl.ds(pl.multiple_of(place * 1024, 1024), 1024), :]
            key_t = rows.T[0:64]
            key_grad = value_grad = 0.0
            for h in range(3):
                cols = slice(h * tokens, (h + 1) * tokens)
                slopes = dot(rows, gt[:, cols])
                load(step, h).wait()
                weight = pbuf[h]
                grad = (weight.astype(F32) * (slopes - drift[0:1, cols])).astype(BF)
                dq[:, cols] += dot(key_t, grad)
                key_grad += dot_nt(qt[0:64, cols], grad)
                value_grad += dot_nt(gt[64:128, cols], weight)

                @pl.when(step < 7)
                def _(h=h):
                    load(step + 1, h).start()

            both = jnp.concatenate([key_grad * LN2, value_grad], axis=0).astype(BF)
            gk[step, 0] = both[:, 0:512]
            gk[step, 1] = both[:, 512:1024]
            key_swap(step).start()
            return carry

        lax.fori_loop(0, 8, key_step, 0)

    pl.run_scoped(key_loop, pltpu.VMEM((3, 1024, tokens), BF))
    def finale(normed):
        fetch = pltpu.make_async_copy(normed_in, normed, s_loc.at[5])
        fetch.start()
        query_gain, key_gain = gain_columns(wq)
        cosine, sine = cos_ref[...], sin_ref[...]

        def unturn(grad, value, gain):
            inverse = column_inverse(value)
            hat = value * inverse
            a, b = grad[:32], grad[32:]
            plain = jnp.concatenate([a * cosine + b * sine, b * cosine - a * sine], axis=0)
            gain_grad = jnp.sum(plain * hat, axis=1, keepdims=True)
            pulled = plain * gain
            back_grad = inverse * (pulled - hat * jnp.mean(pulled * hat, axis=0, keepdims=True))
            return gain_grad, back_grad

        query_gain_grad = 0.0
        for h in range(3):
            part, grad = unturn(
                dq[:, h * tokens : (h + 1) * tokens] * 0.125, raw[64 * h : 64 * h + 64], query_gain
            )
            query_gain_grad += part
            pre[64 * h : 64 * h + 64] = grad
        join_keys(7)
        key_grad, value_grad = sum_kv.finish(0), sum_kv.finish(1)
        key_gain_grad, grad = unturn(key_grad, raw[192:256], key_gain)
        pre[192:256] = grad
        pre[256:320] = value_grad
        pre[320:384] = jnp.zeros((64, tokens), F32)
        pre_n = pre[...].T.astype(BF)
        for i in range(2):
            rows = slice(256 * i, 256 * i + 256)
            back[rows] = dot_nt(pre_n[rows], wq[...]).astype(BF)
        sum_b.begin()
        fetch.wait()
        gain_one = 0.0
        for i in range(4):
            rows = slice(128 * i, 128 * i + 128)
            gain_one += jnp.sum(
                back[rows].astype(F32) * normed[rows].astype(F32), axis=0, keepdims=True
            )
        sum_w[2].column()
        lane = lax.broadcasted_iota(jnp.int32, (64, 1536), 1)
        unit = lax.broadcasted_iota(jnp.int32, (64, 1536), 0)
        spot = lane == (unit // 4) * 96 + lax.rem(unit, 4)

        def spread(column):
            return jnp.sum(jnp.where(spot, column, 0.0), axis=0, keepdims=True)

        lines = jnp.concatenate(
            [
                jnp.zeros((64, 1536), F32),
                gain_one,
                gain_two[...],
                spread(query_gain_grad),
                spread(key_gain_grad),
                jnp.zeros((60, 1536), F32),
            ],
            axis=0,
        )
        sides = lines.T
        sum_b.relay()
        att_n = jnp.concatenate([att_own[...].astype(F32), jnp.zeros((64, tokens), F32)], axis=0).T.astype(BF)
        for i in range(4):
            at = slice(384 * i, 384 * i + 384)
            part = dot(normed[:, at].T, pre_n)
            part = jnp.concatenate([part[:, 0:256], part[:, 256:384] + sides[at]], axis=1)
            whole = jnp.concatenate([part, dot(branch[:, at].T, att_n)], axis=1).astype(BF)
            for q in range(4):
                pw[2 * i + q // 2, q % 2] = whole[96 * q : 96 * q + 96]
        swap_p.start()
        swap_p.wait_recv()

        def join_p(j, carry):
            add_into(pw.at[j, me.core], pw.at[j, me.core], sib_p.at[j])
            return carry

        lax.fori_loop(0, 8, join_p, 0)
        sum_q.begin()
        value = x_ref[...].astype(F32)
        inverse = rms_inverse(value)
        hat = value * inverse
        back_one = jnp.concatenate([sum_b.finish(0), sum_b.finish(1)], axis=0)
        gin[pl.ds(own, 64)] = (
            mid_rows[...]
            + inverse * (back_one - hat * jnp.mean(back_one * hat, axis=-1, keepdims=True))
        ).astype(BF)
        put_in.begin()
        for p in range(3):
            for half in range(2):
                own_w[p, 48 * half : 48 * half + 48] = sum_w[p].finish(half)
        put_in.near()
        sum_q.relay()
        put_in.pair()
        sum_q.column()
        put_in.far()
        for half in range(2):
            own_q[48 * half : 48 * half + 48] = sum_q.finish(half)
        extra[0] = own_q[:, 256:384].T[64:72]
        for p in put_ex:
            p.start()
        put_in.last()
        for p in put_ex:
            p.wait()
        total = extra[0]
        for b in range(1, 8):
            total += extra[b]
        gains[...] = total
        for s in [sum_u, sum_two, sum_b, sum_kv, sum_q, *sum_w, put_two, put_br, put_in]:
            s.sent()
        for k in range(8):
            key_swap(k).wait_send()
        for s in [*swap_w, swap_p, cross]:
            s.wait_send()

    pl.run_scoped(finale, pltpu.VMEM((tokens, 1536), BF))


def backward_part(*operands):
    tokens = 512
    shapes = [
        jax.ShapeDtypeStruct((512, 1536), BF),
        jax.ShapeDtypeStruct((512, 1536), BF),
        jax.ShapeDtypeStruct((96, 640), F32),
        jax.ShapeDtypeStruct((3, 96, 896), F32),
        jax.ShapeDtypeStruct((8, 96), F32),
    ]
    scratch = [
        pltpu.VMEM((1536, 384), BF),
        pltpu.VMEM((16 * tokens, 128), BF),
        pltpu.VMEM((128, 3 * tokens), BF),
        pltpu.VMEM((384, tokens), F32),
        pltpu.VMEM((tokens, 1536), BF),
        pltpu.VMEM((64, 1536), BF),
        pltpu.VMEM((64, 1536), BF),
        pltpu.VMEM((64, 1536), F32),
        pltpu.VMEM((tokens, 1536), BF),
        pltpu.VMEM((128, 3 * tokens), BF),
        pltpu.VMEM((8, 3 * tokens), F32),
        pltpu.VMEM((64, 3 * tokens), F32),
        pltpu.VMEM((8, 2, 128, 512), BF),
        pltpu.VMEM((8, 128, 512), BF),
        pltpu.VMEM((3, 8, 2, 96, 896), BF),
        pltpu.VMEM((3, 8, 96, 896), BF),
        pltpu.VMEM((8, 2, 96, 640), BF),
        pltpu.VMEM((8, 96, 640), BF),
        pltpu.VMEM((tokens, 1536), BF),
        pltpu.VMEM((384, tokens), F32),
        pltpu.VMEM((8, 8, 96), F32),
        *[DMA((9,))] * 8,
        DMA((13,)),
        DMA((13,)),
        DMA((21,)),
        DMA((3,)),
        *ring_scratch(96, 512, True),
        *ring_scratch(32, 1536, True),
        *ring_scratch(32, 1536),
        *ring_scratch(64, 512),
        *ring_scratch(48, 896) * 3,
        *ring_scratch(48, 640),
    ]
    return pl.pallas_call(
        backward_kernel,
        out_shape=shapes,
        in_specs=[HB] * 10 + [VM] * 6 + [HB] * 3 + [VM] * 2,
        out_specs=[VM] * 5,
        scratch_shapes=scratch,
        name="backward_part",
        compiler_params=pltpu.CompilerParams(
            collective_id=1, has_side_effects=True, vmem_limit_bytes=59 << 20
        ),
    )(*operands)


FREQ = [[THETA ** (-2.0 * i / HD)] * 128 for i in range(HD // 2)]


def body(
    block_input, positions, attn_gain, query_weight, key_weight, value_weight, query_gain,
    key_gain, output_weight, ffn_gain, gate_weight, up_weight, down_weight, out_cotangent,
):
    def line(gain):
        return gain.reshape(1, -1)

    wq_s, wo_s, wf_s, cosine, sine = prepare(
        line(positions), line(attn_gain), line(ffn_gain), line(query_gain), line(key_gain),
        jnp.array(FREQ, F32), query_weight, key_weight.T, value_weight.T, output_weight,
        gate_weight, up_weight, down_weight.T,
    )
    results = forward_part(positions, block_input, out_cotangent, wq_s, wo_s, wf_s, cosine, sine)
    results = backward_part(*results, out_cotangent, block_input, cosine, sine)
    return conclude(line(attn_gain), line(ffn_gain), *results)


def solution(mesh):
    in_specs = (
        P("ctx", None),
        P(),
        P("ctx"),
        P("ctx", "tp"),
        P("ctx", "tp"),
        P("ctx", "tp"),
        P("ctx"),
        P("ctx"),
        P("tp", "ctx"),
        P("ctx"),
        P("ctx", "tp"),
        P("ctx", "tp"),
        P("tp", "ctx"),
        P("ctx", None),
    )
    out_specs = (
        P("ctx", None),
        P("ctx", None),
        P("ctx"),
        P("ctx", "tp"),
        P("ctx", "tp"),
        P("ctx", "tp"),
        P("ctx"),
        P("ctx"),
        P("tp", "ctx"),
        P("ctx"),
        P("ctx", "tp"),
        P("ctx", "tp"),
        P("tp", "ctx"),
    )
    return jax.shard_map(body, mesh=mesh, in_specs=in_specs, out_specs=out_specs, check_vma=False)
```

```python
import functools
import math

import jax
import jax.numpy as jnp
from jax import lax
from jax.experimental import pallas as pl
from jax.experimental.pallas import tpu as pltpu
from jax.sharding import PartitionSpec as P

HD = 64
EPS = 1e-05
THETA = 1000000.0
LOG2E = math.log2(math.e)
LN2 = math.log(2.0)
BF = jnp.bfloat16
F32 = jnp.float32
MESH = pl.DeviceIdType.MESH
VM = pl.BlockSpec(memory_space=pltpu.VMEM)
SM = pl.BlockSpec(memory_space=pltpu.SMEM)
HB = pl.BlockSpec(memory_space=pl.ANY)
DMA = pltpu.SemaphoreType.DMA


class Place:
    def __init__(self):
        self.c = lax.axis_index("ctx")
        self.t = lax.axis_index("tp")
        self.core = lax.rem(self.c, 2)
        self.x = lax.rem(self.c // 2, 4)
        self.zh = self.c // 8
        self.y = lax.rem(self.t, 4)
        self.zl = self.t // 4

    def ctx(self, dz, dx, other=0):
        core = self.core if not other else 1 - self.core
        zh = self.zh if not dz else 1 - self.zh
        return (zh * 4 + lax.rem(self.x + dx, 4)) * 2 + core

    def tp(self, dz, dy):
        zl = self.zl if not dz else 1 - self.zl
        return zl * 4 + lax.rem(self.y + dy, 4)


def greet(peers):
    barrier = pltpu.get_barrier_semaphore()
    for peer in peers:
        pl.semaphore_signal(barrier, inc=1, device_id=peer, device_id_type=MESH)
    pl.semaphore_wait(barrier, len(peers))


class Gather:
    def __init__(self, buf, rows, block, pair, right, left, sibling, send, recv, own=None, cross=(), over=False):
        self.buf, self.rows, self.block = buf, rows, block
        self.to = {"z": pair, "r": right, "l": left, "s": sibling}
        self.cross = len(cross) > 0
        if self.cross:
            self.to["zr"], self.to["zl"] = cross
        self.send, self.recv, self.own = send, recv, own
        self.plan = {
            0: ((0, 0), 0, "z"),
            1: ((0, 0), 0, "r"),
            2: ((0, 0), 0, "l"),
            3: ((0, 3), 1, "r"),
            4: ((0, 1), 2, "l"),
            5: ((1, 0), 0, "r"),
            6: ((1, 0), 0, "l"),
            7: ((1, 3), 1, "r"),
            8: ((1, 1), 2, "l"),
            9: ((0, 0), 0, "s"),
            10: ((1, 0), 0, "s"),
            11: ((0, 3), 0, "s"),
            12: ((0, 1), 0, "s"),
            13: ((0, 2), 0, "s"),
            14: ((1, 3), 0, "s"),
            15: ((1, 1), 0, "s"),
            16: ((1, 2), 0, "s"),
        }
        if self.cross:
            self.plan[5] = ((0, 0), 0, "zr")
            self.plan[6] = ((0, 0), 0, "zl")
        self.over = over
        if over:
            self.plan[5] = ((0, 3), 0, "z")
            self.plan[6] = ((0, 1), 0, "z")
            self.plan[7] = ((0, 2), 1, "z")
            self.plan[8] = ((0, 2), 2, "z")
        self.count = 17 if sibling is not None else 9

    def copy(self, k):
        where, part, to = self.plan[k]
        rows = self.rows if part == 0 else self.rows // 2
        start = pl.multiple_of(self.block(*where) * self.rows, self.rows)
        if part == 2:
            start = pl.multiple_of(start + rows, rows)
        there = self.buf.at[pl.ds(start, rows)]
        here = there
        if where == (0, 0) and self.own is not None:
            here = self.own
        return pltpu.make_async_remote_copy(
            src_ref=here,
            dst_ref=there,
            send_sem=self.send.at[k],
            recv_sem=self.recv.at[k],
            device_id=self.to[to],
            device_id_type=MESH,
        )

    def go(self, *which):
        for k in which:
            if k < self.count:
                self.copy(k).start()

    def got(self, *which):
        for k in which:
            if k < self.count:
                self.copy(k).wait_recv()

    def begin(self):
        self.go(0, 1, 2, 9)
        if self.cross:
            self.go(5, 6)

    def near(self):
        self.got(1)
        self.go(3, 11)
        if self.over:
            self.go(5)
        self.got(2)
        self.go(4, 12)
        if self.over:
            self.go(6)

    def pair(self):
        self.got(0)
        if not self.cross and not self.over:
            self.go(5, 6)
        self.go(10)

    def far(self):
        if self.over:
            self.got(3)
            self.go(7)
            self.got(4)
            self.go(8)
            self.got(5, 6)
            return
        self.got(5)
        self.go(7, 14)
        self.got(6)
        self.go(8, 15)
        self.got(3, 4)
        self.go(13)

    def last(self):
        self.got(7, 8)
        self.go(16)

    def sent(self):
        for k in range(self.count):
            self.copy(k).wait_send()

    def end(self):
        self.got(*range(9, 17))
        self.sent()


def ctx_neighbours(me):
    return (
        (me.ctx(1, 0), me.t),
        (me.ctx(0, 1), me.t),
        (me.ctx(0, 3), me.t),
        (me.ctx(0, 0, 1), me.t),
    )


def tp_neighbours(me):
    return (me.c, me.tp(1, 0)), (me.c, me.tp(0, 1)), (me.c, me.tp(0, 3))


def tp_cross(me):
    return (me.c, me.tp(1, 1)), (me.c, me.tp(1, 3))


def rms_inverse(value):
    return lax.rsqrt(jnp.mean(value * value, axis=-1, keepdims=True) + EPS)


def column_inverse(value):
    return lax.rsqrt(jnp.mean(value * value, axis=0, keepdims=True) + EPS)


def gain_columns(wq):
    total = wq[0:64, 256:384].astype(F32)
    for k in range(1, 16):
        total += wq[96 * k : 96 * k + 64, 256:384].astype(F32)
    return total[:, 64:65], total[:, 65:66]


def dot(a, b):
    return jnp.dot(a, b, preferred_element_type=F32)


def dot_nt(a, b):
    return lax.dot_general(a, b, (((1,), (1,)), ((), ())), preferred_element_type=F32)


def dot_tn(a, b):
    return lax.dot_general(a, b, (((0,), (0,)), ((), ())), preferred_element_type=F32)


PAIRS = ((0, 0), (0, 3), (0, 1), (1, 0), (0, 2), (1, 3), (1, 1), (1, 2))


def chip_of(me, step, order):
    dz = sum(jnp.where(step == k, p[0], 0) for k, p in enumerate(order) if p[0])
    dx = sum(jnp.where(step == k, p[1], 0) for k, p in enumerate(order) if p[1])
    return lax.rem(me.zh + dz, 2) * 4 + lax.rem(me.x + dx, 4)


SLOTS = ((1, 2), (0, 2), (1, 1), (1, 3), (0, 1), (0, 3), (1, 0), (0, 0))


def add_into(out, *terms):
    total = terms[0][...].astype(F32)
    for term in terms[1:]:
        total += term[...].astype(F32)
    out[...] = total.astype(out.dtype)


class RingSum:
    def __init__(self, src, half, stage, rel_l, rel_r, col_l, col_r, from_z, pair, right, left, send, recv, cross=()):
        self.src, self.half = src, half
        at_stage = {2: (0, 0), 3: (0, 1), 4: (1, 0), 5: (1, 1)}

        def put(k, part):
            if stage is None:
                return src(k, part)
            rows = pl.ds(part * half, half)
            return stage.at[2 if k == 6 else at_stage[k][0], rows]

        self.put = put
        self.rel_l, self.rel_r, self.col_l, self.col_r, self.from_z = rel_l, rel_r, col_l, col_r, from_z
        self.to = {"z": pair, "r": right, "l": left, "zr": right, "zl": left}
        self.cross = len(cross) > 0
        if self.cross:
            self.to["zr"], self.to["zl"] = cross
        self.send, self.recv = send, recv
        low, high = pl.ds(0, half), pl.ds(half, half)
        self.low, self.high = low, high
        self.last = 14
        self.plan = [
            (src(0, 0), rel_l.at[1], "r"),
            (src(0, 1), rel_r.at[1], "l"),
            (src(1, 0), rel_l.at[0], "r"),
            (src(1, 1), rel_r.at[0], "l"),
            (src(2, 1), col_l.at[1, high], "zr"),
            (src(3, 0), col_r.at[1, low], "zl"),
            (src(4, 1), col_l.at[0, high], "r"),
            (src(5, 0), col_r.at[0, low], "l"),
            (put(2, 0), col_l.at[1, low], "zr"),
            (put(3, 1), col_r.at[1, high], "zl"),
            (put(4, 0), col_l.at[0, low], "r"),
            (put(5, 1), col_r.at[0, high], "l"),
            ((src if self.cross else put)(6, 0), from_z.at[low], "z"),
            ((src if self.cross else put)(6, 1), from_z.at[high], "z"),
        ]

    def copy(self, k):
        here, there, to = self.plan[k]
        return pltpu.make_async_remote_copy(
            src_ref=here,
            dst_ref=there,
            send_sem=self.send.at[k],
            recv_sem=self.recv.at[k],
            device_id=self.to[to],
            device_id_type=MESH,
        )

    def go(self, *which):
        for k in which:
            self.copy(k).start()

    def got(self, *which):
        for k in which:
            self.copy(k).wait_recv()

    def begin(self):
        self.go(*range(8))
        if self.cross:
            self.go(12, 13)

    def relay_right(self, plane):
        k = 2 if plane else 4
        self.got(0 if plane else 2)
        add_into(self.put(k, 0), self.src(k, 0), self.rel_l.at[plane])
        self.go(8 if plane else 10)

    def relay_left(self, plane):
        k = 3 if plane else 5
        self.got(1 if plane else 3)
        add_into(self.put(k, 1), self.src(k, 1), self.rel_r.at[plane])
        self.go(9 if plane else 11)

    def relay(self):
        for plane in (1, 0):
            self.relay_right(plane)
            self.relay_left(plane)

    def column(self):
        self.got(4, 8, 5, 9)
        for part, rows in enumerate((self.low, self.high)):
            add_into(
                self.put(6, part),
                self.src(6, part),
                self.col_l.at[1, rows],
                self.col_r.at[1, rows],
            )
            self.go(12 + part)

    def columns(self, out):
        self.last = 12
        self.got(4, 8, 5, 9, 6, 10, 7, 11)
        for plane, k in ((0, 7), (1, 6)):
            for part, rows in enumerate((self.low, self.high)):
                add_into(
                    out.at[plane, rows],
                    self.src(k, part),
                    self.col_l.at[plane, rows],
                    self.col_r.at[plane, rows],
                )

    def finish(self, part):
        if part == 0:
            self.got(6, 10, 7, 11, 12, 13)
            if self.cross:
                self.got(4, 8, 5, 9)
        rows = self.low if part == 0 else self.high
        total = self.src(7, part)[...].astype(F32)
        terms = [self.col_l.at[0, rows], self.col_r.at[0, rows], self.from_z.at[rows]]
        if self.cross:
            terms += [self.col_l.at[1, rows], self.col_r.at[1, rows]]
        for term in terms:
            total += term[...].astype(F32)
        return total

    def sent(self):
        for k in range(self.last):
            self.copy(k).wait_send()


def ring_scratch(half, width, stage=False):
    return [
        pltpu.VMEM((3, 2 * half, width) if stage else (1, 16, 128), BF),
        pltpu.VMEM((2, half, width), BF),
        pltpu.VMEM((2, half, width), BF),
        pltpu.VMEM((2, 2 * half, width), BF),
        pltpu.VMEM((2, 2 * half, width), BF),
        pltpu.VMEM((2 * half, width), BF),
        DMA((14,)),
        DMA((14,)),
    ]


def ring(src, half, scratch, neighbours, stage=False, cross=()):
    room, rel_l, rel_r, col_l, col_r, from_z, send, recv = scratch
    return RingSum(
        src, half, room if stage else None, rel_l, rel_r, col_l, col_r, from_z, *neighbours[:3],
        send, recv, cross,
    )


def gain_lines(lines, refs):
    lines[...] = jnp.zeros_like(lines)
    for k, ref in enumerate(refs):
        lines[k : k + 1, 0 : ref.shape[1]] = ref[...].astype(F32)
    columns = lines[...].T
    return columns[0:96, 0:1], columns[0:96, 1:2]


def prepare_kernel(
    places, attn_gain, ffn_gain, query_gain, key_gain, freq,
    query, key_t, value_t, output, gate, up, down_t, wq_s, wo_s, wf_s, cosine, sine, lines,
):
    c = lax.axis_index("ctx")
    gain_one, gain_two = gain_lines(lines, [attn_gain, ffn_gain, query_gain, key_gain])
    row = lax.broadcasted_iota(jnp.int32, (96, 64), 0)
    col = lax.broadcasted_iota(jnp.int32, (96, 64), 1)
    sides = jnp.zeros((96, 64), F32)
    for k in range(2):
        for j in range(4):
            at = (row == 4 * c + j) & (col == k)
            sides = jnp.where(at, lines[2 + k : 3 + k, j : j + 1], sides)

    def lifted(weight, gain):
        return (weight.astype(F32) * gain).astype(BF)

    both = jnp.concatenate([key_t[...].astype(F32), value_t[...].astype(F32)], axis=0).T
    wq_s[:, 0:192] = lifted(query[...], gain_one)
    wq_s[:, 192:320] = lifted(both, gain_one)
    wq_s[:, 320:384] = sides.astype(BF)
    wo_s[:, 192:256] = jnp.zeros((96, 64), BF)
    wo_s[:, 0:192] = output[...].astype(F32).T.astype(BF)
    for k in range(3):
        wf_s[:, 896 * k + 768 : 896 * k + 896] = jnp.zeros((96, 128), BF)
    wf_s[:, 0:864] = lifted(gate[...], gain_two)
    wf_s[:, 896:1760] = lifted(up[...], gain_two)
    wf_s[:, 1792:2656] = down_t[...]
    place = places[0:1, pl.ds(pl.multiple_of(c * 512, 512), 512)]
    angle = freq[:, 0:1] * place.astype(F32)
    cosine[...] = jnp.cos(angle)
    sine[...] = jnp.sin(angle)


def prepare(*operands):
    shapes = [
        jax.ShapeDtypeStruct((96, 384), BF),
        jax.ShapeDtypeStruct((96, 256), BF),
        jax.ShapeDtypeStruct((96, 2688), BF),
        jax.ShapeDtypeStruct((32, 512), F32),
        jax.ShapeDtypeStruct((32, 512), F32),
    ]
    return pl.pallas_call(
        prepare_kernel,
        out_shape=shapes,
        in_specs=[VM] * 13,
        out_specs=[VM] * 5,
        scratch_shapes=[pltpu.VMEM((8, 128), F32)],
        name="prepare",
        compiler_params=pltpu.CompilerParams(vmem_limit_bytes=59 << 20),
    )(*operands)


def conclude_kernel(
    attn_gain, ffn_gain, block, gin, own_q, own_w, side,
    block_output, grad_input, g_attn, g_query, g_key, g_value, g_qg, g_kg, g_out, g_ffn, g_gate, g_up, g_down,
    lines,
):
    gain_one, gain_two = gain_lines(lines, [attn_gain, ffn_gain])
    block_output[...] = block[...]
    grad_input[...] = gin[...].astype(F32)
    g_query[...] = own_q[:, 0:192] * gain_one
    both = (own_q[:, 192:320] * gain_one).T
    g_key[...] = both[0:64]
    g_value[...] = both[64:128]
    g_out[...] = own_q[:, 384:576].T
    g_gate[...] = own_w[0, :, 0:864] * gain_two
    g_up[...] = own_w[1, :, 0:864] * gain_two
    g_down[...] = own_w[2, :, 0:864]
    g_attn[...] = side[0:1, 0:96] / lines[0:1, 0:96]
    g_ffn[...] = side[1:2, 0:96] / lines[1:2, 0:96]
    g_qg[...] = side[2:3, 0:4]
    g_kg[...] = side[3:4, 0:4]


def conclude(*operands):
    dims = [
        ((512, 1536), BF), ((512, 1536), F32), ((1, 96), F32), ((96, 192), F32), ((64, 96), F32),
        ((64, 96), F32), ((1, 4), F32), ((1, 4), F32), ((192, 96), F32), ((1, 96), F32),
        ((96, 864), F32), ((96, 864), F32), ((96, 864), F32),
    ]
    results = pl.pallas_call(
        conclude_kernel,
        out_shape=[jax.ShapeDtypeStruct(*d) for d in dims],
        in_specs=[VM] * 7,
        out_specs=[VM] * 13,
        scratch_shapes=[pltpu.VMEM((8, 128), F32)],
        name="conclude",
        compiler_params=pltpu.CompilerParams(vmem_limit_bytes=59 << 20),
    )(*operands)
    results = [r.T if k in (4, 5, 12) else r for k, r in enumerate(results)]
    return tuple(r.reshape(-1) if r.shape[0] == 1 else r for r in results)


def forward_kernel(
    kb, x_ref, cot, wq_s, wo_s, wf_s, cos_ref, sin_ref,
    wq_out, kv_out, qt_out, raw_out, normed_out, low_out, act_out, g_out, u_out, share_out,
    sums, att_own, u_ref, mid_own, col_sum, gain_two, p_all,
    wq, kv, qt, raw, normed, low, act, grad_g, grad_u, share_ref,
    wo_t, wf, wo, att, acc, pbuf, mid, inv, gate, up, ffn,
    s_w, r_w, s_v, r_v, s_f, r_f, s_o, r_o, s_k, r_k, s_a, r_a, s_l, s_p, s_out,
    *rest,
):
    me = Place()
    cn = ctx_neighbours(me)
    tn = tp_neighbours(me)
    cross = tp_cross(me)
    tokens = x_ref.shape[0]
    greet([*cn, *tn, *cross])
    weights = Gather(wq, 96, me.ctx, *cn, s_w, r_w, own=wq_s)
    outs = Gather(wo_t, 96, me.ctx, *cn, s_v, r_v, own=wo_s)
    feed = [
        Gather(
            wf.at[p], 96, me.ctx, *cn, s_f.at[p], r_f.at[p], own=wf_s.at[:, 896 * p : 896 * p + 896]
        )
        for p in range(3)
    ]
    keys = Gather(kv, tokens, me.ctx, *cn, s_k, r_k)
    outw = Gather(
        wo, 96, lambda dz, dy: me.tp(dz, dy) * 2 + me.core, *tn, cn[3], s_o, r_o
    )
    share = [
        Gather(
            att, 64, lambda dz, dy, h=h: me.tp(dz, dy) * 3 + h, *tn, None, s_a.at[h], r_a.at[h],
            cross=cross,
        )
        for h in range(3)
    ]
    sum_f = ring(
        lambda k, part: ffn.at[
            pl.ds(pl.multiple_of(me.tp(*SLOTS[k]) * 64 + 32 * part, 32), 32)
        ],
        32, rest, tn,
    )

    weights.begin()
    outs.begin()
    feed[0].go(1, 2, 9)
    mine = pl.ds(pl.multiple_of(me.c * 96, 96), 96)
    keep = [
        pltpu.make_async_copy(wq_s, wq.at[mine], s_l.at[0]),
        pltpu.make_async_copy(wo_s, wo_t.at[mine], s_l.at[1]),
    ] + [
        pltpu.make_async_copy(wf_s.at[:, 896 * p : 896 * p + 896], wf.at[p, mine], s_l.at[2 + p])
        for p in range(3)
    ]
    for k in keep:
        k.start()
    emits = [
        pltpu.make_async_copy(v, h, s_out.at[k])
        for k, (v, h) in enumerate(
            [
                (wq, wq_out),
                (kv, kv_out),
                (qt, qt_out),
                (raw, raw_out),
                (normed, normed_out),
                (low, low_out),
                (act, act_out),
                (grad_g, g_out),
                (grad_u, u_out),
                (share_ref, share_out),
            ]
        )
    ]

    def norm_rows(i, carry):
        rows = pl.ds(pl.multiple_of(i * 64, 64), 64)
        value = x_ref[rows].astype(F32)
        normed[rows] = (value * rms_inverse(value)).astype(BF)
        return carry

    lax.fori_loop(0, tokens // 64, norm_rows, 0)
    weights.near()
    weights.pair()
    feed[0].go(0)
    outs.near()
    outs.pair()
    emits[4].start()
    weights.far()
    weights.last()
    outs.far()
    outs.last()
    keep[1].wait()
    outs.end()
    heads = wo_t[...].T
    wo[pl.ds(pl.multiple_of(me.t * 192 + me.core * 96, 96), 96)] = jnp.where(
        me.core == 0, heads[0:96], heads[96:192]
    )
    outw.begin()
    keep[0].wait()
    weights.end()
    feed[1].go(1, 2, 9)
    emits[0].start()

    def project(i, carry):
        cols = pl.ds(pl.multiple_of(i * 256, 256), 256)
        raw[:, cols] = dot(normed[cols], wq[...]).T
        return carry

    lax.fori_loop(0, tokens // 256, project, 0)
    emits[3].start()
    feed[0].near()
    query_gain, key_gain = gain_columns(wq)
    cosine, sine = cos_ref[...], sin_ref[...]

    def turned(value, gain):
        hat = value * column_inverse(value) * gain
        a, b = hat[:32], hat[32:]
        return jnp.concatenate([a * cosine - b * sine, b * cosine + a * sine], axis=0)

    both = jnp.concatenate([turned(raw[192:256], key_gain), raw[256:320]], axis=0)
    kv[pl.ds(pl.multiple_of(me.c * tokens, tokens), tokens)] = both.T.astype(BF)
    keys.begin()
    qt[64:128] = jnp.zeros((64, 3 * tokens), BF)
    for h in range(3):
        qt[0:64, h * tokens : (h + 1) * tokens] = (
            turned(raw[64 * h : 64 * h + 64], query_gain) * (LOG2E / 8.0)
        ).astype(BF)
    emits[2].start()
    feed[0].pair()
    outw.near()
    acc[...] = jnp.zeros_like(acc)
    ones = jnp.concatenate([jnp.ones((1, 1024), BF), jnp.zeros((15, 1024), BF)], axis=0)
    apart = lax.broadcasted_iota(jnp.int32, (256, 256), 0) - lax.broadcasted_iota(
        jnp.int32, (256, 256), 1
    )

    def attend(h, place, slot):
        rows = kv[pl.ds(pl.multiple_of(place * 1024, 1024), 1024), :]
        scores = dot(rows, qt[:, pl.ds(pl.multiple_of(h * tokens, tokens), tokens)])
        parts = []
        for a in range(4):
            line = []
            for b in range(2):
                sub = scores[a * 256 : a * 256 + 256, b * 256 : b * 256 + 256]
                seen = apart <= kb[me.c * 512 + b * 256] - kb[place * 1024 + a * 256]
                line.append(jnp.where(seen, jnp.exp2(sub), 0.0).astype(BF))
            parts.append(jnp.concatenate(line, axis=1))
        weight = jnp.concatenate(parts, axis=0)
        pbuf[slot] = weight
        left = jnp.concatenate([rows.T[64:128], ones], axis=0)
        return dot(left, weight)

    def store(h, place, slot):
        return pltpu.make_async_copy(pbuf.at[slot], p_all.at[place, h], s_p.at[slot])

    def close(h):
        total = acc[h, 64:65]
        sums[0:1, h * tokens : (h + 1) * tokens] = total
        value = (acc[h, 0:64] / total).astype(BF)
        att_own[64 * h : 64 * h + 64] = value
        att[pl.ds(pl.multiple_of(me.t * 192 + 64 * h, 64), 64)] = value
        share[h].begin()

    def first_head(step, carry):
        @pl.when(step == 0)
        def _():
            keys.got(9)

        @pl.when(step == 1)
        def _():
            keys.near()
            feed[1].go(0)
            outw.pair()
            keys.got(11)

        @pl.when(step == 2)
        def _():
            keys.pair()
            feed[1].near()
            feed[2].go(0)
            keys.got(12)

        @pl.when(step == 3)
        def _():
            keys.got(10)

        @pl.when(step == 4)
        def _():
            keys.far()
            feed[0].far()
            feed[2].go(1, 2, 9)
            outw.far()
            keys.got(13)

        @pl.when(step == 5)
        def _():
            feed[1].pair()
            keys.got(14)

        @pl.when(step == 6)
        def _():
            keys.last()
            keys.got(15)

        @pl.when(step == 7)
        def _():
            keys.got(16)
            feed[0].last()
            feed[2].near()
            outw.last()
            emits[1].start()

        place = chip_of(me, step, PAIRS)
        slot = lax.rem(step, 4)

        @pl.when(step >= 4)
        def _():
            store(0, place, slot).wait()

        acc[0] += attend(0, place, slot)
        store(0, place, slot).start()
        return carry

    lax.fori_loop(0, 8, first_head, 0)
    close(0)

    def more_heads(i, carry):
        @pl.when(i == 1)
        def _():
            feed[2].pair()

        @pl.when(i == 2)
        def _():
            share[0].near()
            share[0].pair()

        @pl.when(i == 3)
        def _():
            feed[1].far()
            share[0].far()

        @pl.when(i == 4)
        def _():
            close(1)
            share[0].last()

        @pl.when(i == 5)
        def _():
            feed[1].last()

        @pl.when(i == 6)
        def _():
            share[1].near()
            share[1].pair()

        @pl.when(i == 7)
        def _():
            feed[2].far()
            share[1].far()

        h = 1 + i // 4
        for half in range(2):
            place = chip_of(me, 2 * lax.rem(i, 4) + half, PAIRS)
            slot = 2 * lax.rem(i, 2) + half
            store(h, place, slot).wait()
            acc[h] += attend(h, place, slot)
            store(h, place, slot).start()
        return carry

    lax.fori_loop(0, 8, more_heads, 0)
    close(2)
    share[1].last()
    share[2].near()
    share[2].pair()
    share[2].far()
    share[2].last()
    outw.end()

    def forward_rows(i, carry):
        rows = pl.ds(pl.multiple_of(i * 256, 256), 256)
        value = x_ref[rows].astype(F32) + dot(att[:, rows].T, wo[...])
        inverse = rms_inverse(value)
        mid[rows] = value
        inv[rows] = jnp.broadcast_to(inverse, (256, 128))
        low[rows] = (value * inverse).astype(BF)
        return carry

    lax.fori_loop(0, 2, forward_rows, 0)
    emits[5].start()
    keep[2].wait()
    feed[0].end()
    feed[2].last()

    def gate_rows(i, carry):
        rows = pl.ds(pl.multiple_of(i * 256, 256), 256)
        gate[rows] = dot(low[rows], wf[0])
        return carry

    lax.fori_loop(0, 2, gate_rows, 0)
    keep[3].wait()
    feed[1].end()

    def up_rows(i, carry):
        rows = pl.ds(pl.multiple_of(i * 256, 256), 256)
        u = dot(low[rows], wf[1])
        up[rows] = u
        g = gate[rows]
        act[rows] = (g * jax.nn.sigmoid(g) * u).astype(BF)
        return carry

    lax.fori_loop(0, 2, up_rows, 0)
    emits[6].start()
    keep[4].wait()
    feed[2].end()

    def down_rows(i, carry):
        rows = pl.ds(pl.multiple_of(i * 256, 256), 256)
        ffn[rows] = dot_nt(act[rows], wf[2]).astype(BF)
        return carry

    lax.fori_loop(0, 2, down_rows, 0)
    sum_f.begin()
    gain_two[...] = jnp.zeros_like(gain_two)

    def backward_rows(i, carry):
        @pl.when(i == 1)
        def _():
            sum_f.relay()

        rows = pl.ds(pl.multiple_of(i * 256, 256), 256)
        ct = cot[rows]
        g, u = gate[rows], up[rows]
        sig = jax.nn.sigmoid(g)
        grad_act = dot(ct, wf[2])
        gg = (grad_act * u * sig * (1.0 + g * (1.0 - sig))).astype(BF)
        gu = (grad_act * g * sig).astype(BF)
        grad_g[rows] = gg
        grad_u[rows] = gu
        back = dot_nt(gg, wf[0]) + dot_nt(gu, wf[1])
        hat = low[rows].astype(F32)
        both = back * hat
        gain_two[...] += jnp.sum(both, axis=0, keepdims=True)
        pull = jnp.mean(both, axis=-1, keepdims=True)
        part = (ct.astype(F32) * 0.125 + inv[rows][:, 0:1] * (back - hat * pull)).astype(BF)
        share_ref[rows] = part
        u_ref[:, rows] = dot_nt(wo[...], part).astype(BF)
        return carry

    lax.fori_loop(0, 2, backward_rows, 0)
    for k in range(7, 10):
        emits[k].start()
    mid_own[...] = mid[pl.ds(pl.multiple_of(me.t * 64, 64), 64)]
    sum_f.columns(col_sum)
    for k in range(10):
        emits[k].wait()
    keys.sent()
    sum_f.sent()
    for s in share:
        s.sent()
    for slot in range(4):
        store(0, 0, slot).wait()


def forward_part(*operands):
    tokens = 512
    kept = [
        ((1536, 384), BF),
        ((16 * tokens, 128), BF),
        ((128, 3 * tokens), BF),
        ((384, tokens), F32),
        ((tokens, 1536), BF),
        ((tokens, 1536), BF),
        ((tokens, 896), BF),
        ((tokens, 896), BF),
        ((tokens, 896), BF),
        ((tokens, 1536), BF),
    ]
    shapes = [jax.ShapeDtypeStruct(*k) for k in kept] + [
        jax.ShapeDtypeStruct((8, 3 * tokens), F32),
        jax.ShapeDtypeStruct((192, tokens), BF),
        jax.ShapeDtypeStruct((1536, tokens), BF),
        jax.ShapeDtypeStruct((64, 1536), F32),
        jax.ShapeDtypeStruct((2, 64, 1536), BF),
        jax.ShapeDtypeStruct((1, 1536), F32),
        jax.ShapeDtypeStruct((8, 3, 1024, tokens), BF),
    ]
    scratch = [
        *[pltpu.VMEM(*k) for k in kept],
        pltpu.VMEM((1536, 256), BF),
        pltpu.VMEM((3, 1536, 896), BF),
        pltpu.VMEM((1536, 1536), BF),
        pltpu.VMEM((1536, tokens), BF),
        pltpu.VMEM((3, 80, tokens), F32),
        pltpu.VMEM((4, 1024, tokens), BF),
        pltpu.VMEM((tokens, 1536), F32),
        pltpu.VMEM((tokens, 128), F32),
        pltpu.VMEM((tokens, 896), F32),
        pltpu.VMEM((tokens, 896), F32),
        pltpu.VMEM((tokens, 1536), BF),
        *[DMA((17,))] * 4,
        *[DMA((3, 17))] * 2,
        *[DMA((17,))] * 4,
        *[DMA((3, 9))] * 2,
        DMA((5,)),
        DMA((4,)),
        DMA((10,)),
        *ring_scratch(32, 1536),
    ]
    return pl.pallas_call(
        forward_kernel,
        out_shape=shapes,
        in_specs=[SM] + [VM] * 7,
        out_specs=[HB] * 10 + [VM] * 6 + [HB],
        scratch_shapes=scratch,
        name="forward_part",
        compiler_params=pltpu.CompilerParams(
            collective_id=0, has_side_effects=True, vmem_limit_bytes=59 << 20
        ),
    )(*operands)


def backward_kernel(
    wq_in, kv_in, qt_in, raw_in, normed_in, low, act, grad_g, grad_u, share_in,
    sums, att_own, u_ref, mid_own, col_sum, gain_two, p_all, cot, x_in, cos_ref, sin_ref,
    blk, gin, own_q, own_w, gains,
    wq, kv, qt, raw, share_ref, x_ref, col_z,
    mid_rows, branch, gt, drift, dq, gk, gk_sib, wg, sib_w, pw, sib_p, po, sib_o, back, pre, extra,
    s_blk, r_blk, s_br, r_br, s_in, r_in, s_ex, r_ex, s_sib, r_sib, s_loc, s_p,
    *rest,
):
    me = Place()
    cn = ctx_neighbours(me)
    tn = tp_neighbours(me)
    sib = cn[3]
    tokens = 512
    scratch = [rest[8 * k : 8 * k + 8] for k in range(9)]
    crossing = tp_cross(me)
    greet([*cn, *tn, *crossing, (me.c, me.tp(0, 2)), (me.c, me.tp(1, 2))])

    def tp_block(k):
        return me.tp(*SLOTS[k])

    def chip(k):
        dz, dx = SLOTS[k]
        return me.ctx(dz, dx) // 2

    def rows_of(ref, size):
        def src(k, part):
            start = pl.multiple_of(tp_block(k) * size, size) + part * (size // 2)
            return ref.at[pl.ds(pl.multiple_of(start, size // 2), size // 2)]

        return src

    sum_u = ring(rows_of(u_ref, 192), 96, scratch[0], tn, True, crossing)
    sum_two = ring(rows_of(share_ref, 64), 32, scratch[1], tn, True, crossing)
    sum_b = ring(rows_of(back, 64), 32, scratch[2], tn, False, crossing)
    sum_kv = ring(
        lambda k, part: gk.at[k, me.core, pl.ds(64 * part, 64)], 64, scratch[3], cn
    )
    sum_w = [
        ring(
            lambda k, part, p=p: wg.at[p, chip(k), me.core, pl.ds(48 * part, 48)],
            48,
            scratch[4 + p],
            cn,
        )
        for p in range(3)
    ]
    sum_q = ring(
        lambda k, part: pw.at[chip(k), me.core, pl.ds(48 * part, 48)], 48, scratch[7], cn
    )
    sum_o = ring(
        lambda k, part: po.at[chip(k), me.core, pl.ds(48 * part, 48)], 48, scratch[8], cn
    )
    put_two = Gather(blk, 64, me.tp, *tn, None, s_blk, r_blk, over=True)
    put_br = Gather(branch, 64, me.tp, *tn, None, s_br, r_br)
    put_in = Gather(gin, 64, me.tp, *tn, None, s_in, r_in)
    others = [(dz, dy) for dz in (0, 1) for dy in range(4) if (dz, dy) != (0, 0)]
    put_ex = [
        pltpu.make_async_remote_copy(
            src_ref=extra.at[0],
            dst_ref=extra.at[1 + k],
            send_sem=s_ex.at[k],
            recv_sem=r_ex.at[k],
            device_id=(me.c, me.tp(*o)),
            device_id_type=MESH,
        )
        for k, o in enumerate(others)
    ]

    def to_sibling(k, here, there):
        return pltpu.make_async_remote_copy(
            src_ref=here,
            dst_ref=there,
            send_sem=s_sib.at[k],
            recv_sem=r_sib.at[k],
            device_id=sib,
            device_id_type=MESH,
        )

    def key_swap(k):
        return to_sibling(k, gk.at[k, 1 - me.core], gk_sib.at[k])

    swap_w = [to_sibling(8 + p, wg.at[p, :, 1 - me.core], sib_w.at[p]) for p in range(3)]
    swap_p = to_sibling(11, pw.at[:, 1 - me.core], sib_p)
    swap_o = to_sibling(13, po.at[:, 1 - me.core], sib_o)
    cross = pltpu.make_async_remote_copy(
        src_ref=col_sum.at[1],
        dst_ref=col_z,
        send_sem=s_sib.at[12],
        recv_sem=r_sib.at[12],
        device_id=tn[0],
        device_id_type=MESH,
    )
    takes = [
        pltpu.make_async_copy(h, v, s_loc.at[14 + k])
        for k, (h, v) in enumerate(
            [
                (wq_in, wq),
                (kv_in, kv),
                (qt_in, qt),
                (raw_in, raw),
                (share_in, share_ref),
                (x_in.at[pl.ds(pl.multiple_of(me.t * 64, 64), 64)], x_ref),
            ]
        )
    ]

    sum_u.begin()
    cross.start()

    def weight_grads(b_low, b_cot, b_one, b_two):
        def load(k, here, there):
            return pltpu.make_async_copy(here, there, s_loc.at[k])

        loads = [load(0, low, b_low), load(1, grad_g, b_one), load(2, grad_u, b_two)]
        loads += [load(3, cot, b_cot), load(4, act, b_one)]
        for k in loads[0:4] + takes:
            k.start()
        loads[0].wait()
        for p, (left, right) in enumerate([(b_low, b_one), (b_low, b_two), (b_cot, b_one)]):
            loads[(1, 2, 4)[p]].wait()
            if p == 2:
                loads[3].wait()

            def chunk(i, carry, p=p, left=left, right=right):
                at = pl.ds(pl.multiple_of(384 * i, 384), 384)
                whole = dot(left[:, at].T, right[...]).astype(BF)
                for q in range(4):
                    wg[p, 2 * i + q // 2, q % 2] = whole[96 * q : 96 * q + 96]
                return carry

            lax.fori_loop(0, 4, chunk, 0)
            swap_w[p].start()
            if p == 0:
                loads[4].start()
                sum_u.relay()

    pl.run_scoped(
        weight_grads,
        pltpu.VMEM((tokens, 1536), BF),
        pltpu.VMEM((tokens, 1536), BF),
        pltpu.VMEM((tokens, 896), BF),
        pltpu.VMEM((tokens, 896), BF),
    )

    def join_w(p):
        swap_w[p].wait_recv()

        def one(j, carry):
            add_into(wg.at[p, j, me.core], wg.at[p, j, me.core], sib_w.at[p, j])
            return carry

        lax.fori_loop(0, 8, one, 0)

    join_w(0)
    sum_w[0].begin()
    for k in takes:
        k.wait()
    grad_att = jnp.concatenate([sum_u.finish(0), sum_u.finish(1)], axis=0)
    own = pl.multiple_of(me.t * 64, 64)
    cross.wait_recv()
    blk[pl.ds(own, 64)] = (
        mid_own[...] + col_sum[0].astype(F32) + col_z[...].astype(F32)
    ).astype(BF)
    sum_two.begin()
    put_two.begin()
    gt[0:64] = jnp.zeros((64, 3 * tokens), BF)
    for h in range(3):
        cols = slice(h * tokens, (h + 1) * tokens)
        grad = grad_att[64 * h : 64 * h + 64]
        inverse = 1.0 / sums[0:1, cols]
        gt[64:128, cols] = (grad * inverse).astype(BF)
        drift[0:1, cols] = (
            jnp.sum(grad * att_own[64 * h : 64 * h + 64].astype(F32), axis=0, keepdims=True)
            * inverse
        )
    dq[...] = jnp.zeros_like(dq)

    def join_keys(k):
        key_swap(k).wait_recv()
        add_into(gk.at[k, me.core], gk.at[k, me.core], gk_sib.at[k])

    def key_loop(pbuf):
        def load(step, h):
            return pltpu.make_async_copy(
                p_all.at[chip_of(me, step, SLOTS), h], pbuf.at[h], s_p.at[h]
            )

        for h in range(3):
            load(0, h).start()

        def key_step(step, carry):
            @pl.when(step == 1)
            def _():
                join_keys(0)
                sum_kv.go(0, 1)
                sum_two.relay()
                sum_w[0].relay()
                join_w(1)
                sum_w[1].begin()

            @pl.when(step == 2)
            def _():
                join_keys(1)
                sum_kv.go(2, 3)
                put_two.near()

            @pl.when(step == 3)
            def _():
                join_keys(2)
                sum_kv.go(4)
                sum_kv.relay_right(1)
                branch_rows = jnp.concatenate([sum_two.finish(0), sum_two.finish(1)], axis=0)
                mid_rows[...] = branch_rows
                branch[pl.ds(own, 64)] = branch_rows.astype(BF)
                put_br.begin()
                sum_w[0].column()
                sum_w[1].relay()
                join_w(2)
                sum_w[2].begin()

            @pl.when(step == 4)
            def _():
                join_keys(3)
                sum_kv.go(5)
                sum_kv.relay_left(1)
                put_two.far()

            @pl.when(step == 5)
            def _():
                join_keys(4)
                sum_kv.go(6)
                sum_kv.relay_right(0)
                sum_w[1].column()
                put_two.pair()
                put_br.near()
                put_br.pair()

            @pl.when(step == 6)
            def _():
                join_keys(5)
                sum_kv.go(7)
                sum_kv.relay_left(0)
                put_br.far()
                put_two.last()
                sum_w[2].relay()

            @pl.when(step == 7)
            def _():
                join_keys(6)
                sum_kv.column()
                put_br.last()

            place = chip_of(me, step, SLOTS)
            rows = kv[pl.ds(pl.multiple_of(place * 1024, 1024), 1024), :]
            key_t = rows.T[0:64]
            key_grad = value_grad = 0.0
            for h in range(3):
                cols = slice(h * tokens, (h + 1) * tokens)
                slopes = dot(rows, gt[:, cols])
                load(step, h).wait()
                weight = pbuf[h]
                grad = (weight.astype(F32) * (slopes - drift[0:1, cols])).astype(BF)
                dq[:, cols] += dot(key_t, grad)
                key_grad += dot_nt(qt[0:64, cols], grad)
                value_grad += dot_nt(gt[64:128, cols], weight)

                @pl.when(step < 7)
                def _(h=h):
                    load(step + 1, h).start()

            both = jnp.concatenate([key_grad * LN2, value_grad], axis=0).astype(BF)
            gk[step, 0] = both[:, 0:512]
            gk[step, 1] = both[:, 512:1024]
            key_swap(step).start()
            return carry

        lax.fori_loop(0, 8, key_step, 0)

    pl.run_scoped(key_loop, pltpu.VMEM((3, 1024, tokens), BF))
    def finale(normed):
        fetch = pltpu.make_async_copy(normed_in, normed, s_loc.at[5])
        fetch.start()
        att_n = jnp.concatenate(
            [att_own[...].astype(F32), jnp.zeros((64, tokens), F32)], axis=0
        ).T.astype(BF)
        for i in range(4):
            at = slice(384 * i, 384 * i + 384)
            whole = dot(branch[:, at].T, att_n).astype(BF)
            for q in range(4):
                po[2 * i + q // 2, q % 2] = whole[96 * q : 96 * q + 96]
        swap_o.start()
        query_gain, key_gain = gain_columns(wq)
        cosine, sine = cos_ref[...], sin_ref[...]

        def unturn(grad, value, gain):
            inverse = column_inverse(value)
            hat = value * inverse
            a, b = grad[:32], grad[32:]
            plain = jnp.concatenate([a * cosine + b * sine, b * cosine - a * sine], axis=0)
            gain_grad = jnp.sum(plain * hat, axis=1, keepdims=True)
            pulled = plain * gain
            back_grad = inverse * (pulled - hat * jnp.mean(pulled * hat, axis=0, keepdims=True))
            return gain_grad, back_grad

        query_gain_grad = 0.0
        for h in range(3):
            part, grad = unturn(
                dq[:, h * tokens : (h + 1) * tokens] * 0.125, raw[64 * h : 64 * h + 64], query_gain
            )
            query_gain_grad += part
            pre[64 * h : 64 * h + 64] = grad
        join_keys(7)
        key_grad, value_grad = sum_kv.finish(0), sum_kv.finish(1)
        key_gain_grad, grad = unturn(key_grad, raw[192:256], key_gain)
        pre[192:256] = grad
        pre[256:320] = value_grad
        pre[320:384] = jnp.zeros((64, tokens), F32)
        pre_n = pre[...].T.astype(BF)
        for i in range(2):
            rows = slice(256 * i, 256 * i + 256)
            back[rows] = dot_nt(pre_n[rows], wq[...]).astype(BF)
        sum_b.begin()
        fetch.wait()
        gain_one = 0.0
        for i in range(4):
            rows = slice(128 * i, 128 * i + 128)
            gain_one += jnp.sum(
                back[rows].astype(F32) * normed[rows].astype(F32), axis=0, keepdims=True
            )
        sum_w[2].column()
        swap_o.wait_recv()

        def join_o(j, carry):
            add_into(po.at[j, me.core], po.at[j, me.core], sib_o.at[j])
            return carry

        lax.fori_loop(0, 8, join_o, 0)
        sum_o.begin()
        lane = lax.broadcasted_iota(jnp.int32, (64, 1536), 1)
        unit = lax.broadcasted_iota(jnp.int32, (64, 1536), 0)
        spot = lane == (unit // 4) * 96 + lax.rem(unit, 4)

        def spread(column):
            return jnp.sum(jnp.where(spot, column, 0.0), axis=0, keepdims=True)

        lines = jnp.concatenate(
            [
                jnp.zeros((64, 1536), F32),
                gain_one,
                gain_two[...],
                spread(query_gain_grad),
                spread(key_gain_grad),
                jnp.zeros((60, 1536), F32),
            ],
            axis=0,
        )
        sides = lines.T
        sum_b.relay()
        for i in range(4):
            at = slice(384 * i, 384 * i + 384)
            part = dot(normed[:, at].T, pre_n)
            whole = jnp.concatenate([part[:, 0:256], part[:, 256:384] + sides[at]], axis=1).astype(BF)
            for q in range(4):
                pw[2 * i + q // 2, q % 2] = whole[96 * q : 96 * q + 96]
        swap_p.start()
        sum_o.relay()
        swap_p.wait_recv()

        def join_p(j, carry):
            add_into(pw.at[j, me.core], pw.at[j, me.core], sib_p.at[j])
            return carry

        lax.fori_loop(0, 8, join_p, 0)
        sum_q.begin()
        value = x_ref[...].astype(F32)
        inverse = rms_inverse(value)
        hat = value * inverse
        back_one = jnp.concatenate([sum_b.finish(0), sum_b.finish(1)], axis=0)
        gin[pl.ds(own, 64)] = (
            mid_rows[...]
            + inverse * (back_one - hat * jnp.mean(back_one * hat, axis=-1, keepdims=True))
        ).astype(BF)
        put_in.begin()
        for p in range(3):
            for half in range(2):
                own_w[p, 48 * half : 48 * half + 48] = sum_w[p].finish(half)
        put_in.near()
        sum_q.relay()
        sum_o.column()
        put_in.pair()
        sum_q.column()
        put_in.far()
        for half in range(2):
            own_q[48 * half : 48 * half + 48, 0:384] = sum_q.finish(half)
        extra[0] = own_q[:, 256:384].T[64:72]
        for p in put_ex:
            p.start()
        for half in range(2):
            own_q[48 * half : 48 * half + 48, 384:640] = sum_o.finish(half)
        put_in.last()
        for p in put_ex:
            p.wait()
        total = extra[0]
        for b in range(1, 8):
            total += extra[b]
        gains[...] = total
        for s in [sum_u, sum_two, sum_b, sum_kv, sum_q, sum_o, *sum_w, put_two, put_br, put_in]:
            s.sent()
        for k in range(8):
            key_swap(k).wait_send()
        for s in [*swap_w, swap_p, swap_o, cross]:
            s.wait_send()

    pl.run_scoped(finale, pltpu.VMEM((tokens, 1536), BF))


def backward_part(*operands):
    tokens = 512
    shapes = [
        jax.ShapeDtypeStruct((512, 1536), BF),
        jax.ShapeDtypeStruct((512, 1536), BF),
        jax.ShapeDtypeStruct((96, 640), F32),
        jax.ShapeDtypeStruct((3, 96, 896), F32),
        jax.ShapeDtypeStruct((8, 96), F32),
    ]
    scratch = [
        pltpu.VMEM((1536, 384), BF),
        pltpu.VMEM((16 * tokens, 128), BF),
        pltpu.VMEM((128, 3 * tokens), BF),
        pltpu.VMEM((384, tokens), F32),
        pltpu.VMEM((tokens, 1536), BF),
        pltpu.VMEM((64, 1536), BF),
        pltpu.VMEM((64, 1536), BF),
        pltpu.VMEM((64, 1536), F32),
        pltpu.VMEM((tokens, 1536), BF),
        pltpu.VMEM((128, 3 * tokens), BF),
        pltpu.VMEM((8, 3 * tokens), F32),
        pltpu.VMEM((64, 3 * tokens), F32),
        pltpu.VMEM((8, 2, 128, 512), BF),
        pltpu.VMEM((8, 128, 512), BF),
        pltpu.VMEM((3, 8, 2, 96, 896), BF),
        pltpu.VMEM((3, 8, 96, 896), BF),
        pltpu.VMEM((8, 2, 96, 384), BF),
        pltpu.VMEM((8, 96, 384), BF),
        pltpu.VMEM((8, 2, 96, 256), BF),
        pltpu.VMEM((8, 96, 256), BF),
        pltpu.VMEM((tokens, 1536), BF),
        pltpu.VMEM((384, tokens), F32),
        pltpu.VMEM((8, 8, 96), F32),
        *[DMA((9,))] * 8,
        DMA((14,)),
        DMA((14,)),
        DMA((21,)),
        DMA((3,)),
        *ring_scratch(96, 512, True),
        *ring_scratch(32, 1536, True),
        *ring_scratch(32, 1536),
        *ring_scratch(64, 512),
        *ring_scratch(48, 896) * 3,
        *ring_scratch(48, 384),
        *ring_scratch(48, 256),
    ]
    return pl.pallas_call(
        backward_kernel,
        out_shape=shapes,
        in_specs=[HB] * 10 + [VM] * 6 + [HB] * 3 + [VM] * 2,
        out_specs=[VM] * 5,
        scratch_shapes=scratch,
        name="backward_part",
        compiler_params=pltpu.CompilerParams(
            collective_id=1, has_side_effects=True, vmem_limit_bytes=59 << 20
        ),
    )(*operands)


FREQ = [[THETA ** (-2.0 * i / HD)] * 128 for i in range(HD // 2)]


def body(
    block_input, positions, attn_gain, query_weight, key_weight, value_weight, query_gain,
    key_gain, output_weight, ffn_gain, gate_weight, up_weight, down_weight, out_cotangent,
):
    def line(gain):
        return gain.reshape(1, -1)

    wq_s, wo_s, wf_s, cosine, sine = prepare(
        line(positions), line(attn_gain), line(ffn_gain), line(query_gain), line(key_gain),
        jnp.array(FREQ, F32), query_weight, key_weight.T, value_weight.T, output_weight,
        gate_weight, up_weight, down_weight.T,
    )
    results = forward_part(positions, block_input, out_cotangent, wq_s, wo_s, wf_s, cosine, sine)
    results = backward_part(*results, out_cotangent, block_input, cosine, sine)
    return conclude(line(attn_gain), line(ffn_gain), *results)


def solution(mesh):
    in_specs = (
        P("ctx", None),
        P(),
        P("ctx"),
        P("ctx", "tp"),
        P("ctx", "tp"),
        P("ctx", "tp"),
        P("ctx"),
        P("ctx"),
        P("tp", "ctx"),
        P("ctx"),
        P("ctx", "tp"),
        P("ctx", "tp"),
        P("tp", "ctx"),
        P("ctx", None),
    )
    out_specs = (
        P("ctx", None),
        P("ctx", None),
        P("ctx"),
        P("ctx", "tp"),
        P("ctx", "tp"),
        P("ctx", "tp"),
        P("ctx"),
        P("ctx"),
        P("tp", "ctx"),
        P("ctx"),
        P("ctx", "tp"),
        P("ctx", "tp"),
        P("tp", "ctx"),
    )
    return jax.shard_map(body, mesh=mesh, in_specs=in_specs, out_specs=out_specs, check_vma=False)
```

```python
import functools
import math

import jax
import jax.numpy as jnp
from jax import lax
from jax.experimental import pallas as pl
from jax.experimental.pallas import tpu as pltpu
from jax.sharding import PartitionSpec as P

HD = 64
EPS = 1e-05
THETA = 1000000.0
LOG2E = math.log2(math.e)
LN2 = math.log(2.0)
BF = jnp.bfloat16
F32 = jnp.float32
MESH = pl.DeviceIdType.MESH
VM = pl.BlockSpec(memory_space=pltpu.VMEM)
SM = pl.BlockSpec(memory_space=pltpu.SMEM)
HB = pl.BlockSpec(memory_space=pl.ANY)
DMA = pltpu.SemaphoreType.DMA


class Place:
    def __init__(self):
        self.c = lax.axis_index("ctx")
        self.t = lax.axis_index("tp")
        self.core = lax.rem(self.c, 2)
        self.x = lax.rem(self.c // 2, 4)
        self.zh = self.c // 8
        self.y = lax.rem(self.t, 4)
        self.zl = self.t // 4

    def ctx(self, dz, dx, other=0):
        core = self.core if not other else 1 - self.core
        zh = self.zh if not dz else 1 - self.zh
        return (zh * 4 + lax.rem(self.x + dx, 4)) * 2 + core

    def tp(self, dz, dy):
        zl = self.zl if not dz else 1 - self.zl
        return zl * 4 + lax.rem(self.y + dy, 4)


def greet(peers):
    barrier = pltpu.get_barrier_semaphore()
    for peer in peers:
        pl.semaphore_signal(barrier, inc=1, device_id=peer, device_id_type=MESH)
    pl.semaphore_wait(barrier, len(peers))


class Gather:
    def __init__(self, buf, rows, block, pair, right, left, sibling, send, recv, own=None, cross=(), over=False):
        self.buf, self.rows, self.block = buf, rows, block
        self.to = {"z": pair, "r": right, "l": left, "s": sibling}
        self.cross = len(cross) > 0
        if self.cross:
            self.to["zr"], self.to["zl"] = cross
        self.send, self.recv, self.own = send, recv, own
        self.plan = {
            0: ((0, 0), 0, "z"),
            1: ((0, 0), 0, "r"),
            2: ((0, 0), 0, "l"),
            3: ((0, 3), 1, "r"),
            4: ((0, 1), 2, "l"),
            5: ((1, 0), 0, "r"),
            6: ((1, 0), 0, "l"),
            7: ((1, 3), 1, "r"),
            8: ((1, 1), 2, "l"),
            9: ((0, 0), 0, "s"),
            10: ((1, 0), 0, "s"),
            11: ((0, 3), 0, "s"),
            12: ((0, 1), 0, "s"),
            13: ((0, 2), 0, "s"),
            14: ((1, 3), 0, "s"),
            15: ((1, 1), 0, "s"),
            16: ((1, 2), 0, "s"),
        }
        if self.cross:
            self.plan[5] = ((0, 0), 0, "zr")
            self.plan[6] = ((0, 0), 0, "zl")
        self.over = over
        if over:
            self.plan[5] = ((0, 3), 0, "z")
            self.plan[6] = ((0, 1), 0, "z")
            self.plan[7] = ((0, 2), 1, "z")
            self.plan[8] = ((0, 2), 2, "z")
        self.count = 17 if sibling is not None else 9

    def copy(self, k):
        where, part, to = self.plan[k]
        rows = self.rows if part == 0 else self.rows // 2
        start = pl.multiple_of(self.block(*where) * self.rows, self.rows)
        if part == 2:
            start = pl.multiple_of(start + rows, rows)
        there = self.buf.at[pl.ds(start, rows)]
        here = there
        if where == (0, 0) and self.own is not None:
            here = self.own
        return pltpu.make_async_remote_copy(
            src_ref=here,
            dst_ref=there,
            send_sem=self.send.at[k],
            recv_sem=self.recv.at[k],
            device_id=self.to[to],
            device_id_type=MESH,
        )

    def go(self, *which):
        for k in which:
            if k < self.count:
                self.copy(k).start()

    def got(self, *which):
        for k in which:
            if k < self.count:
                self.copy(k).wait_recv()

    def begin(self):
        self.go(0, 1, 2, 9)
        if self.cross:
            self.go(5, 6)

    def near(self):
        self.got(1)
        self.go(3, 11)
        if self.over:
            self.go(5)
        self.got(2)
        self.go(4, 12)
        if self.over:
            self.go(6)

    def pair(self):
        self.got(0)
        if not self.cross and not self.over:
            self.go(5, 6)
        self.go(10)

    def far(self):
        if self.over:
            self.got(3)
            self.go(7)
            self.got(4)
            self.go(8)
            self.got(5, 6)
            return
        self.got(5)
        self.go(7, 14)
        self.got(6)
        self.go(8, 15)
        self.got(3, 4)
        self.go(13)

    def last(self):
        self.got(7, 8)
        self.go(16)

    def sent(self):
        for k in range(self.count):
            self.copy(k).wait_send()

    def end(self):
        self.got(*range(9, 17))
        self.sent()


def ctx_neighbours(me):
    return (
        (me.ctx(1, 0), me.t),
        (me.ctx(0, 1), me.t),
        (me.ctx(0, 3), me.t),
        (me.ctx(0, 0, 1), me.t),
    )


def tp_neighbours(me):
    return (me.c, me.tp(1, 0)), (me.c, me.tp(0, 1)), (me.c, me.tp(0, 3))


def tp_cross(me):
    return (me.c, me.tp(1, 1)), (me.c, me.tp(1, 3))


def rms_inverse(value):
    return lax.rsqrt(jnp.mean(value * value, axis=-1, keepdims=True) + EPS)


def column_inverse(value):
    return lax.rsqrt(jnp.mean(value * value, axis=0, keepdims=True) + EPS)


def gain_columns(wq):
    total = wq[0:64, 256:384].astype(F32)
    for k in range(1, 16):
        total += wq[96 * k : 96 * k + 64, 256:384].astype(F32)
    return total[:, 64:65], total[:, 65:66]


def dot(a, b):
    return jnp.dot(a, b, preferred_element_type=F32)


def dot_nt(a, b):
    return lax.dot_general(a, b, (((1,), (1,)), ((), ())), preferred_element_type=F32)


def dot_tn(a, b):
    return lax.dot_general(a, b, (((0,), (0,)), ((), ())), preferred_element_type=F32)


PAIRS = ((0, 0), (0, 3), (0, 1), (1, 0), (0, 2), (1, 3), (1, 1), (1, 2))


def chip_of(me, step, order):
    dz = sum(jnp.where(step == k, p[0], 0) for k, p in enumerate(order) if p[0])
    dx = sum(jnp.where(step == k, p[1], 0) for k, p in enumerate(order) if p[1])
    return lax.rem(me.zh + dz, 2) * 4 + lax.rem(me.x + dx, 4)


SLOTS = ((1, 2), (0, 2), (1, 1), (1, 3), (0, 1), (0, 3), (1, 0), (0, 0))


def add_into(out, *terms):
    total = terms[0][...].astype(F32)
    for term in terms[1:]:
        total += term[...].astype(F32)
    out[...] = total.astype(out.dtype)


class RingSum:
    def __init__(self, src, half, stage, rel_l, rel_r, col_l, col_r, from_z, pair, right, left, send, recv, cross=()):
        self.src, self.half = src, half
        at_stage = {2: (0, 0), 3: (0, 1), 4: (1, 0), 5: (1, 1)}

        def put(k, part):
            if stage is None:
                return src(k, part)
            rows = pl.ds(part * half, half)
            return stage.at[2 if k == 6 else at_stage[k][0], rows]

        self.put = put
        self.rel_l, self.rel_r, self.col_l, self.col_r, self.from_z = rel_l, rel_r, col_l, col_r, from_z
        self.to = {"z": pair, "r": right, "l": left, "zr": right, "zl": left}
        self.cross = len(cross) > 0
        if self.cross:
            self.to["zr"], self.to["zl"] = cross
        self.send, self.recv = send, recv
        low, high = pl.ds(0, half), pl.ds(half, half)
        self.low, self.high = low, high
        self.last = 14
        self.plan = [
            (src(0, 0), rel_l.at[1], "r"),
            (src(0, 1), rel_r.at[1], "l"),
            (src(1, 0), rel_l.at[0], "r"),
            (src(1, 1), rel_r.at[0], "l"),
            (src(2, 1), col_l.at[1, high], "zr"),
            (src(3, 0), col_r.at[1, low], "zl"),
            (src(4, 1), col_l.at[0, high], "r"),
            (src(5, 0), col_r.at[0, low], "l"),
            (put(2, 0), col_l.at[1, low], "zr"),
            (put(3, 1), col_r.at[1, high], "zl"),
            (put(4, 0), col_l.at[0, low], "r"),
            (put(5, 1), col_r.at[0, high], "l"),
            ((src if self.cross else put)(6, 0), from_z.at[low], "z"),
            ((src if self.cross else put)(6, 1), from_z.at[high], "z"),
        ]

    def copy(self, k):
        here, there, to = self.plan[k]
        return pltpu.make_async_remote_copy(
            src_ref=here,
            dst_ref=there,
            send_sem=self.send.at[k],
            recv_sem=self.recv.at[k],
            device_id=self.to[to],
            device_id_type=MESH,
        )

    def go(self, *which):
        for k in which:
            self.copy(k).start()

    def got(self, *which):
        for k in which:
            self.copy(k).wait_recv()

    def begin(self):
        self.go(*range(8))
        if self.cross:
            self.go(12, 13)

    def relay_right(self, plane):
        k = 2 if plane else 4
        self.got(0 if plane else 2)
        add_into(self.put(k, 0), self.src(k, 0), self.rel_l.at[plane])
        self.go(8 if plane else 10)

    def relay_left(self, plane):
        k = 3 if plane else 5
        self.got(1 if plane else 3)
        add_into(self.put(k, 1), self.src(k, 1), self.rel_r.at[plane])
        self.go(9 if plane else 11)

    def relay(self):
        for plane in (1, 0):
            self.relay_right(plane)
            self.relay_left(plane)

    def column(self):
        self.got(4, 8, 5, 9)
        for part, rows in enumerate((self.low, self.high)):
            add_into(
                self.put(6, part),
                self.src(6, part),
                self.col_l.at[1, rows],
                self.col_r.at[1, rows],
            )
            self.go(12 + part)

    def columns(self, out):
        self.last = 12
        self.got(4, 8, 5, 9, 6, 10, 7, 11)
        for plane, k in ((0, 7), (1, 6)):
            for part, rows in enumerate((self.low, self.high)):
                add_into(
                    out.at[plane, rows],
                    self.src(k, part),
                    self.col_l.at[plane, rows],
                    self.col_r.at[plane, rows],
                )

    def finish(self, part):
        if part == 0:
            self.got(6, 10, 7, 11, 12, 13)
            if self.cross:
                self.got(4, 8, 5, 9)
        rows = self.low if part == 0 else self.high
        total = self.src(7, part)[...].astype(F32)
        terms = [self.col_l.at[0, rows], self.col_r.at[0, rows], self.from_z.at[rows]]
        if self.cross:
            terms += [self.col_l.at[1, rows], self.col_r.at[1, rows]]
        for term in terms:
            total += term[...].astype(F32)
        return total

    def sent(self):
        for k in range(self.last):
            self.copy(k).wait_send()


def ring_scratch(half, width, stage=False):
    return [
        pltpu.VMEM((3, 2 * half, width) if stage else (1, 16, 128), BF),
        pltpu.VMEM((2, half, width), BF),
        pltpu.VMEM((2, half, width), BF),
        pltpu.VMEM((2, 2 * half, width), BF),
        pltpu.VMEM((2, 2 * half, width), BF),
        pltpu.VMEM((2 * half, width), BF),
        DMA((14,)),
        DMA((14,)),
    ]


def ring(src, half, scratch, neighbours, stage=False, cross=()):
    room, rel_l, rel_r, col_l, col_r, from_z, send, recv = scratch
    return RingSum(
        src, half, room if stage else None, rel_l, rel_r, col_l, col_r, from_z, *neighbours[:3],
        send, recv, cross,
    )


def gain_lines(lines, refs):
    lines[...] = jnp.zeros_like(lines)
    for k, ref in enumerate(refs):
        lines[k : k + 1, 0 : ref.shape[1]] = ref[...].astype(F32)
    columns = lines[...].T
    return columns[0:96, 0:1], columns[0:96, 1:2]


def prepare_kernel(
    places, attn_gain, ffn_gain, query_gain, key_gain, freq,
    query, key_t, value_t, output, gate, up, down_t, wq_s, wo_s, wf_s, cosine, sine, lines,
):
    c = lax.axis_index("ctx")
    gain_one, gain_two = gain_lines(lines, [attn_gain, ffn_gain, query_gain, key_gain])
    row = lax.broadcasted_iota(jnp.int32, (96, 64), 0)
    col = lax.broadcasted_iota(jnp.int32, (96, 64), 1)
    sides = jnp.zeros((96, 64), F32)
    for k in range(2):
        for j in range(4):
            at = (row == 4 * c + j) & (col == k)
            sides = jnp.where(at, lines[2 + k : 3 + k, j : j + 1], sides)

    def lifted(weight, gain):
        return (weight.astype(F32) * gain).astype(BF)

    both = jnp.concatenate([key_t[...].astype(F32), value_t[...].astype(F32)], axis=0).T
    wq_s[:, 0:192] = lifted(query[...], gain_one)
    wq_s[:, 192:320] = lifted(both, gain_one)
    wq_s[:, 320:384] = sides.astype(BF)
    wo_s[:, 192:256] = jnp.zeros((96, 64), BF)
    wo_s[:, 0:192] = output[...].astype(F32).T.astype(BF)
    for k in range(3):
        wf_s[:, 896 * k + 768 : 896 * k + 896] = jnp.zeros((96, 128), BF)
    wf_s[:, 0:864] = lifted(gate[...], gain_two)
    wf_s[:, 896:1760] = lifted(up[...], gain_two)
    wf_s[:, 1792:2656] = down_t[...]
    place = places[0:1, pl.ds(pl.multiple_of(c * 512, 512), 512)]
    angle = freq[:, 0:1] * place.astype(F32)
    cosine[...] = jnp.cos(angle)
    sine[...] = jnp.sin(angle)


def prepare(*operands):
    shapes = [
        jax.ShapeDtypeStruct((96, 384), BF),
        jax.ShapeDtypeStruct((96, 256), BF),
        jax.ShapeDtypeStruct((96, 2688), BF),
        jax.ShapeDtypeStruct((32, 512), F32),
        jax.ShapeDtypeStruct((32, 512), F32),
    ]
    return pl.pallas_call(
        prepare_kernel,
        out_shape=shapes,
        in_specs=[VM] * 13,
        out_specs=[VM] * 5,
        scratch_shapes=[pltpu.VMEM((8, 128), F32)],
        name="prepare",
        compiler_params=pltpu.CompilerParams(vmem_limit_bytes=59 << 20),
    )(*operands)


def conclude_kernel(
    attn_gain, ffn_gain, block, gin, own_q, own_w, side,
    block_output, grad_input, g_attn, g_query, g_key, g_value, g_qg, g_kg, g_out, g_ffn, g_gate, g_up, g_down,
    lines,
):
    gain_one, gain_two = gain_lines(lines, [attn_gain, ffn_gain])
    block_output[...] = block[...]
    grad_input[...] = gin[...].astype(F32)
    g_query[...] = own_q[:, 0:192] * gain_one
    both = (own_q[:, 192:320] * gain_one).T
    g_key[...] = both[0:64]
    g_value[...] = both[64:128]
    g_out[...] = own_q[:, 384:576].T
    g_gate[...] = own_w[0, :, 0:864] * gain_two
    g_up[...] = own_w[1, :, 0:864] * gain_two
    g_down[...] = own_w[2, :, 0:864]
    g_attn[...] = side[0:1, 0:96] / lines[0:1, 0:96]
    g_ffn[...] = side[1:2, 0:96] / lines[1:2, 0:96]
    g_qg[...] = side[2:3, 0:4]
    g_kg[...] = side[3:4, 0:4]


def conclude(*operands):
    dims = [
        ((512, 1536), BF), ((512, 1536), F32), ((1, 96), F32), ((96, 192), F32), ((64, 96), F32),
        ((64, 96), F32), ((1, 4), F32), ((1, 4), F32), ((192, 96), F32), ((1, 96), F32),
        ((96, 864), F32), ((96, 864), F32), ((96, 864), F32),
    ]
    results = pl.pallas_call(
        conclude_kernel,
        out_shape=[jax.ShapeDtypeStruct(*d) for d in dims],
        in_specs=[VM] * 7,
        out_specs=[VM] * 13,
        scratch_shapes=[pltpu.VMEM((8, 128), F32)],
        name="conclude",
        compiler_params=pltpu.CompilerParams(vmem_limit_bytes=59 << 20),
    )(*operands)
    results = [r.T if k in (4, 5, 12) else r for k, r in enumerate(results)]
    return tuple(r.reshape(-1) if r.shape[0] == 1 else r for r in results)


def forward_kernel(
    kb, x_ref, cot, wq_s, wo_s, wf_s, cos_ref, sin_ref,
    wq_out, kv_out, qt_out, raw_out, normed_out, low_out, act_out, g_out, u_out, share_out,
    sums, att_own, u_ref, mid_own, col_sum, gain_two, p_all,
    wq, kv, qt, raw, normed, low, act, grad_g, grad_u, share_ref,
    wo_t, wf, wo, att, acc, pbuf, mid, inv, gate, up, ffn,
    s_w, r_w, s_v, r_v, s_f, r_f, s_o, r_o, s_k, r_k, s_a, r_a, s_l, s_p, s_out,
    *rest,
):
    me = Place()
    cn = ctx_neighbours(me)
    tn = tp_neighbours(me)
    cross = tp_cross(me)
    tokens = x_ref.shape[0]
    greet([*cn, *tn, *cross])
    weights = Gather(wq, 96, me.ctx, *cn, s_w, r_w, own=wq_s)
    outs = Gather(wo_t, 96, me.ctx, *cn, s_v, r_v, own=wo_s)
    feed = [
        Gather(
            wf.at[p], 96, me.ctx, *cn, s_f.at[p], r_f.at[p], own=wf_s.at[:, 896 * p : 896 * p + 896]
        )
        for p in range(3)
    ]
    keys = Gather(kv, tokens, me.ctx, *cn, s_k, r_k)
    outw = Gather(
        wo, 96, lambda dz, dy: me.tp(dz, dy) * 2 + me.core, *tn, cn[3], s_o, r_o
    )
    share = [
        Gather(
            att, 64, lambda dz, dy, h=h: me.tp(dz, dy) * 3 + h, *tn, None, s_a.at[h], r_a.at[h],
            cross=cross,
        )
        for h in range(3)
    ]
    sum_f = ring(
        lambda k, part: ffn.at[
            pl.ds(pl.multiple_of(me.tp(*SLOTS[k]) * 64 + 32 * part, 32), 32)
        ],
        32, rest, tn,
    )

    weights.begin()
    outs.begin()
    feed[0].go(1, 2, 9)
    mine = pl.ds(pl.multiple_of(me.c * 96, 96), 96)
    keep = [
        pltpu.make_async_copy(wq_s, wq.at[mine], s_l.at[0]),
        pltpu.make_async_copy(wo_s, wo_t.at[mine], s_l.at[1]),
    ] + [
        pltpu.make_async_copy(wf_s.at[:, 896 * p : 896 * p + 896], wf.at[p, mine], s_l.at[2 + p])
        for p in range(3)
    ]
    for k in keep:
        k.start()
    emits = [
        pltpu.make_async_copy(v, h, s_out.at[k])
        for k, (v, h) in enumerate(
            [
                (wq, wq_out),
                (kv, kv_out),
                (qt, qt_out),
                (raw, raw_out),
                (normed, normed_out),
                (low, low_out),
                (act, act_out),
                (grad_g, g_out),
                (grad_u, u_out),
                (share_ref, share_out),
            ]
        )
    ]

    def norm_rows(i, carry):
        rows = pl.ds(pl.multiple_of(i * 64, 64), 64)
        value = x_ref[rows].astype(F32)
        normed[rows] = (value * rms_inverse(value)).astype(BF)
        return carry

    lax.fori_loop(0, tokens // 64, norm_rows, 0)
    weights.near()
    weights.pair()
    feed[0].go(0)
    outs.near()
    outs.pair()
    emits[4].start()
    weights.far()
    weights.last()
    outs.far()
    outs.last()
    keep[1].wait()
    outs.end()
    heads = wo_t[...].T
    wo[pl.ds(pl.multiple_of(me.t * 192 + me.core * 96, 96), 96)] = jnp.where(
        me.core == 0, heads[0:96], heads[96:192]
    )
    outw.begin()
    keep[0].wait()
    weights.end()
    feed[1].go(1, 2, 9)
    emits[0].start()

    def project(i, carry):
        cols = pl.ds(pl.multiple_of(i * 256, 256), 256)
        raw[:, cols] = dot(normed[cols], wq[...]).T
        return carry

    lax.fori_loop(0, tokens // 256, project, 0)
    emits[3].start()
    feed[0].near()
    query_gain, key_gain = gain_columns(wq)
    cosine, sine = cos_ref[...], sin_ref[...]

    def turned(value, gain):
        hat = value * column_inverse(value) * gain
        a, b = hat[:32], hat[32:]
        return jnp.concatenate([a * cosine - b * sine, b * cosine + a * sine], axis=0)

    both = jnp.concatenate([turned(raw[192:256], key_gain), raw[256:320]], axis=0)
    kv[pl.ds(pl.multiple_of(me.c * tokens, tokens), tokens)] = both.T.astype(BF)
    keys.begin()
    qt[64:128] = jnp.zeros((64, 3 * tokens), BF)
    for h in range(3):
        qt[0:64, h * tokens : (h + 1) * tokens] = (
            turned(raw[64 * h : 64 * h + 64], query_gain) * (LOG2E / 8.0)
        ).astype(BF)
    emits[2].start()
    feed[0].pair()
    outw.near()
    acc[...] = jnp.zeros_like(acc)
    ones = jnp.concatenate([jnp.ones((1, 1024), BF), jnp.zeros((15, 1024), BF)], axis=0)
    apart = lax.broadcasted_iota(jnp.int32, (256, 256), 0) - lax.broadcasted_iota(
        jnp.int32, (256, 256), 1
    )

    def attend(h, place, slot):
        rows = kv[pl.ds(pl.multiple_of(place * 1024, 1024), 1024), :]
        scores = dot(rows, qt[:, pl.ds(pl.multiple_of(h * tokens, tokens), tokens)])
        parts = []
        for a in range(4):
            line = []
            for b in range(2):
                sub = scores[a * 256 : a * 256 + 256, b * 256 : b * 256 + 256]
                seen = apart <= kb[me.c * 512 + b * 256] - kb[place * 1024 + a * 256]
                line.append(jnp.where(seen, jnp.exp2(sub), 0.0).astype(BF))
            parts.append(jnp.concatenate(line, axis=1))
        weight = jnp.concatenate(parts, axis=0)
        pbuf[slot] = weight
        left = jnp.concatenate([rows.T[64:128], ones], axis=0)
        return dot(left, weight)

    def store(h, place, slot):
        return pltpu.make_async_copy(pbuf.at[slot], p_all.at[place, h], s_p.at[slot])

    def close(h):
        total = acc[h, 64:65]
        sums[0:1, h * tokens : (h + 1) * tokens] = total
        value = (acc[h, 0:64] / total).astype(BF)
        att_own[64 * h : 64 * h + 64] = value
        att[pl.ds(pl.multiple_of(me.t * 192 + 64 * h, 64), 64)] = value
        share[h].begin()

    def task(h, step, slot):
        place = chip_of(me, step, PAIRS)
        acc[h] += attend(h, place, slot)
        store(h, place, slot).start()

    def arriving(step, carry):
        @pl.when(step == 0)
        def _():
            keys.got(9)

        @pl.when(step == 1)
        def _():
            keys.near()
            feed[1].go(0)
            outw.pair()
            keys.got(11)

        @pl.when(step == 2)
        def _():
            keys.pair()
            feed[1].near()
            feed[2].go(0)
            keys.got(12)

        @pl.when(step == 3)
        def _():
            keys.got(10)
            outw.far()

        @pl.when(step >= 2)
        def _():
            for h in range(3):
                store(h, 0, 3 * lax.rem(step, 2) + h).wait()

        for h in range(3):
            task(h, step, 3 * lax.rem(step, 2) + h)
        return carry

    lax.fori_loop(0, 4, arriving, 0)

    def arrived(i, carry):
        @pl.when(i == 0)
        def _():
            keys.far()
            feed[0].far()
            feed[2].go(1, 2, 9)
            keys.got(13)
            keys.got(14)

        @pl.when(i == 1)
        def _():
            feed[1].pair()
            keys.last()
            keys.got(15)
            keys.got(16)
            emits[1].start()

        @pl.when(i == 2)
        def _():
            close(0)
            feed[0].last()
            outw.last()

        @pl.when(i == 3)
        def _():
            feed[2].near()

        @pl.when(i == 4)
        def _():
            close(1)
            feed[2].pair()

        @pl.when(i == 5)
        def _():
            share[0].near()
            share[0].pair()

        h = i // 2
        for half in range(2):
            slot = lax.rem(2 * i + half, 6)
            store(h, 0, slot).wait()
            task(h, 4 + 2 * lax.rem(i, 2) + half, slot)
        return carry

    lax.fori_loop(0, 6, arrived, 0)
    close(2)
    feed[1].far()
    share[0].far()
    share[1].near()
    share[1].pair()
    share[1].far()
    share[2].near()
    share[2].pair()
    share[2].far()
    feed[2].far()
    share[0].last()
    share[1].last()
    feed[1].last()
    share[2].last()
    outw.end()

    def forward_rows(i, carry):
        rows = pl.ds(pl.multiple_of(i * 256, 256), 256)
        value = x_ref[rows].astype(F32) + dot(att[:, rows].T, wo[...])
        inverse = rms_inverse(value)
        mid[rows] = value
        inv[rows] = jnp.broadcast_to(inverse, (256, 128))
        low[rows] = (value * inverse).astype(BF)
        return carry

    lax.fori_loop(0, 2, forward_rows, 0)
    emits[5].start()
    keep[2].wait()
    feed[0].end()
    feed[2].last()

    def gate_rows(i, carry):
        rows = pl.ds(pl.multiple_of(i * 256, 256), 256)
        gate[rows] = dot(low[rows], wf[0])
        return carry

    lax.fori_loop(0, 2, gate_rows, 0)
    keep[3].wait()
    feed[1].end()

    def up_rows(i, carry):
        rows = pl.ds(pl.multiple_of(i * 256, 256), 256)
        u = dot(low[rows], wf[1])
        up[rows] = u
        g = gate[rows]
        act[rows] = (g * jax.nn.sigmoid(g) * u).astype(BF)
        return carry

    lax.fori_loop(0, 2, up_rows, 0)
    emits[6].start()
    keep[4].wait()
    feed[2].end()

    def down_rows(i, carry):
        rows = pl.ds(pl.multiple_of(i * 256, 256), 256)
        ffn[rows] = dot_nt(act[rows], wf[2]).astype(BF)
        return carry

    lax.fori_loop(0, 2, down_rows, 0)
    sum_f.begin()
    gain_two[...] = jnp.zeros_like(gain_two)

    def backward_rows(i, carry):
        @pl.when(i == 1)
        def _():
            sum_f.relay()

        rows = pl.ds(pl.multiple_of(i * 256, 256), 256)
        ct = cot[rows]
        g, u = gate[rows], up[rows]
        sig = jax.nn.sigmoid(g)
        grad_act = dot(ct, wf[2])
        gg = (grad_act * u * sig * (1.0 + g * (1.0 - sig))).astype(BF)
        gu = (grad_act * g * sig).astype(BF)
        grad_g[rows] = gg
        grad_u[rows] = gu
        back = dot_nt(gg, wf[0]) + dot_nt(gu, wf[1])
        hat = low[rows].astype(F32)
        both = back * hat
        gain_two[...] += jnp.sum(both, axis=0, keepdims=True)
        pull = jnp.mean(both, axis=-1, keepdims=True)
        part = (ct.astype(F32) * 0.125 + inv[rows][:, 0:1] * (back - hat * pull)).astype(BF)
        share_ref[rows] = part
        u_ref[:, rows] = dot_nt(wo[...], part).astype(BF)
        return carry

    lax.fori_loop(0, 2, backward_rows, 0)
    for k in range(7, 10):
        emits[k].start()
    mid_own[...] = mid[pl.ds(pl.multiple_of(me.t * 64, 64), 64)]
    sum_f.columns(col_sum)
    for k in range(10):
        emits[k].wait()
    keys.sent()
    sum_f.sent()
    for s in share:
        s.sent()
    for slot in range(6):
        store(0, 0, slot).wait()


def forward_part(*operands):
    tokens = 512
    kept = [
        ((1536, 384), BF),
        ((16 * tokens, 128), BF),
        ((128, 3 * tokens), BF),
        ((384, tokens), F32),
        ((tokens, 1536), BF),
        ((tokens, 1536), BF),
        ((tokens, 896), BF),
        ((tokens, 896), BF),
        ((tokens, 896), BF),
        ((tokens, 1536), BF),
    ]
    shapes = [jax.ShapeDtypeStruct(*k) for k in kept] + [
        jax.ShapeDtypeStruct((8, 3 * tokens), F32),
        jax.ShapeDtypeStruct((192, tokens), BF),
        jax.ShapeDtypeStruct((1536, tokens), BF),
        jax.ShapeDtypeStruct((64, 1536), F32),
        jax.ShapeDtypeStruct((2, 64, 1536), BF),
        jax.ShapeDtypeStruct((1, 1536), F32),
        jax.ShapeDtypeStruct((8, 3, 1024, tokens), BF),
    ]
    scratch = [
        *[pltpu.VMEM(*k) for k in kept],
        pltpu.VMEM((1536, 256), BF),
        pltpu.VMEM((3, 1536, 896), BF),
        pltpu.VMEM((1536, 1536), BF),
        pltpu.VMEM((1536, tokens), BF),
        pltpu.VMEM((3, 80, tokens), F32),
        pltpu.VMEM((6, 1024, tokens), BF),
        pltpu.VMEM((tokens, 1536), F32),
        pltpu.VMEM((tokens, 128), F32),
        pltpu.VMEM((tokens, 896), F32),
        pltpu.VMEM((tokens, 896), F32),
        pltpu.VMEM((tokens, 1536), BF),
        *[DMA((17,))] * 4,
        *[DMA((3, 17))] * 2,
        *[DMA((17,))] * 4,
        *[DMA((3, 9))] * 2,
        DMA((5,)),
        DMA((6,)),
        DMA((10,)),
        *ring_scratch(32, 1536),
    ]
    return pl.pallas_call(
        forward_kernel,
        out_shape=shapes,
        in_specs=[SM] + [VM] * 7,
        out_specs=[HB] * 10 + [VM] * 6 + [HB],
        scratch_shapes=scratch,
        name="forward_part",
        compiler_params=pltpu.CompilerParams(
            collective_id=0, has_side_effects=True, vmem_limit_bytes=59 << 20
        ),
    )(*operands)


def backward_kernel(
    wq_in, kv_in, qt_in, raw_in, normed_in, low, act, grad_g, grad_u, share_in,
    sums, att_own, u_ref, mid_own, col_sum, gain_two, p_all, cot, x_in, cos_ref, sin_ref,
    blk, gin, own_q, own_w, gains,
    wq, kv, qt, raw, share_ref, x_ref, col_z,
    mid_rows, branch, gt, drift, dq, gk, gk_sib, wg, sib_w, pw, sib_p, po, sib_o, back, pre, extra,
    s_blk, r_blk, s_br, r_br, s_in, r_in, s_ex, r_ex, s_sib, r_sib, s_loc, s_p,
    *rest,
):
    me = Place()
    cn = ctx_neighbours(me)
    tn = tp_neighbours(me)
    sib = cn[3]
    tokens = 512
    scratch = [rest[8 * k : 8 * k + 8] for k in range(9)]
    crossing = tp_cross(me)
    greet([*cn, *tn, *crossing, (me.c, me.tp(0, 2)), (me.c, me.tp(1, 2))])

    def tp_block(k):
        return me.tp(*SLOTS[k])

    def chip(k):
        dz, dx = SLOTS[k]
        return me.ctx(dz, dx) // 2

    def rows_of(ref, size):
        def src(k, part):
            start = pl.multiple_of(tp_block(k) * size, size) + part * (size // 2)
            return ref.at[pl.ds(pl.multiple_of(start, size // 2), size // 2)]

        return src

    sum_u = ring(rows_of(u_ref, 192), 96, scratch[0], tn, True, crossing)
    sum_two = ring(rows_of(share_ref, 64), 32, scratch[1], tn, True, crossing)
    sum_b = ring(rows_of(back, 64), 32, scratch[2], tn, False, crossing)
    sum_kv = ring(
        lambda k, part: gk.at[k, me.core, pl.ds(64 * part, 64)], 64, scratch[3], cn
    )
    sum_w = [
        ring(
            lambda k, part, p=p: wg.at[p, chip(k), me.core, pl.ds(48 * part, 48)],
            48,
            scratch[4 + p],
            cn,
        )
        for p in range(3)
    ]
    sum_q = ring(
        lambda k, part: pw.at[chip(k), me.core, pl.ds(48 * part, 48)], 48, scratch[7], cn
    )
    sum_o = ring(
        lambda k, part: po.at[chip(k), me.core, pl.ds(48 * part, 48)], 48, scratch[8], cn
    )
    put_two = Gather(blk, 64, me.tp, *tn, None, s_blk, r_blk, over=True)
    put_br = Gather(branch, 64, me.tp, *tn, None, s_br, r_br)
    put_in = Gather(gin, 64, me.tp, *tn, None, s_in, r_in)
    others = [(dz, dy) for dz in (0, 1) for dy in range(4) if (dz, dy) != (0, 0)]
    put_ex = [
        pltpu.make_async_remote_copy(
            src_ref=extra.at[0],
            dst_ref=extra.at[1 + k],
            send_sem=s_ex.at[k],
            recv_sem=r_ex.at[k],
            device_id=(me.c, me.tp(*o)),
            device_id_type=MESH,
        )
        for k, o in enumerate(others)
    ]

    def to_sibling(k, here, there):
        return pltpu.make_async_remote_copy(
            src_ref=here,
            dst_ref=there,
            send_sem=s_sib.at[k],
            recv_sem=r_sib.at[k],
            device_id=sib,
            device_id_type=MESH,
        )

    def key_swap(k):
        return to_sibling(k, gk.at[k, 1 - me.core], gk_sib.at[k])

    swap_w = [to_sibling(8 + p, wg.at[p, :, 1 - me.core], sib_w.at[p]) for p in range(3)]
    swap_p = to_sibling(11, pw.at[:, 1 - me.core], sib_p)
    swap_o = to_sibling(13, po.at[:, 1 - me.core], sib_o)
    cross = pltpu.make_async_remote_copy(
        src_ref=col_sum.at[1],
        dst_ref=col_z,
        send_sem=s_sib.at[12],
        recv_sem=r_sib.at[12],
        device_id=tn[0],
        device_id_type=MESH,
    )
    takes = [
        pltpu.make_async_copy(h, v, s_loc.at[14 + k])
        for k, (h, v) in enumerate(
            [
                (wq_in, wq),
                (kv_in, kv),
                (qt_in, qt),
                (raw_in, raw),
                (share_in, share_ref),
                (x_in.at[pl.ds(pl.multiple_of(me.t * 64, 64), 64)], x_ref),
            ]
        )
    ]

    sum_u.begin()
    cross.start()

    def weight_grads(b_low, b_cot, b_one, b_two):
        def load(k, here, there):
            return pltpu.make_async_copy(here, there, s_loc.at[k])

        loads = [load(0, low, b_low), load(1, grad_g, b_one), load(2, grad_u, b_two)]
        loads += [load(3, cot, b_cot), load(4, act, b_one)]
        for k in loads[0:4] + takes:
            k.start()
        loads[0].wait()
        for p, (left, right) in enumerate([(b_low, b_one), (b_low, b_two), (b_cot, b_one)]):
            loads[(1, 2, 4)[p]].wait()
            if p == 2:
                loads[3].wait()

            def chunk(i, carry, p=p, left=left, right=right):
                at = pl.ds(pl.multiple_of(384 * i, 384), 384)
                whole = dot(left[:, at].T, right[...]).astype(BF)
                for q in range(4):
                    wg[p, 2 * i + q // 2, q % 2] = whole[96 * q : 96 * q + 96]
                return carry

            lax.fori_loop(0, 4, chunk, 0)
            swap_w[p].start()
            if p == 0:
                loads[4].start()
                sum_u.relay()

    pl.run_scoped(
        weight_grads,
        pltpu.VMEM((tokens, 1536), BF),
        pltpu.VMEM((tokens, 1536), BF),
        pltpu.VMEM((tokens, 896), BF),
        pltpu.VMEM((tokens, 896), BF),
    )

    def join_w(p):
        swap_w[p].wait_recv()

        def one(j, carry):
            add_into(wg.at[p, j, me.core], wg.at[p, j, me.core], sib_w.at[p, j])
            return carry

        lax.fori_loop(0, 8, one, 0)

    join_w(0)
    sum_w[0].begin()
    for k in takes:
        k.wait()
    grad_att = jnp.concatenate([sum_u.finish(0), sum_u.finish(1)], axis=0)
    own = pl.multiple_of(me.t * 64, 64)
    cross.wait_recv()
    blk[pl.ds(own, 64)] = (
        mid_own[...] + col_sum[0].astype(F32) + col_z[...].astype(F32)
    ).astype(BF)
    sum_two.begin()
    put_two.begin()
    gt[0:64] = jnp.zeros((64, 3 * tokens), BF)
    for h in range(3):
        cols = slice(h * tokens, (h + 1) * tokens)
        grad = grad_att[64 * h : 64 * h + 64]
        inverse = 1.0 / sums[0:1, cols]
        gt[64:128, cols] = (grad * inverse).astype(BF)
        drift[0:1, cols] = (
            jnp.sum(grad * att_own[64 * h : 64 * h + 64].astype(F32), axis=0, keepdims=True)
            * inverse
        )
    dq[...] = jnp.zeros_like(dq)

    def join_keys(k):
        key_swap(k).wait_recv()
        add_into(gk.at[k, me.core], gk.at[k, me.core], gk_sib.at[k])

    def key_loop(pbuf):
        def load(step, h):
            return pltpu.make_async_copy(
                p_all.at[chip_of(me, step, SLOTS), h], pbuf.at[h], s_p.at[h]
            )

        for h in range(3):
            load(0, h).start()

        def key_step(step, carry):
            @pl.when(step == 1)
            def _():
                join_keys(0)
                sum_kv.go(0, 1)
                sum_two.relay()
                sum_w[0].relay()
                join_w(1)
                sum_w[1].begin()

            @pl.when(step == 2)
            def _():
                join_keys(1)
                sum_kv.go(2, 3)
                put_two.near()

            @pl.when(step == 3)
            def _():
                join_keys(2)
                sum_kv.go(4)
                sum_kv.relay_right(1)
                branch_rows = jnp.concatenate([sum_two.finish(0), sum_two.finish(1)], axis=0)
                mid_rows[...] = branch_rows
                branch[pl.ds(own, 64)] = branch_rows.astype(BF)
                put_br.begin()
                sum_w[0].column()
                sum_w[1].relay()
                join_w(2)
                sum_w[2].begin()

            @pl.when(step == 4)
            def _():
                join_keys(3)
                sum_kv.go(5)
                sum_kv.relay_left(1)
                put_two.far()

            @pl.when(step == 5)
            def _():
                join_keys(4)
                sum_kv.go(6)
                sum_kv.relay_right(0)
                sum_w[1].column()
                put_two.pair()
                put_br.near()
                put_br.pair()

            @pl.when(step == 6)
            def _():
                join_keys(5)
                sum_kv.go(7)
                sum_kv.relay_left(0)
                put_br.far()
                put_two.last()
                sum_w[2].relay()

            @pl.when(step == 7)
            def _():
                join_keys(6)
                sum_kv.column()
                put_br.last()

            place = chip_of(me, step, SLOTS)
            rows = kv[pl.ds(pl.multiple_of(place * 1024, 1024), 1024), :]
            key_t = rows.T[0:64]
            key_grad = value_grad = 0.0
            for h in range(3):
                cols = slice(h * tokens, (h + 1) * tokens)
                slopes = dot(rows, gt[:, cols])
                load(step, h).wait()
                weight = pbuf[h]
                grad = (weight.astype(F32) * (slopes - drift[0:1, cols])).astype(BF)
                dq[:, cols] += dot(key_t, grad)
                key_grad += dot_nt(qt[0:64, cols], grad)
                value_grad += dot_nt(gt[64:128, cols], weight)

                @pl.when(step < 7)
                def _(h=h):
                    load(step + 1, h).start()

            both = jnp.concatenate([key_grad * LN2, value_grad], axis=0).astype(BF)
            gk[step, 0] = both[:, 0:512]
            gk[step, 1] = both[:, 512:1024]
            key_swap(step).start()
            return carry

        lax.fori_loop(0, 8, key_step, 0)

    pl.run_scoped(key_loop, pltpu.VMEM((3, 1024, tokens), BF))
    def finale(normed):
        fetch = pltpu.make_async_copy(normed_in, normed, s_loc.at[5])
        fetch.start()
        att_n = jnp.concatenate(
            [att_own[...].astype(F32), jnp.zeros((64, tokens), F32)], axis=0
        ).T.astype(BF)
        for i in range(4):
            at = slice(384 * i, 384 * i + 384)
            whole = dot(branch[:, at].T, att_n).astype(BF)
            for q in range(4):
                po[2 * i + q // 2, q % 2] = whole[96 * q : 96 * q + 96]
        swap_o.start()
        query_gain, key_gain = gain_columns(wq)
        cosine, sine = cos_ref[...], sin_ref[...]

        def unturn(grad, value, gain):
            inverse = column_inverse(value)
            hat = value * inverse
            a, b = grad[:32], grad[32:]
            plain = jnp.concatenate([a * cosine + b * sine, b * cosine - a * sine], axis=0)
            gain_grad = jnp.sum(plain * hat, axis=1, keepdims=True)
            pulled = plain * gain
            back_grad = inverse * (pulled - hat * jnp.mean(pulled * hat, axis=0, keepdims=True))
            return gain_grad, back_grad

        query_gain_grad = 0.0
        for h in range(3):
            part, grad = unturn(
                dq[:, h * tokens : (h + 1) * tokens] * 0.125, raw[64 * h : 64 * h + 64], query_gain
            )
            query_gain_grad += part
            pre[64 * h : 64 * h + 64] = grad
        join_keys(7)
        key_grad, value_grad = sum_kv.finish(0), sum_kv.finish(1)
        key_gain_grad, grad = unturn(key_grad, raw[192:256], key_gain)
        pre[192:256] = grad
        pre[256:320] = value_grad
        pre[320:384] = jnp.zeros((64, tokens), F32)
        pre_n = pre[...].T.astype(BF)
        for i in range(2):
            rows = slice(256 * i, 256 * i + 256)
            back[rows] = dot_nt(pre_n[rows], wq[...]).astype(BF)
        sum_b.begin()
        fetch.wait()
        gain_one = 0.0
        for i in range(4):
            rows = slice(128 * i, 128 * i + 128)
            gain_one += jnp.sum(
                back[rows].astype(F32) * normed[rows].astype(F32), axis=0, keepdims=True
            )
        sum_w[2].column()
        swap_o.wait_recv()

        def join_o(j, carry):
            add_into(po.at[j, me.core], po.at[j, me.core], sib_o.at[j])
            return carry

        lax.fori_loop(0, 8, join_o, 0)
        sum_o.begin()
        lane = lax.broadcasted_iota(jnp.int32, (64, 1536), 1)
        unit = lax.broadcasted_iota(jnp.int32, (64, 1536), 0)
        spot = lane == (unit // 4) * 96 + lax.rem(unit, 4)

        def spread(column):
            return jnp.sum(jnp.where(spot, column, 0.0), axis=0, keepdims=True)

        lines = jnp.concatenate(
            [
                jnp.zeros((64, 1536), F32),
                gain_one,
                gain_two[...],
                spread(query_gain_grad),
                spread(key_gain_grad),
                jnp.zeros((60, 1536), F32),
            ],
            axis=0,
        )
        sides = lines.T
        sum_b.relay()
        for i in range(4):
            at = slice(384 * i, 384 * i + 384)
            part = dot(normed[:, at].T, pre_n)
            whole = jnp.concatenate([part[:, 0:256], part[:, 256:384] + sides[at]], axis=1).astype(BF)
            for q in range(4):
                pw[2 * i + q // 2, q % 2] = whole[96 * q : 96 * q + 96]
        swap_p.start()
        sum_o.relay()
        swap_p.wait_recv()

        def join_p(j, carry):
            add_into(pw.at[j, me.core], pw.at[j, me.core], sib_p.at[j])
            return carry

        lax.fori_loop(0, 8, join_p, 0)
        sum_q.begin()
        value = x_ref[...].astype(F32)
        inverse = rms_inverse(value)
        hat = value * inverse
        back_one = jnp.concatenate([sum_b.finish(0), sum_b.finish(1)], axis=0)
        gin[pl.ds(own, 64)] = (
            mid_rows[...]
            + inverse * (back_one - hat * jnp.mean(back_one * hat, axis=-1, keepdims=True))
        ).astype(BF)
        put_in.begin()
        for p in range(3):
            for half in range(2):
                own_w[p, 48 * half : 48 * half + 48] = sum_w[p].finish(half)
        put_in.near()
        sum_q.relay()
        sum_o.column()
        put_in.pair()
        sum_q.column()
        put_in.far()
        for half in range(2):
            own_q[48 * half : 48 * half + 48, 0:384] = sum_q.finish(half)
        extra[0] = own_q[:, 256:384].T[64:72]
        for p in put_ex:
            p.start()
        for half in range(2):
            own_q[48 * half : 48 * half + 48, 384:640] = sum_o.finish(half)
        put_in.last()
        for p in put_ex:
            p.wait()
        total = extra[0]
        for b in range(1, 8):
            total += extra[b]
        gains[...] = total
        for s in [sum_u, sum_two, sum_b, sum_kv, sum_q, sum_o, *sum_w, put_two, put_br, put_in]:
            s.sent()
        for k in range(8):
            key_swap(k).wait_send()
        for s in [*swap_w, swap_p, swap_o, cross]:
            s.wait_send()

    pl.run_scoped(finale, pltpu.VMEM((tokens, 1536), BF))


def backward_part(*operands):
    tokens = 512
    shapes = [
        jax.ShapeDtypeStruct((512, 1536), BF),
        jax.ShapeDtypeStruct((512, 1536), BF),
        jax.ShapeDtypeStruct((96, 640), F32),
        jax.ShapeDtypeStruct((3, 96, 896), F32),
        jax.ShapeDtypeStruct((8, 96), F32),
    ]
    scratch = [
        pltpu.VMEM((1536, 384), BF),
        pltpu.VMEM((16 * tokens, 128), BF),
        pltpu.VMEM((128, 3 * tokens), BF),
        pltpu.VMEM((384, tokens), F32),
        pltpu.VMEM((tokens, 1536), BF),
        pltpu.VMEM((64, 1536), BF),
        pltpu.VMEM((64, 1536), BF),
        pltpu.VMEM((64, 1536), F32),
        pltpu.VMEM((tokens, 1536), BF),
        pltpu.VMEM((128, 3 * tokens), BF),
        pltpu.VMEM((8, 3 * tokens), F32),
        pltpu.VMEM((64, 3 * tokens), F32),
        pltpu.VMEM((8, 2, 128, 512), BF),
        pltpu.VMEM((8, 128, 512), BF),
        pltpu.VMEM((3, 8, 2, 96, 896), BF),
        pltpu.VMEM((3, 8, 96, 896), BF),
        pltpu.VMEM((8, 2, 96, 384), BF),
        pltpu.VMEM((8, 96, 384), BF),
        pltpu.VMEM((8, 2, 96, 256), BF),
        pltpu.VMEM((8, 96, 256), BF),
        pltpu.VMEM((tokens, 1536), BF),
        pltpu.VMEM((384, tokens), F32),
        pltpu.VMEM((8, 8, 96), F32),
        *[DMA((9,))] * 8,
        DMA((14,)),
        DMA((14,)),
        DMA((21,)),
        DMA((3,)),
        *ring_scratch(96, 512, True),
        *ring_scratch(32, 1536, True),
        *ring_scratch(32, 1536),
        *ring_scratch(64, 512),
        *ring_scratch(48, 896) * 3,
        *ring_scratch(48, 384),
        *ring_scratch(48, 256),
    ]
    return pl.pallas_call(
        backward_kernel,
        out_shape=shapes,
        in_specs=[HB] * 10 + [VM] * 6 + [HB] * 3 + [VM] * 2,
        out_specs=[VM] * 5,
        scratch_shapes=scratch,
        name="backward_part",
        compiler_params=pltpu.CompilerParams(
            collective_id=1, has_side_effects=True, vmem_limit_bytes=59 << 20
        ),
    )(*operands)


FREQ = [[THETA ** (-2.0 * i / HD)] * 128 for i in range(HD // 2)]


def body(
    block_input, positions, attn_gain, query_weight, key_weight, value_weight, query_gain,
    key_gain, output_weight, ffn_gain, gate_weight, up_weight, down_weight, out_cotangent,
):
    def line(gain):
        return gain.reshape(1, -1)

    wq_s, wo_s, wf_s, cosine, sine = prepare(
        line(positions), line(attn_gain), line(ffn_gain), line(query_gain), line(key_gain),
        jnp.array(FREQ, F32), query_weight, key_weight.T, value_weight.T, output_weight,
        gate_weight, up_weight, down_weight.T,
    )
    results = forward_part(positions, block_input, out_cotangent, wq_s, wo_s, wf_s, cosine, sine)
    results = backward_part(*results, out_cotangent, block_input, cosine, sine)
    return conclude(line(attn_gain), line(ffn_gain), *results)


def solution(mesh):
    in_specs = (
        P("ctx", None),
        P(),
        P("ctx"),
        P("ctx", "tp"),
        P("ctx", "tp"),
        P("ctx", "tp"),
        P("ctx"),
        P("ctx"),
        P("tp", "ctx"),
        P("ctx"),
        P("ctx", "tp"),
        P("ctx", "tp"),
        P("tp", "ctx"),
        P("ctx", None),
    )
    out_specs = (
        P("ctx", None),
        P("ctx", None),
        P("ctx"),
        P("ctx", "tp"),
        P("ctx", "tp"),
        P("ctx", "tp"),
        P("ctx"),
        P("ctx"),
        P("tp", "ctx"),
        P("ctx"),
        P("ctx", "tp"),
        P("ctx", "tp"),
        P("tp", "ctx"),
    )
    return jax.shard_map(body, mesh=mesh, in_specs=in_specs, out_specs=out_specs, check_vma=False)
```

```python
import functools
import math

import jax
import jax.numpy as jnp
from jax import lax
from jax.experimental import pallas as pl
from jax.experimental.pallas import tpu as pltpu
from jax.sharding import PartitionSpec as P

HD = 64
EPS = 1e-05
THETA = 1000000.0
LOG2E = math.log2(math.e)
LN2 = math.log(2.0)
BF = jnp.bfloat16
F32 = jnp.float32
MESH = pl.DeviceIdType.MESH
VM = pl.BlockSpec(memory_space=pltpu.VMEM)
SM = pl.BlockSpec(memory_space=pltpu.SMEM)
HB = pl.BlockSpec(memory_space=pl.ANY)
DMA = pltpu.SemaphoreType.DMA


class Place:
    def __init__(self):
        self.c = lax.axis_index("ctx")
        self.t = lax.axis_index("tp")
        self.core = lax.rem(self.c, 2)
        self.x = lax.rem(self.c // 2, 4)
        self.zh = self.c // 8
        self.y = lax.rem(self.t, 4)
        self.zl = self.t // 4

    def ctx(self, dz, dx, other=0):
        core = self.core if not other else 1 - self.core
        zh = self.zh if not dz else 1 - self.zh
        return (zh * 4 + lax.rem(self.x + dx, 4)) * 2 + core

    def tp(self, dz, dy):
        zl = self.zl if not dz else 1 - self.zl
        return zl * 4 + lax.rem(self.y + dy, 4)


def greet(peers):
    barrier = pltpu.get_barrier_semaphore()
    for peer in peers:
        pl.semaphore_signal(barrier, inc=1, device_id=peer, device_id_type=MESH)
    pl.semaphore_wait(barrier, len(peers))


class Gather:
    def __init__(self, buf, rows, block, pair, right, left, sibling, send, recv, own=None, cross=(), over=False):
        self.buf, self.rows, self.block = buf, rows, block
        self.to = {"z": pair, "r": right, "l": left, "s": sibling}
        self.cross = len(cross) > 0
        if self.cross:
            self.to["zr"], self.to["zl"] = cross
        self.send, self.recv, self.own = send, recv, own
        self.plan = {
            0: ((0, 0), 0, "z"),
            1: ((0, 0), 0, "r"),
            2: ((0, 0), 0, "l"),
            3: ((0, 3), 1, "r"),
            4: ((0, 1), 2, "l"),
            5: ((1, 0), 0, "r"),
            6: ((1, 0), 0, "l"),
            7: ((1, 3), 1, "r"),
            8: ((1, 1), 2, "l"),
            9: ((0, 0), 0, "s"),
            10: ((1, 0), 0, "s"),
            11: ((0, 3), 0, "s"),
            12: ((0, 1), 0, "s"),
            13: ((0, 2), 0, "s"),
            14: ((1, 3), 0, "s"),
            15: ((1, 1), 0, "s"),
            16: ((1, 2), 0, "s"),
        }
        if self.cross:
            self.plan[5] = ((0, 0), 0, "zr")
            self.plan[6] = ((0, 0), 0, "zl")
        self.over = over
        if over:
            self.plan[5] = ((0, 3), 0, "z")
            self.plan[6] = ((0, 1), 0, "z")
            self.plan[7] = ((0, 2), 1, "z")
            self.plan[8] = ((0, 2), 2, "z")
        self.count = 17 if sibling is not None else 9

    def copy(self, k):
        where, part, to = self.plan[k]
        rows = self.rows if part == 0 else self.rows // 2
        start = pl.multiple_of(self.block(*where) * self.rows, self.rows)
        if part == 2:
            start = pl.multiple_of(start + rows, rows)
        there = self.buf.at[pl.ds(start, rows)]
        here = there
        if where == (0, 0) and self.own is not None:
            here = self.own
        return pltpu.make_async_remote_copy(
            src_ref=here,
            dst_ref=there,
            send_sem=self.send.at[k],
            recv_sem=self.recv.at[k],
            device_id=self.to[to],
            device_id_type=MESH,
        )

    def go(self, *which):
        for k in which:
            if k < self.count:
                self.copy(k).start()

    def got(self, *which):
        for k in which:
            if k < self.count:
                self.copy(k).wait_recv()

    def begin(self):
        self.go(0, 1, 2, 9)
        if self.cross:
            self.go(5, 6)

    def near(self):
        self.got(1)
        self.go(3, 11)
        if self.over:
            self.go(5)
        self.got(2)
        self.go(4, 12)
        if self.over:
            self.go(6)

    def pair(self):
        self.got(0)
        if not self.cross and not self.over:
            self.go(5, 6)
        self.go(10)

    def far(self):
        if self.over:
            self.got(3)
            self.go(7)
            self.got(4)
            self.go(8)
            self.got(5, 6)
            return
        self.got(5)
        self.go(7, 14)
        self.got(6)
        self.go(8, 15)
        self.got(3, 4)
        self.go(13)

    def last(self):
        self.got(7, 8)
        self.go(16)

    def sent(self):
        for k in range(self.count):
            self.copy(k).wait_send()

    def end(self):
        self.got(*range(9, 17))
        self.sent()


def ctx_neighbours(me):
    return (
        (me.ctx(1, 0), me.t),
        (me.ctx(0, 1), me.t),
        (me.ctx(0, 3), me.t),
        (me.ctx(0, 0, 1), me.t),
    )


def tp_neighbours(me):
    return (me.c, me.tp(1, 0)), (me.c, me.tp(0, 1)), (me.c, me.tp(0, 3))


def tp_cross(me):
    return (me.c, me.tp(1, 1)), (me.c, me.tp(1, 3))


def rms_inverse(value):
    return lax.rsqrt(jnp.mean(value * value, axis=-1, keepdims=True) + EPS)


def column_inverse(value):
    return lax.rsqrt(jnp.mean(value * value, axis=0, keepdims=True) + EPS)


def gain_columns(wq):
    total = wq[0:64, 256:384].astype(F32)
    for k in range(1, 16):
        total += wq[96 * k : 96 * k + 64, 256:384].astype(F32)
    return total[:, 64:65], total[:, 65:66]


def dot(a, b):
    return jnp.dot(a, b, preferred_element_type=F32)


def dot_nt(a, b):
    return lax.dot_general(a, b, (((1,), (1,)), ((), ())), preferred_element_type=F32)


def dot_tn(a, b):
    return lax.dot_general(a, b, (((0,), (0,)), ((), ())), preferred_element_type=F32)


PAIRS = ((0, 0), (0, 3), (0, 1), (1, 0), (0, 2), (1, 3), (1, 1), (1, 2))


def chip_of(me, step, order):
    dz = sum(jnp.where(step == k, p[0], 0) for k, p in enumerate(order) if p[0])
    dx = sum(jnp.where(step == k, p[1], 0) for k, p in enumerate(order) if p[1])
    return lax.rem(me.zh + dz, 2) * 4 + lax.rem(me.x + dx, 4)


SLOTS = ((1, 2), (0, 2), (1, 1), (1, 3), (0, 1), (0, 3), (1, 0), (0, 0))


def add_into(out, *terms):
    total = terms[0][...].astype(F32)
    for term in terms[1:]:
        total += term[...].astype(F32)
    out[...] = total.astype(out.dtype)


class RingSum:
    def __init__(self, src, half, stage, rel_l, rel_r, col_l, col_r, from_z, pair, right, left, send, recv, cross=()):
        self.src, self.half = src, half
        at_stage = {2: (0, 0), 3: (0, 1), 4: (1, 0), 5: (1, 1)}

        def put(k, part):
            if stage is None:
                return src(k, part)
            rows = pl.ds(part * half, half)
            return stage.at[2 if k == 6 else at_stage[k][0], rows]

        self.put = put
        self.rel_l, self.rel_r, self.col_l, self.col_r, self.from_z = rel_l, rel_r, col_l, col_r, from_z
        self.to = {"z": pair, "r": right, "l": left, "zr": right, "zl": left}
        self.cross = len(cross) > 0
        if self.cross:
            self.to["zr"], self.to["zl"] = cross
        self.send, self.recv = send, recv
        low, high = pl.ds(0, half), pl.ds(half, half)
        self.low, self.high = low, high
        self.last = 14
        self.plan = [
            (src(0, 0), rel_l.at[1], "r"),
            (src(0, 1), rel_r.at[1], "l"),
            (src(1, 0), rel_l.at[0], "r"),
            (src(1, 1), rel_r.at[0], "l"),
            (src(2, 1), col_l.at[1, high], "zr"),
            (src(3, 0), col_r.at[1, low], "zl"),
            (src(4, 1), col_l.at[0, high], "r"),
            (src(5, 0), col_r.at[0, low], "l"),
            (put(2, 0), col_l.at[1, low], "zr"),
            (put(3, 1), col_r.at[1, high], "zl"),
            (put(4, 0), col_l.at[0, low], "r"),
            (put(5, 1), col_r.at[0, high], "l"),
            ((src if self.cross else put)(6, 0), from_z.at[low], "z"),
            ((src if self.cross else put)(6, 1), from_z.at[high], "z"),
        ]

    def copy(self, k):
        here, there, to = self.plan[k]
        return pltpu.make_async_remote_copy(
            src_ref=here,
            dst_ref=there,
            send_sem=self.send.at[k],
            recv_sem=self.recv.at[k],
            device_id=self.to[to],
            device_id_type=MESH,
        )

    def go(self, *which):
        for k in which:
            self.copy(k).start()

    def got(self, *which):
        for k in which:
            self.copy(k).wait_recv()

    def begin(self):
        self.go(*range(8))
        if self.cross:
            self.go(12, 13)

    def relay_right(self, plane):
        k = 2 if plane else 4
        self.got(0 if plane else 2)
        add_into(self.put(k, 0), self.src(k, 0), self.rel_l.at[plane])
        self.go(8 if plane else 10)

    def relay_left(self, plane):
        k = 3 if plane else 5
        self.got(1 if plane else 3)
        add_into(self.put(k, 1), self.src(k, 1), self.rel_r.at[plane])
        self.go(9 if plane else 11)

    def relay(self):
        for plane in (1, 0):
            self.relay_right(plane)
            self.relay_left(plane)

    def column(self):
        self.got(4, 8, 5, 9)
        for part, rows in enumerate((self.low, self.high)):
            add_into(
                self.put(6, part),
                self.src(6, part),
                self.col_l.at[1, rows],
                self.col_r.at[1, rows],
            )
            self.go(12 + part)

    def columns(self, out):
        self.last = 12
        self.got(4, 8, 5, 9, 6, 10, 7, 11)
        for plane, k in ((0, 7), (1, 6)):
            for part, rows in enumerate((self.low, self.high)):
                add_into(
                    out.at[plane, rows],
                    self.src(k, part),
                    self.col_l.at[plane, rows],
                    self.col_r.at[plane, rows],
                )

    def finish(self, part):
        if part == 0:
            self.got(6, 10, 7, 11, 12, 13)
            if self.cross:
                self.got(4, 8, 5, 9)
        rows = self.low if part == 0 else self.high
        total = self.src(7, part)[...].astype(F32)
        terms = [self.col_l.at[0, rows], self.col_r.at[0, rows], self.from_z.at[rows]]
        if self.cross:
            terms += [self.col_l.at[1, rows], self.col_r.at[1, rows]]
        for term in terms:
            total += term[...].astype(F32)
        return total

    def sent(self):
        for k in range(self.last):
            self.copy(k).wait_send()


def ring_scratch(half, width, stage=False):
    return [
        pltpu.VMEM((3, 2 * half, width) if stage else (1, 16, 128), BF),
        pltpu.VMEM((2, half, width), BF),
        pltpu.VMEM((2, half, width), BF),
        pltpu.VMEM((2, 2 * half, width), BF),
        pltpu.VMEM((2, 2 * half, width), BF),
        pltpu.VMEM((2 * half, width), BF),
        DMA((14,)),
        DMA((14,)),
    ]


def ring(src, half, scratch, neighbours, stage=False, cross=()):
    room, rel_l, rel_r, col_l, col_r, from_z, send, recv = scratch
    return RingSum(
        src, half, room if stage else None, rel_l, rel_r, col_l, col_r, from_z, *neighbours[:3],
        send, recv, cross,
    )


def gain_lines(lines, refs):
    lines[...] = jnp.zeros_like(lines)
    for k, ref in enumerate(refs):
        lines[k : k + 1, 0 : ref.shape[1]] = ref[...].astype(F32)
    columns = lines[...].T
    return columns[0:96, 0:1], columns[0:96, 1:2]


def prepare_kernel(
    places, attn_gain, ffn_gain, query_gain, key_gain, freq,
    query, key_t, value_t, output, gate, up, down_t, wq_s, wo_s, wf_s, cosine, sine, lines,
):
    c = lax.axis_index("ctx")
    gain_one, gain_two = gain_lines(lines, [attn_gain, ffn_gain, query_gain, key_gain])
    row = lax.broadcasted_iota(jnp.int32, (96, 64), 0)
    col = lax.broadcasted_iota(jnp.int32, (96, 64), 1)
    sides = jnp.zeros((96, 64), F32)
    for k in range(2):
        for j in range(4):
            at = (row == 4 * c + j) & (col == k)
            sides = jnp.where(at, lines[2 + k : 3 + k, j : j + 1], sides)

    def lifted(weight, gain):
        return (weight.astype(F32) * gain).astype(BF)

    both = jnp.concatenate([key_t[...].astype(F32), value_t[...].astype(F32)], axis=0).T
    wq_s[:, 0:192] = lifted(query[...], gain_one)
    wq_s[:, 192:320] = lifted(both, gain_one)
    wq_s[:, 320:384] = sides.astype(BF)
    wo_s[:, 192:256] = jnp.zeros((96, 64), BF)
    wo_s[:, 0:192] = output[...].astype(F32).T.astype(BF)
    for k in range(3):
        wf_s[:, 896 * k + 768 : 896 * k + 896] = jnp.zeros((96, 128), BF)
    wf_s[:, 0:864] = lifted(gate[...], gain_two)
    wf_s[:, 896:1760] = lifted(up[...], gain_two)
    wf_s[:, 1792:2656] = down_t[...]
    place = places[0:1, pl.ds(pl.multiple_of(c * 512, 512), 512)]
    angle = freq[:, 0:1] * place.astype(F32)
    cosine[...] = jnp.cos(angle)
    sine[...] = jnp.sin(angle)


def prepare(*operands):
    shapes = [
        jax.ShapeDtypeStruct((96, 384), BF),
        jax.ShapeDtypeStruct((96, 256), BF),
        jax.ShapeDtypeStruct((96, 2688), BF),
        jax.ShapeDtypeStruct((32, 512), F32),
        jax.ShapeDtypeStruct((32, 512), F32),
    ]
    return pl.pallas_call(
        prepare_kernel,
        out_shape=shapes,
        in_specs=[VM] * 13,
        out_specs=[VM] * 5,
        scratch_shapes=[pltpu.VMEM((8, 128), F32)],
        name="prepare",
        compiler_params=pltpu.CompilerParams(vmem_limit_bytes=59 << 20),
    )(*operands)


def conclude_kernel(
    attn_gain, ffn_gain, block, gin, own_q, own_w, side,
    block_output, grad_input, g_attn, g_query, g_key, g_value, g_qg, g_kg, g_out, g_ffn, g_gate, g_up, g_down,
    lines,
):
    gain_one, gain_two = gain_lines(lines, [attn_gain, ffn_gain])
    block_output[...] = block[...]
    grad_input[...] = gin[...].astype(F32)
    g_query[...] = own_q[:, 0:192] * gain_one
    both = (own_q[:, 192:320] * gain_one).T
    g_key[...] = both[0:64]
    g_value[...] = both[64:128]
    g_out[...] = own_q[:, 384:576].T
    g_gate[...] = own_w[0, :, 0:864] * gain_two
    g_up[...] = own_w[1, :, 0:864] * gain_two
    g_down[...] = own_w[2, :, 0:864]
    g_attn[...] = side[0:1, 0:96] / lines[0:1, 0:96]
    g_ffn[...] = side[1:2, 0:96] / lines[1:2, 0:96]
    g_qg[...] = side[2:3, 0:4]
    g_kg[...] = side[3:4, 0:4]


def conclude(*operands):
    dims = [
        ((512, 1536), BF), ((512, 1536), F32), ((1, 96), F32), ((96, 192), F32), ((64, 96), F32),
        ((64, 96), F32), ((1, 4), F32), ((1, 4), F32), ((192, 96), F32), ((1, 96), F32),
        ((96, 864), F32), ((96, 864), F32), ((96, 864), F32),
    ]
    results = pl.pallas_call(
        conclude_kernel,
        out_shape=[jax.ShapeDtypeStruct(*d) for d in dims],
        in_specs=[VM] * 7,
        out_specs=[VM] * 13,
        scratch_shapes=[pltpu.VMEM((8, 128), F32)],
        name="conclude",
        compiler_params=pltpu.CompilerParams(vmem_limit_bytes=59 << 20),
    )(*operands)
    results = [r.T if k in (4, 5, 12) else r for k, r in enumerate(results)]
    return tuple(r.reshape(-1) if r.shape[0] == 1 else r for r in results)


def forward_kernel(
    kb, x_ref, cot, wq_s, wo_s, wf_s, cos_ref, sin_ref,
    wq_out, kv_out, qt_out, raw_out, normed_out, low_out, act_out, g_out, u_out, share_out,
    sums, att_own, u_ref, mid_own, col_sum, gain_two, p_all,
    wq, kv, qt, raw, normed, low, act, grad_g, grad_u, share_ref,
    wo_t, wf, wo, att, acc, pbuf, mid, inv, gate, up, ffn,
    s_w, r_w, s_v, r_v, s_f, r_f, s_o, r_o, s_k, r_k, s_a, r_a, s_l, s_p, s_out,
    *rest,
):
    me = Place()
    cn = ctx_neighbours(me)
    tn = tp_neighbours(me)
    cross = tp_cross(me)
    tokens = x_ref.shape[0]
    greet([*cn, *tn, *cross])
    weights = Gather(wq, 96, me.ctx, *cn, s_w, r_w, own=wq_s)
    outs = Gather(wo_t, 96, me.ctx, *cn, s_v, r_v, own=wo_s)
    feed = [
        Gather(
            wf.at[p], 96, me.ctx, *cn, s_f.at[p], r_f.at[p], own=wf_s.at[:, 896 * p : 896 * p + 896]
        )
        for p in range(3)
    ]
    keys = Gather(kv, tokens, me.ctx, *cn, s_k, r_k)
    outw = Gather(
        wo, 96, lambda dz, dy: me.tp(dz, dy) * 2 + me.core, *tn, cn[3], s_o, r_o
    )
    share = [
        Gather(
            att, 64, lambda dz, dy, h=h: me.tp(dz, dy) * 3 + h, *tn, None, s_a.at[h], r_a.at[h],
            cross=cross,
        )
        for h in range(3)
    ]
    sum_f = ring(
        lambda k, part: ffn.at[
            pl.ds(pl.multiple_of(me.tp(*SLOTS[k]) * 64 + 32 * part, 32), 32)
        ],
        32, rest, tn,
    )

    weights.begin()
    outs.begin()
    feed[0].go(1, 2, 9)
    mine = pl.ds(pl.multiple_of(me.c * 96, 96), 96)
    keep = [
        pltpu.make_async_copy(wq_s, wq.at[mine], s_l.at[0]),
        pltpu.make_async_copy(wo_s, wo_t.at[mine], s_l.at[1]),
    ] + [
        pltpu.make_async_copy(wf_s.at[:, 896 * p : 896 * p + 896], wf.at[p, mine], s_l.at[2 + p])
        for p in range(3)
    ]
    for k in keep:
        k.start()
    emits = [
        pltpu.make_async_copy(v, h, s_out.at[k])
        for k, (v, h) in enumerate(
            [
                (wq, wq_out),
                (kv, kv_out),
                (qt, qt_out),
                (raw, raw_out),
                (normed, normed_out),
                (low, low_out),
                (act, act_out),
                (grad_g, g_out),
                (grad_u, u_out),
                (share_ref, share_out),
            ]
        )
    ]

    def norm_rows(i, carry):
        rows = pl.ds(pl.multiple_of(i * 64, 64), 64)
        value = x_ref[rows].astype(F32)
        normed[rows] = (value * rms_inverse(value)).astype(BF)
        return carry

    lax.fori_loop(0, tokens // 64, norm_rows, 0)
    weights.near()
    weights.pair()
    feed[0].go(0)
    outs.near()
    outs.pair()
    emits[4].start()
    weights.far()
    weights.last()
    outs.far()
    outs.last()
    keep[1].wait()
    outs.end()
    heads = wo_t[...].T
    wo[pl.ds(pl.multiple_of(me.t * 192 + me.core * 96, 96), 96)] = jnp.where(
        me.core == 0, heads[0:96], heads[96:192]
    )
    outw.begin()
    keep[0].wait()
    weights.end()
    feed[1].go(1, 2, 9)
    emits[0].start()

    def project(i, carry):
        cols = pl.ds(pl.multiple_of(i * 256, 256), 256)
        raw[:, cols] = dot(normed[cols], wq[...]).T
        return carry

    lax.fori_loop(0, tokens // 256, project, 0)
    emits[3].start()
    feed[0].near()
    query_gain, key_gain = gain_columns(wq)
    cosine, sine = cos_ref[...], sin_ref[...]

    def turned(value, gain):
        hat = value * column_inverse(value) * gain
        a, b = hat[:32], hat[32:]
        return jnp.concatenate([a * cosine - b * sine, b * cosine + a * sine], axis=0)

    both = jnp.concatenate([turned(raw[192:256], key_gain), raw[256:320]], axis=0)
    kv[pl.ds(pl.multiple_of(me.c * tokens, tokens), tokens)] = both.T.astype(BF)
    keys.begin()
    qt[64:128] = jnp.zeros((64, 3 * tokens), BF)
    for h in range(3):
        qt[0:64, h * tokens : (h + 1) * tokens] = (
            turned(raw[64 * h : 64 * h + 64], query_gain) * (LOG2E / 8.0)
        ).astype(BF)
    emits[2].start()
    feed[0].pair()
    outw.near()
    acc[...] = jnp.zeros_like(acc)
    ones = jnp.concatenate([jnp.ones((1, 1024), BF), jnp.zeros((15, 1024), BF)], axis=0)
    apart = lax.broadcasted_iota(jnp.int32, (256, 256), 0) - lax.broadcasted_iota(
        jnp.int32, (256, 256), 1
    )

    def attend(h, place, slot):
        rows = kv[pl.ds(pl.multiple_of(place * 1024, 1024), 1024), :]
        scores = dot(rows, qt[:, pl.ds(pl.multiple_of(h * tokens, tokens), tokens)])
        parts = []
        for a in range(4):
            line = []
            for b in range(2):
                sub = scores[a * 256 : a * 256 + 256, b * 256 : b * 256 + 256]
                seen = apart <= kb[me.c * 512 + b * 256] - kb[place * 1024 + a * 256]
                line.append(jnp.where(seen, jnp.exp2(sub), 0.0).astype(BF))
            parts.append(jnp.concatenate(line, axis=1))
        weight = jnp.concatenate(parts, axis=0)
        pbuf[slot] = weight
        left = jnp.concatenate([rows.T[64:128], ones], axis=0)
        return dot(left, weight)

    def store(h, place, slot):
        return pltpu.make_async_copy(pbuf.at[slot], p_all.at[place, h], s_p.at[slot])

    def close(h):
        total = acc[h, 64:65]
        sums[0:1, h * tokens : (h + 1) * tokens] = total
        value = (acc[h, 0:64] / total).astype(BF)
        att_own[64 * h : 64 * h + 64] = value
        att[pl.ds(pl.multiple_of(me.t * 192 + 64 * h, 64), 64)] = value
        share[h].begin()

    def task(h, step, slot):
        place = chip_of(me, step, PAIRS)
        acc[h] += attend(h, place, slot)
        store(h, place, slot).start()

    def arriving(step, carry):
        @pl.when(step == 0)
        def _():
            keys.got(9)

        @pl.when(step == 1)
        def _():
            keys.near()
            feed[1].go(0)
            outw.pair()
            keys.got(11)

        @pl.when(step == 2)
        def _():
            keys.pair()
            feed[1].near()
            feed[2].go(0)
            keys.got(12)

        @pl.when(step == 3)
        def _():
            keys.got(10)
            outw.far()

        @pl.when(step >= 2)
        def _():
            for h in range(3):
                store(h, 0, 3 * lax.rem(step, 2) + h).wait()

        for h in range(3):
            task(h, step, 3 * lax.rem(step, 2) + h)
        return carry

    lax.fori_loop(0, 4, arriving, 0)

    def arrived(i, carry):
        @pl.when(i == 0)
        def _():
            keys.far()
            feed[0].far()
            feed[2].go(1, 2, 9)
            keys.got(13)
            keys.got(14)

        @pl.when(i == 1)
        def _():
            feed[1].pair()
            keys.last()
            keys.got(15)
            keys.got(16)
            emits[1].start()

        @pl.when(i == 2)
        def _():
            close(0)
            feed[0].last()
            outw.last()

        @pl.when(i == 3)
        def _():
            feed[2].near()

        @pl.when(i == 4)
        def _():
            close(1)
            feed[2].pair()

        @pl.when(i == 5)
        def _():
            share[0].near()
            share[0].pair()

        h = i // 2
        for half in range(2):
            slot = lax.rem(2 * i + half, 6)
            store(h, 0, slot).wait()
            task(h, 4 + 2 * lax.rem(i, 2) + half, slot)
        return carry

    lax.fori_loop(0, 6, arrived, 0)
    close(2)
    feed[1].far()
    share[0].far()
    share[1].near()
    share[1].pair()
    share[1].far()
    share[2].near()
    share[2].pair()
    share[2].far()
    feed[2].far()
    share[0].last()
    share[1].last()
    feed[1].last()
    share[2].last()
    outw.end()

    def forward_rows(i, carry):
        rows = pl.ds(pl.multiple_of(i * 256, 256), 256)
        value = x_ref[rows].astype(F32) + dot(att[:, rows].T, wo[...])
        inverse = rms_inverse(value)
        mid[rows] = value
        inv[rows] = jnp.broadcast_to(inverse, (256, 128))
        low[rows] = (value * inverse).astype(BF)
        return carry

    lax.fori_loop(0, 2, forward_rows, 0)
    emits[5].start()
    keep[2].wait()
    feed[0].end()
    feed[2].last()

    def gate_rows(i, carry):
        rows = pl.ds(pl.multiple_of(i * 256, 256), 256)
        gate[rows] = dot(low[rows], wf[0])
        return carry

    lax.fori_loop(0, 2, gate_rows, 0)
    keep[3].wait()
    feed[1].end()

    def up_rows(i, carry):
        rows = pl.ds(pl.multiple_of(i * 256, 256), 256)
        u = dot(low[rows], wf[1])
        up[rows] = u
        g = gate[rows]
        act[rows] = (g * jax.nn.sigmoid(g) * u).astype(BF)
        return carry

    lax.fori_loop(0, 2, up_rows, 0)
    emits[6].start()
    keep[4].wait()
    feed[2].end()

    def down_rows(i, carry):
        rows = pl.ds(pl.multiple_of(i * 256, 256), 256)
        ffn[rows] = dot_nt(act[rows], wf[2]).astype(BF)
        return carry

    lax.fori_loop(0, 2, down_rows, 0)
    sum_f.begin()
    gain_two[...] = jnp.zeros_like(gain_two)

    def backward_rows(i, carry):
        @pl.when(i == 1)
        def _():
            sum_f.relay()

        rows = pl.ds(pl.multiple_of(i * 256, 256), 256)
        ct = cot[rows]
        g, u = gate[rows], up[rows]
        sig = jax.nn.sigmoid(g)
        grad_act = dot(ct, wf[2])
        gg = (grad_act * u * sig * (1.0 + g * (1.0 - sig))).astype(BF)
        gu = (grad_act * g * sig).astype(BF)
        grad_g[rows] = gg
        grad_u[rows] = gu
        back = dot_nt(gg, wf[0]) + dot_nt(gu, wf[1])
        hat = low[rows].astype(F32)
        both = back * hat
        gain_two[...] += jnp.sum(both, axis=0, keepdims=True)
        pull = jnp.mean(both, axis=-1, keepdims=True)
        part = (ct.astype(F32) * 0.125 + inv[rows][:, 0:1] * (back - hat * pull)).astype(BF)
        share_ref[rows] = part
        u_ref[:, rows] = dot_nt(wo[...], part).astype(BF)
        return carry

    lax.fori_loop(0, 2, backward_rows, 0)
    for k in range(7, 10):
        emits[k].start()
    mid_own[...] = mid[pl.ds(pl.multiple_of(me.t * 64, 64), 64)]
    sum_f.columns(col_sum)
    for k in range(10):
        emits[k].wait()
    keys.sent()
    sum_f.sent()
    for s in share:
        s.sent()
    for slot in range(6):
        store(0, 0, slot).wait()


def forward_part(*operands):
    tokens = 512
    kept = [
        ((1536, 384), BF),
        ((16 * tokens, 128), BF),
        ((128, 3 * tokens), BF),
        ((384, tokens), F32),
        ((tokens, 1536), BF),
        ((tokens, 1536), BF),
        ((tokens, 896), BF),
        ((tokens, 896), BF),
        ((tokens, 896), BF),
        ((tokens, 1536), BF),
    ]
    shapes = [jax.ShapeDtypeStruct(*k) for k in kept] + [
        jax.ShapeDtypeStruct((8, 3 * tokens), F32),
        jax.ShapeDtypeStruct((192, tokens), BF),
        jax.ShapeDtypeStruct((1536, tokens), BF),
        jax.ShapeDtypeStruct((64, 1536), F32),
        jax.ShapeDtypeStruct((2, 64, 1536), BF),
        jax.ShapeDtypeStruct((1, 1536), F32),
        jax.ShapeDtypeStruct((8, 3, 1024, tokens), BF),
    ]
    scratch = [
        *[pltpu.VMEM(*k) for k in kept],
        pltpu.VMEM((1536, 256), BF),
        pltpu.VMEM((3, 1536, 896), BF),
        pltpu.VMEM((1536, 1536), BF),
        pltpu.VMEM((1536, tokens), BF),
        pltpu.VMEM((3, 80, tokens), F32),
        pltpu.VMEM((6, 1024, tokens), BF),
        pltpu.VMEM((tokens, 1536), F32),
        pltpu.VMEM((tokens, 128), F32),
        pltpu.VMEM((tokens, 896), F32),
        pltpu.VMEM((tokens, 896), F32),
        pltpu.VMEM((tokens, 1536), BF),
        *[DMA((17,))] * 4,
        *[DMA((3, 17))] * 2,
        *[DMA((17,))] * 4,
        *[DMA((3, 9))] * 2,
        DMA((5,)),
        DMA((6,)),
        DMA((10,)),
        *ring_scratch(32, 1536),
    ]
    return pl.pallas_call(
        forward_kernel,
        out_shape=shapes,
        in_specs=[SM] + [VM] * 7,
        out_specs=[HB] * 10 + [VM] * 6 + [HB],
        scratch_shapes=scratch,
        name="forward_part",
        compiler_params=pltpu.CompilerParams(
            collective_id=0, has_side_effects=True, vmem_limit_bytes=59 << 20
        ),
    )(*operands)


def backward_kernel(
    wq_in, kv_in, qt_in, raw_in, normed_in, low, act, grad_g, grad_u, share_in,
    sums, att_own, u_ref, mid_own, col_sum, gain_two, p_all, cot, x_in, cos_ref, sin_ref,
    blk, gin, own_q, own_w, gains,
    wq, kv, qt, raw, share_ref, x_ref, col_z,
    mid_rows, branch, gt, drift, dq, gk, gk_sib, wg, sib_w, pw, sib_p, po, sib_o, back, pre, extra,
    s_blk, r_blk, s_br, r_br, s_in, r_in, s_ex, r_ex, s_sib, r_sib, s_loc, s_p,
    *rest,
):
    me = Place()
    cn = ctx_neighbours(me)
    tn = tp_neighbours(me)
    sib = cn[3]
    tokens = 512
    scratch = [rest[8 * k : 8 * k + 8] for k in range(9)]
    crossing = tp_cross(me)

    def tp_block(k):
        return me.tp(*SLOTS[k])

    def chip(k):
        dz, dx = SLOTS[k]
        return me.ctx(dz, dx) // 2

    def rows_of(ref, size):
        def src(k, part):
            start = pl.multiple_of(tp_block(k) * size, size) + part * (size // 2)
            return ref.at[pl.ds(pl.multiple_of(start, size // 2), size // 2)]

        return src

    sum_u = ring(rows_of(u_ref, 192), 96, scratch[0], tn, True, crossing)
    sum_two = ring(rows_of(share_ref, 64), 32, scratch[1], tn, True, crossing)
    sum_b = ring(rows_of(back, 64), 32, scratch[2], tn, False, crossing)
    sum_kv = ring(
        lambda k, part: gk.at[k, me.core, pl.ds(64 * part, 64)], 64, scratch[3], cn
    )
    sum_w = [
        ring(
            lambda k, part, p=p: wg.at[p, chip(k), me.core, pl.ds(48 * part, 48)],
            48,
            scratch[4 + p],
            cn,
        )
        for p in range(3)
    ]
    sum_q = ring(
        lambda k, part: pw.at[chip(k), me.core, pl.ds(48 * part, 48)], 48, scratch[7], cn
    )
    sum_o = ring(
        lambda k, part: po.at[chip(k), me.core, pl.ds(48 * part, 48)], 48, scratch[8], cn
    )
    put_two = Gather(blk, 64, me.tp, *tn, None, s_blk, r_blk, over=True)
    put_br = Gather(branch, 64, me.tp, *tn, None, s_br, r_br)
    put_in = Gather(gin, 64, me.tp, *tn, None, s_in, r_in)
    others = [(dz, dy) for dz in (0, 1) for dy in range(4) if (dz, dy) != (0, 0)]
    put_ex = [
        pltpu.make_async_remote_copy(
            src_ref=extra.at[0],
            dst_ref=extra.at[1 + k],
            send_sem=s_ex.at[k],
            recv_sem=r_ex.at[k],
            device_id=(me.c, me.tp(*o)),
            device_id_type=MESH,
        )
        for k, o in enumerate(others)
    ]

    def to_sibling(k, here, there):
        return pltpu.make_async_remote_copy(
            src_ref=here,
            dst_ref=there,
            send_sem=s_sib.at[k],
            recv_sem=r_sib.at[k],
            device_id=sib,
            device_id_type=MESH,
        )

    def key_swap(k):
        return to_sibling(k, gk.at[k, 1 - me.core], gk_sib.at[k])

    swap_w = [to_sibling(8 + p, wg.at[p, :, 1 - me.core], sib_w.at[p]) for p in range(3)]
    swap_p = to_sibling(11, pw.at[:, 1 - me.core], sib_p)
    swap_o = to_sibling(13, po.at[:, 1 - me.core], sib_o)
    cross = pltpu.make_async_remote_copy(
        src_ref=col_sum.at[1],
        dst_ref=col_z,
        send_sem=s_sib.at[12],
        recv_sem=r_sib.at[12],
        device_id=tn[0],
        device_id_type=MESH,
    )
    takes = [
        pltpu.make_async_copy(h, v, s_loc.at[14 + k])
        for k, (h, v) in enumerate(
            [
                (wq_in, wq),
                (kv_in, kv),
                (qt_in, qt),
                (raw_in, raw),
                (share_in, share_ref),
                (x_in.at[pl.ds(pl.multiple_of(me.t * 64, 64), 64)], x_ref),
            ]
        )
    ]


    def weight_grads(b_low, b_cot, b_one, b_two):
        def load(k, here, there):
            return pltpu.make_async_copy(here, there, s_loc.at[k])

        loads = [load(0, low, b_low), load(1, grad_g, b_one), load(2, grad_u, b_two)]
        loads += [load(3, cot, b_cot), load(4, act, b_one)]
        for k in loads[0:4] + takes:
            k.start()
        greet([*cn, *tn, *crossing, (me.c, me.tp(0, 2)), (me.c, me.tp(1, 2))])
        sum_u.begin()
        cross.start()
        loads[0].wait()
        for p, (left, right) in enumerate([(b_low, b_one), (b_low, b_two), (b_cot, b_one)]):
            loads[(1, 2, 4)[p]].wait()
            if p == 2:
                loads[3].wait()

            def chunk(i, carry, p=p, left=left, right=right):
                if p == 1:

                    @pl.when(i == 3)
                    def _():
                        sum_u.relay()

                at = pl.ds(pl.multiple_of(384 * i, 384), 384)
                whole = dot(left[:, at].T, right[...]).astype(BF)
                for q in range(4):
                    wg[p, 2 * i + q // 2, q % 2] = whole[96 * q : 96 * q + 96]
                return carry

            lax.fori_loop(0, 4, chunk, 0)
            swap_w[p].start()
            if p == 0:
                loads[4].start()

    pl.run_scoped(
        weight_grads,
        pltpu.VMEM((tokens, 1536), BF),
        pltpu.VMEM((tokens, 1536), BF),
        pltpu.VMEM((tokens, 896), BF),
        pltpu.VMEM((tokens, 896), BF),
    )

    def join_w(p):
        swap_w[p].wait_recv()

        def one(j, carry):
            add_into(wg.at[p, j, me.core], wg.at[p, j, me.core], sib_w.at[p, j])
            return carry

        lax.fori_loop(0, 8, one, 0)

    join_w(0)
    sum_w[0].begin()
    for k in takes:
        k.wait()
    grad_att = jnp.concatenate([sum_u.finish(0), sum_u.finish(1)], axis=0)
    own = pl.multiple_of(me.t * 64, 64)
    cross.wait_recv()
    blk[pl.ds(own, 64)] = (
        mid_own[...] + col_sum[0].astype(F32) + col_z[...].astype(F32)
    ).astype(BF)
    sum_two.begin()
    put_two.begin()
    gt[0:64] = jnp.zeros((64, 3 * tokens), BF)
    for h in range(3):
        cols = slice(h * tokens, (h + 1) * tokens)
        grad = grad_att[64 * h : 64 * h + 64]
        inverse = 1.0 / sums[0:1, cols]
        gt[64:128, cols] = (grad * inverse).astype(BF)
        drift[0:1, cols] = (
            jnp.sum(grad * att_own[64 * h : 64 * h + 64].astype(F32), axis=0, keepdims=True)
            * inverse
        )
    dq[...] = jnp.zeros_like(dq)

    def join_keys(k):
        key_swap(k).wait_recv()
        add_into(gk.at[k, me.core], gk.at[k, me.core], gk_sib.at[k])

    def key_loop(pbuf):
        def load(step, h):
            return pltpu.make_async_copy(
                p_all.at[chip_of(me, step, SLOTS), h], pbuf.at[h], s_p.at[h]
            )

        for h in range(3):
            load(0, h).start()

        def key_step(step, carry):
            @pl.when(step == 1)
            def _():
                join_keys(0)
                sum_kv.go(0, 1)
                sum_two.relay()
                sum_w[0].relay()
                join_w(1)
                sum_w[1].begin()

            @pl.when(step == 2)
            def _():
                join_keys(1)
                sum_kv.go(2, 3)
                put_two.near()

            @pl.when(step == 3)
            def _():
                join_keys(2)
                sum_kv.go(4)
                sum_kv.relay_right(1)
                branch_rows = jnp.concatenate([sum_two.finish(0), sum_two.finish(1)], axis=0)
                mid_rows[...] = branch_rows
                branch[pl.ds(own, 64)] = branch_rows.astype(BF)
                put_br.begin()
                sum_w[0].column()
                sum_w[1].relay()
                join_w(2)
                sum_w[2].begin()

            @pl.when(step == 4)
            def _():
                join_keys(3)
                sum_kv.go(5)
                sum_kv.relay_left(1)
                put_two.far()

            @pl.when(step == 5)
            def _():
                join_keys(4)
                sum_kv.go(6)
                sum_kv.relay_right(0)
                sum_w[1].column()
                put_two.pair()
                put_br.near()
                put_br.pair()

            @pl.when(step == 6)
            def _():
                join_keys(5)
                sum_kv.go(7)
                sum_kv.relay_left(0)
                put_br.far()
                put_two.last()
                sum_w[2].relay()

            @pl.when(step == 7)
            def _():
                join_keys(6)
                sum_kv.column()
                put_br.last()

            place = chip_of(me, step, SLOTS)
            rows = kv[pl.ds(pl.multiple_of(place * 1024, 1024), 1024), :]
            key_t = rows.T[0:64]
            key_grad = value_grad = 0.0
            for h in range(3):
                cols = slice(h * tokens, (h + 1) * tokens)
                slopes = dot(rows, gt[:, cols])
                load(step, h).wait()
                weight = pbuf[h]
                grad = (weight.astype(F32) * (slopes - drift[0:1, cols])).astype(BF)
                dq[:, cols] += dot(key_t, grad)
                key_grad += dot_nt(qt[0:64, cols], grad)
                value_grad += dot_nt(gt[64:128, cols], weight)

                @pl.when(step < 7)
                def _(h=h):
                    load(step + 1, h).start()

            both = jnp.concatenate([key_grad * LN2, value_grad], axis=0).astype(BF)
            gk[step, 0] = both[:, 0:512]
            gk[step, 1] = both[:, 512:1024]
            key_swap(step).start()
            return carry

        lax.fori_loop(0, 8, key_step, 0)

    pl.run_scoped(key_loop, pltpu.VMEM((3, 1024, tokens), BF))
    def finale(normed):
        fetch = pltpu.make_async_copy(normed_in, normed, s_loc.at[5])
        fetch.start()
        att_n = jnp.concatenate(
            [att_own[...].astype(F32), jnp.zeros((64, tokens), F32)], axis=0
        ).T.astype(BF)
        for i in range(4):
            at = slice(384 * i, 384 * i + 384)
            whole = dot(branch[:, at].T, att_n).astype(BF)
            for q in range(4):
                po[2 * i + q // 2, q % 2] = whole[96 * q : 96 * q + 96]
        swap_o.start()
        query_gain, key_gain = gain_columns(wq)
        cosine, sine = cos_ref[...], sin_ref[...]

        def unturn(grad, value, gain):
            inverse = column_inverse(value)
            hat = value * inverse
            a, b = grad[:32], grad[32:]
            plain = jnp.concatenate([a * cosine + b * sine, b * cosine - a * sine], axis=0)
            gain_grad = jnp.sum(plain * hat, axis=1, keepdims=True)
            pulled = plain * gain
            back_grad = inverse * (pulled - hat * jnp.mean(pulled * hat, axis=0, keepdims=True))
            return gain_grad, back_grad

        query_gain_grad = 0.0
        for h in range(3):
            part, grad = unturn(
                dq[:, h * tokens : (h + 1) * tokens] * 0.125, raw[64 * h : 64 * h + 64], query_gain
            )
            query_gain_grad += part
            pre[64 * h : 64 * h + 64] = grad
        join_keys(7)
        key_grad, value_grad = sum_kv.finish(0), sum_kv.finish(1)
        key_gain_grad, grad = unturn(key_grad, raw[192:256], key_gain)
        pre[192:256] = grad
        pre[256:320] = value_grad
        pre[320:384] = jnp.zeros((64, tokens), F32)
        pre_n = pre[...].T.astype(BF)
        for i in range(2):
            rows = slice(256 * i, 256 * i + 256)
            back[rows] = dot_nt(pre_n[rows], wq[...]).astype(BF)
        sum_b.begin()
        fetch.wait()
        gain_one = 0.0
        for i in range(4):
            rows = slice(128 * i, 128 * i + 128)
            gain_one += jnp.sum(
                back[rows].astype(F32) * normed[rows].astype(F32), axis=0, keepdims=True
            )
        sum_w[2].column()
        swap_o.wait_recv()

        def join_o(j, carry):
            add_into(po.at[j, me.core], po.at[j, me.core], sib_o.at[j])
            return carry

        lax.fori_loop(0, 8, join_o, 0)
        sum_o.begin()
        lane = lax.broadcasted_iota(jnp.int32, (64, 1536), 1)
        unit = lax.broadcasted_iota(jnp.int32, (64, 1536), 0)
        spot = lane == (unit // 4) * 96 + lax.rem(unit, 4)

        def spread(column):
            return jnp.sum(jnp.where(spot, column, 0.0), axis=0, keepdims=True)

        lines = jnp.concatenate(
            [
                jnp.zeros((64, 1536), F32),
                gain_one,
                gain_two[...],
                spread(query_gain_grad),
                spread(key_gain_grad),
                jnp.zeros((60, 1536), F32),
            ],
            axis=0,
        )
        sides = lines.T
        sum_b.relay()
        for i in range(4):
            at = slice(384 * i, 384 * i + 384)
            part = dot(normed[:, at].T, pre_n)
            whole = jnp.concatenate([part[:, 0:256], part[:, 256:384] + sides[at]], axis=1).astype(BF)
            for q in range(4):
                pw[2 * i + q // 2, q % 2] = whole[96 * q : 96 * q + 96]
        swap_p.start()
        sum_o.relay()
        swap_p.wait_recv()

        def join_p(j, carry):
            add_into(pw.at[j, me.core], pw.at[j, me.core], sib_p.at[j])
            return carry

        lax.fori_loop(0, 8, join_p, 0)
        sum_q.begin()
        value = x_ref[...].astype(F32)
        inverse = rms_inverse(value)
        hat = value * inverse
        back_one = jnp.concatenate([sum_b.finish(0), sum_b.finish(1)], axis=0)
        gin[pl.ds(own, 64)] = (
            mid_rows[...]
            + inverse * (back_one - hat * jnp.mean(back_one * hat, axis=-1, keepdims=True))
        ).astype(BF)
        put_in.begin()
        for p in range(3):
            for half in range(2):
                own_w[p, 48 * half : 48 * half + 48] = sum_w[p].finish(half)
        put_in.near()
        sum_q.relay()
        sum_o.column()
        put_in.pair()
        sum_q.column()
        put_in.far()
        for half in range(2):
            own_q[48 * half : 48 * half + 48, 0:384] = sum_q.finish(half)
        extra[0] = own_q[:, 256:384].T[64:72]
        for p in put_ex:
            p.start()
        for half in range(2):
            own_q[48 * half : 48 * half + 48, 384:640] = sum_o.finish(half)
        put_in.last()
        for p in put_ex:
            p.wait()
        total = extra[0]
        for b in range(1, 8):
            total += extra[b]
        gains[...] = total
        for s in [sum_u, sum_two, sum_b, sum_kv, sum_q, sum_o, *sum_w, put_two, put_br, put_in]:
            s.sent()
        for k in range(8):
            key_swap(k).wait_send()
        for s in [*swap_w, swap_p, swap_o, cross]:
            s.wait_send()

    pl.run_scoped(finale, pltpu.VMEM((tokens, 1536), BF))


def backward_part(*operands):
    tokens = 512
    shapes = [
        jax.ShapeDtypeStruct((512, 1536), BF),
        jax.ShapeDtypeStruct((512, 1536), BF),
        jax.ShapeDtypeStruct((96, 640), F32),
        jax.ShapeDtypeStruct((3, 96, 896), F32),
        jax.ShapeDtypeStruct((8, 96), F32),
    ]
    scratch = [
        pltpu.VMEM((1536, 384), BF),
        pltpu.VMEM((16 * tokens, 128), BF),
        pltpu.VMEM((128, 3 * tokens), BF),
        pltpu.VMEM((384, tokens), F32),
        pltpu.VMEM((tokens, 1536), BF),
        pltpu.VMEM((64, 1536), BF),
        pltpu.VMEM((64, 1536), BF),
        pltpu.VMEM((64, 1536), F32),
        pltpu.VMEM((tokens, 1536), BF),
        pltpu.VMEM((128, 3 * tokens), BF),
        pltpu.VMEM((8, 3 * tokens), F32),
        pltpu.VMEM((64, 3 * tokens), F32),
        pltpu.VMEM((8, 2, 128, 512), BF),
        pltpu.VMEM((8, 128, 512), BF),
        pltpu.VMEM((3, 8, 2, 96, 896), BF),
        pltpu.VMEM((3, 8, 96, 896), BF),
        pltpu.VMEM((8, 2, 96, 384), BF),
        pltpu.VMEM((8, 96, 384), BF),
        pltpu.VMEM((8, 2, 96, 256), BF),
        pltpu.VMEM((8, 96, 256), BF),
        pltpu.VMEM((tokens, 1536), BF),
        pltpu.VMEM((384, tokens), F32),
        pltpu.VMEM((8, 8, 96), F32),
        *[DMA((9,))] * 8,
        DMA((14,)),
        DMA((14,)),
        DMA((21,)),
        DMA((3,)),
        *ring_scratch(96, 512, True),
        *ring_scratch(32, 1536, True),
        *ring_scratch(32, 1536),
        *ring_scratch(64, 512),
        *ring_scratch(48, 896) * 3,
        *ring_scratch(48, 384),
        *ring_scratch(48, 256),
    ]
    return pl.pallas_call(
        backward_kernel,
        out_shape=shapes,
        in_specs=[HB] * 10 + [VM] * 6 + [HB] * 3 + [VM] * 2,
        out_specs=[VM] * 5,
        scratch_shapes=scratch,
        name="backward_part",
        compiler_params=pltpu.CompilerParams(
            collective_id=1, has_side_effects=True, vmem_limit_bytes=59 << 20
        ),
    )(*operands)


FREQ = [[THETA ** (-2.0 * i / HD)] * 128 for i in range(HD // 2)]


def body(
    block_input, positions, attn_gain, query_weight, key_weight, value_weight, query_gain,
    key_gain, output_weight, ffn_gain, gate_weight, up_weight, down_weight, out_cotangent,
):
    def line(gain):
        return gain.reshape(1, -1)

    wq_s, wo_s, wf_s, cosine, sine = prepare(
        line(positions), line(attn_gain), line(ffn_gain), line(query_gain), line(key_gain),
        jnp.array(FREQ, F32), query_weight, key_weight.T, value_weight.T, output_weight,
        gate_weight, up_weight, down_weight.T,
    )
    results = forward_part(positions, block_input, out_cotangent, wq_s, wo_s, wf_s, cosine, sine)
    results = backward_part(*results, out_cotangent, block_input, cosine, sine)
    return conclude(line(attn_gain), line(ffn_gain), *results)


def solution(mesh):
    in_specs = (
        P("ctx", None),
        P(),
        P("ctx"),
        P("ctx", "tp"),
        P("ctx", "tp"),
        P("ctx", "tp"),
        P("ctx"),
        P("ctx"),
        P("tp", "ctx"),
        P("ctx"),
        P("ctx", "tp"),
        P("ctx", "tp"),
        P("tp", "ctx"),
        P("ctx", None),
    )
    out_specs = (
        P("ctx", None),
        P("ctx", None),
        P("ctx"),
        P("ctx", "tp"),
        P("ctx", "tp"),
        P("ctx", "tp"),
        P("ctx"),
        P("ctx"),
        P("tp", "ctx"),
        P("ctx"),
        P("ctx", "tp"),
        P("ctx", "tp"),
        P("tp", "ctx"),
    )
    return jax.shard_map(body, mesh=mesh, in_specs=in_specs, out_specs=out_specs, check_vma=False)
```
